32 devices in a mesh: dp: 8 (over z, y), tensor: 4 (over x, core).
Axes of the slice: x: 2, y: 2, z: 4, core: 2. Of those that a mesh axis runs over, the one named last changes fastest.
Arguments:
- noised: int32 [16, 1024], P('dp', 'tensor'), may hold values from 0 to 26
- targets: int32 [16, 1024], P('dp', 'tensor'), may hold values from 0 to 26
- timesteps: int32 [16, 4], P('dp'), may hold values from 0 to 999
- segments: int32 [16, 1024], P('dp'), may hold values from 0 to 3, as said below
- embedding: float32 [27, 512], replicated, may hold values from -6 to 6
- out_head: float32 [512, 27], replicated, may hold values from -0.25 to 0.25
- norm_gains: float32 [3, 512], replicated, may hold values from 0.5 to 1.5
- w_qkv: float32 [512, 1536], P(None, 'tensor'), may hold values from -0.25 to 0.25
- w_out: float32 [512, 512], P('tensor'), may hold values from -1.5 to 1.5
- w_up: float32 [512, 2048], P(None, 'tensor')
- w_down: float32 [2048, 512], P('tensor')
- mom_qkv: float32 [512, 1536], P(None, 'tensor'), may hold values from -0.0034179688 to 0.0034179688
- mom_out: float32 [512, 512], P('tensor'), may hold values from -0.0034179688 to 0.0034179688
- mom_up: float32 [512, 2048], P(None, 'tensor'), may hold values from -0.0034179688 to 0.0034179688
- mom_down: float32 [2048, 512], P('tensor'), may hold values from -0.0034179688 to 0.0034179688
- embed_m: float32 [27, 512], replicated, may hold values from -0.00036621094 to 0.00036621094
- embed_v: float32 [27, 512], replicated, may hold values from 9.536744e-10 to 3.8146974e-09
- head_m: float32 [512, 27], replicated, may hold values from -0.00036621094 to 0.00036621094
- head_v: float32 [512, 27], replicated, may hold values from 1.5894573e-08 to 6.357829e-08
- gains_m: float32 [3, 512], replicated, may hold values from -0.001953125 to 0.001953125
- gains_v: float32 [3, 512], replicated, may hold values from 4.1325887e-07 to 1.5894572e-06
Outputs:
- block_out: bfloat16 [16, 1024, 512], P('dp', 'tensor')
- input_grad: float32 [16, 1024, 512], P('dp', 'tensor')
- grad_norm: float32 [], replicated
- mom_qkv_new: float32 [512, 1536], P(None, 'tensor')
- qkv_new: float32 [512, 1536], P(None, 'tensor')
- mom_out_new: float32 [512, 512], P('tensor')
- out_new: float32 [512, 512], P('tensor')
- mom_up_new: float32 [512, 2048], P(None, 'tensor')
- up_new: float32 [512, 2048], P(None, 'tensor')
- mom_down_new: float32 [2048, 512], P('tensor')
- down_new: float32 [2048, 512], P('tensor')
- embed_m_new: float32 [27, 512], replicated
- embed_v_new: float32 [27, 512], replicated
- embed_new: float32 [27, 512], replicated
- head_m_new: float32 [512, 27], replicated
- head_v_new: float32 [512, 27], replicated
- head_new: float32 [512, 27], replicated
- gains_m_new: float32 [3, 512], replicated
- gains_v_new: float32 [3, 512], replicated
- gains_new: float32 [3, 512], replicated
The draws below stay inside these ranges and needn't reach their ends.
Inputs may be any that keep to these rules, and one draw needn't show every extreme that they name: `segments`: in each row the span number starts at 0, never falls, and steps up by one at exactly 3 positions.
All inputs are finite; a program needn't handle non-finite values.
Results may differ from the reference program's by a relative error of at most 0.011.
Values may be sent and summed in bfloat16 or wider, within the bound.
No kernel may reach another device: no remote copies, remote signals or barrier semaphores. Data moves between devices by JAX's collectives and lax.ppermute only.
A program may use at most 192 MiB of HBM per device.

```python
import math
import jax
import jax.numpy as jnp
from jax import lax

D = 512
HEADS = 8
HEAD_DIM = 64
FF = 2048
VOCAB = 27
LEN = 1024
SPANS = 4
TSTEPS = 1000
NS_STEPS = 5
STEP = 10
ROWS = 16


def draw_segments(key, part):
    key = jax.random.fold_in(key, 11)
    key_one, key_two, key_three = jax.random.split(key, 3)
    first_cut = jax.random.randint(key_one, (ROWS, 1), 1, LEN // 8 + 1)
    long_span = 3 * LEN // 4 + jax.random.randint(key_two, (ROWS, 1), 1, LEN // 16 + 1)
    second_cut = first_cut + long_span
    third_cut = second_cut + jax.random.randint(key_three, (ROWS, 1), 1, LEN - second_cut)
    position = jnp.arange(LEN, dtype=jnp.int32)[None, :]
    counted = (position >= first_cut).astype(jnp.int32) + (position >= second_cut).astype(jnp.int32)
    return counted + (position >= third_cut).astype(jnp.int32)


def draw_w_up(key, part):
    key = jax.random.fold_in(key, 21)
    base_draw = jax.random.normal(key, (D, FF), jnp.float32)
    column_ramp = 0.6 + 1.2 * jnp.arange(FF, dtype=jnp.float32) / (FF - 1)
    return base_draw * column_ramp[None, :] * D ** (-0.5)


def draw_w_down(key, part):
    key = jax.random.fold_in(key, 31)
    base_draw = jax.random.normal(key, (FF, D), jnp.float32)
    row_ramp = 0.6 + 1.2 * jnp.arange(FF, dtype=jnp.float32) / (FF - 1)
    return base_draw * row_ramp[:, None] * FF ** (-0.5)


def set_ends(values, rng, low, top_value):
    index_at = [jax.random.randint(jax.random.fold_in(rng, axis), (), 0, length) for axis, length in enumerate(values.shape)]
    widest = values.shape.index(max(values.shape))
    next_to = index_at[:widest] + [(index_at[widest] + 1) % values.shape[widest]] + index_at[widest + 1:]
    return values.at[tuple(index_at)].set(low).at[tuple(next_to)].set(top_value)


def levels(key, shape, pieces, smallest, top_value):
    gain, own = 1.0, jax.random.fold_in(key, 6)
    for dim, parts in pieces:
        steps = jnp.exp(jax.random.uniform(jax.random.fold_in(own, dim), (parts,), jnp.float32, smallest / len(pieces), top_value / len(pieces)))
        gain = gain * jnp.repeat(steps, shape[dim] // parts).reshape([-1 if axis == dim else 1 for axis in range(len(shape))])
    return gain


def scatter_about(key, shape, scale, most, pieces=(), kind=jnp.bfloat16):
    values = scale * jax.random.normal(key, shape, jnp.float32)
    if pieces:
        values = values * levels(key, shape, pieces, -0.22, 0.18)
    return jnp.clip(values, -most, most).astype(kind)


def setup_inputs(seed: int = 0) -> dict:
    key_list = jax.random.split(jax.random.key(seed), 22)
    noised = set_ends(jax.random.randint(key_list[0], (ROWS, LEN), 0, VOCAB), jax.random.fold_in(key_list[0], 1), 0, VOCAB - 1).astype(jnp.int32)
    targets = set_ends(jax.random.randint(key_list[1], (ROWS, LEN), 0, VOCAB), jax.random.fold_in(key_list[1], 1), 0, VOCAB - 1).astype(jnp.int32)
    timesteps = set_ends(jax.random.randint(key_list[2], (ROWS, SPANS), 0, TSTEPS), jax.random.fold_in(key_list[2], 1), 0, TSTEPS - 1).astype(jnp.int32)
    segments = draw_segments(jax.random.fold_in(key_list[21], 71), 0)
    embedding = scatter_about(key_list[4], (VOCAB, D), 1.0, 6.0, (), jnp.float32)
    out_head = scatter_about(key_list[5], (D, VOCAB), D ** -0.5, 0.25, (), jnp.float32)
    norm_gains = jnp.clip(1.0 + 0.1 * jax.random.normal(key_list[6], (3, D), jnp.float32), 0.5, 1.5)
    w_qkv = scatter_about(key_list[7], (D, 3 * D), D ** -0.5, 0.25, ((1, 4),), jnp.float32)
    w_out = scatter_about(key_list[8], (D, D), (D // 32) ** -0.5, 1.5, ((0, 4),), jnp.float32)
    w_up = draw_w_up(jax.random.fold_in(key_list[21], 71), 0)
    w_down = draw_w_down(jax.random.fold_in(key_list[21], 71), 0)
    mom_qkv = scatter_about(key_list[11], (D, 3 * D), ((4 * D * D + 2 * D * FF) ** -0.5), 0.0034179688, ((1, 4),), jnp.float32)
    mom_out = scatter_about(key_list[12], (D, D), ((4 * D * D + 2 * D * FF) ** -0.5), 0.0034179688, ((0, 4),), jnp.float32)
    mom_up = scatter_about(key_list[13], (D, FF), ((4 * D * D + 2 * D * FF) ** -0.5), 0.0034179688, ((1, 4),), jnp.float32)
    mom_down = scatter_about(key_list[14], (FF, D), ((4 * D * D + 2 * D * FF) ** -0.5), 0.0034179688, ((0, 4),), jnp.float32)
    embed_m = scatter_about(key_list[15], (VOCAB, D), (0.11 * (4 * D * D + 2 * D * FF) ** -0.5), 0.00036621094, (), jnp.float32)
    embed_v = jnp.clip(jnp.exp(jax.random.uniform(key_list[16], (VOCAB, D), jnp.float32, math.log(9.536743617033494e-10), math.log(3.814697446813398e-09))), 9.536743617033494e-10, 3.814697446813398e-09)
    head_m = scatter_about(key_list[17], (D, VOCAB), (0.11 * (4 * D * D + 2 * D * FF) ** -0.5), 0.00036621094, (), jnp.float32)
    head_v = jnp.clip(jnp.exp(jax.random.uniform(key_list[18], (D, VOCAB), jnp.float32, math.log(1.5894572769070692e-08), math.log(6.357829107628277e-08))), 1.5894572769070692e-08, 6.357829107628277e-08)
    gains_m = scatter_about(key_list[19], (3, D), (0.55 * (4 * D * D + 2 * D * FF) ** -0.5), 0.001953125, (), jnp.float32)
    gains_v = jnp.clip(jnp.exp(jax.random.uniform(key_list[20], (3, D), jnp.float32, math.log(4.132588742322696e-07), math.log(1.589457156114804e-06))), 4.132588742322696e-07, 1.589457156114804e-06)
    return dict(noised=noised, targets=targets, timesteps=timesteps, segments=segments, embedding=embedding, out_head=out_head, norm_gains=norm_gains, w_qkv=w_qkv, w_out=w_out, w_up=w_up, w_down=w_down, mom_qkv=mom_qkv, mom_out=mom_out, mom_up=mom_up, mom_down=mom_down, embed_m=embed_m, embed_v=embed_v, head_m=head_m, head_v=head_v, gains_m=gains_m, gains_v=gains_v)


HIGHEST_PREC = lax.Precision.HIGHEST
NORM_EPS = 1e-05
MASK_FILL = -1e+30
MUON_MOMENTUM = 0.5
MUON_RATE = 0.3
MUON_DECAY = 0.1
SCHULZ_LINEAR = 3.4445
SCHULZ_SQUARE = -4.775
SCHULZ_CUBE = 2.0315
ADAM_BETA_ONE = 0.9
ADAM_BETA_TWO = 0.95
ADAM_EPS = 1e-08
EMBED_RATE = 0.3
HEAD_RATE = 0.02
GAIN_RATE = 0.6
WEIGHT_DECAY = 0.1
CLIP_NORM = 1.0

@jax.custom_vjp
def low(v):
    return lax.optimization_barrier(v.astype(jnp.bfloat16)).astype(jnp.float32)

@jax.custom_vjp
def low_back(v):
    return v

def low_keep(v):
    return (low(v), None)

def low_pass(kept, grad):
    return (grad,)

def back_keep(v):
    return (v, None)

def back_low(kept, grad):
    return (low(grad),)
low.defvjp(low_keep, low_pass)
low_back.defvjp(back_keep, back_low)

def rounded(values_in):
    return low_back(low(values_in))

def sinus(steps_in, model_width):
    half_width = model_width // 2
    freq_rates = jnp.exp(-math.log(10000.0) * jnp.arange(half_width).astype(jnp.float32) / half_width)
    angles = steps_in.astype(jnp.float32)[..., None] * freq_rates
    return jnp.concatenate([jnp.sin(angles), jnp.cos(angles)], axis=-1)

def layer_norm(values_in, gain_vec):
    feat_mean = lax.optimization_barrier(jnp.mean(values_in, axis=-1, keepdims=True))
    centered = values_in - feat_mean
    variance = lax.optimization_barrier(jnp.mean(centered * centered, axis=-1, keepdims=True))
    return centered * lax.rsqrt(variance + NORM_EPS) * gain_vec

def row_forward(hidden0, segment_row, target_row, gain_w, qkv_w, out_w, up_w, down_w, head_w):
    score_scale = HEAD_DIM ** (-0.5)
    normed1 = low(layer_norm(hidden0, gain_w[0]))
    qkv_all = rounded(jnp.dot(normed1, low(qkv_w), precision=HIGHEST_PREC)).reshape(LEN, HEADS, 3, HEAD_DIM)
    query_heads = qkv_all[:, :, 0]
    key_heads = qkv_all[:, :, 1]
    value_heads = qkv_all[:, :, 2]
    scores = low_back(jnp.einsum('qhd,khd->hqk', query_heads, key_heads, precision=HIGHEST_PREC) * score_scale)
    same_span = segment_row[:, None] == segment_row[None, :]
    scores = jnp.where(same_span[None], scores, MASK_FILL)
    attend_probs = jax.nn.softmax(scores, axis=-1)
    context = jnp.einsum('hqk,khd->qhd', low(attend_probs), value_heads, precision=HIGHEST_PREC)
    context = rounded(context.reshape(LEN, D))
    attn_out = low_back(jnp.dot(context, low(out_w), precision=HIGHEST_PREC))
    hidden1 = hidden0 + attn_out
    normed2 = low(layer_norm(hidden1, gain_w[1]))
    upper_pre = low_back(jnp.dot(normed2, low(up_w), precision=HIGHEST_PREC))
    activation = low(jax.nn.gelu(upper_pre, approximate=False))
    ffn_out = low_back(jnp.dot(activation, low(down_w), precision=HIGHEST_PREC))
    hidden2 = hidden1 + ffn_out
    normed3 = layer_norm(hidden2, gain_w[2])
    logits = jnp.dot(normed3, head_w, precision=HIGHEST_PREC)
    picked = jnp.take_along_axis(logits, target_row[:, None].astype(jnp.int32), axis=1)[:, 0]
    row_loss = jnp.sum(jax.nn.logsumexp(logits, axis=1) - picked)
    return (row_loss, hidden2)

def orthogonalize(matrix):
    iterate = matrix / (jnp.sqrt(jnp.sum(matrix * matrix)) + 1e-07)
    for sweep in range(NS_STEPS):
        gram_mat = jnp.dot(iterate, iterate.T, precision=HIGHEST_PREC)
        poly_mat = SCHULZ_SQUARE * gram_mat + SCHULZ_CUBE * jnp.dot(gram_mat, gram_mat, precision=HIGHEST_PREC)
        iterate = SCHULZ_LINEAR * iterate + jnp.dot(poly_mat, iterate, precision=HIGHEST_PREC)
    return iterate

def muon_weight(weight, ortho_part, longest):
    return weight * (1.0 - MUON_RATE * MUON_DECAY) - MUON_RATE * 0.2 * math.sqrt(longest) * ortho_part

def adam_step(weight, grad_in, first_m, second_m, step_rate, decay_rate):
    first_new = ADAM_BETA_ONE * first_m + (1.0 - ADAM_BETA_ONE) * grad_in
    second_new = ADAM_BETA_TWO * second_m + (1.0 - ADAM_BETA_TWO) * grad_in * grad_in
    first_hat = first_new / (1.0 - ADAM_BETA_ONE ** STEP)
    second_hat = second_new / (1.0 - ADAM_BETA_TWO ** STEP)
    weight_new = weight * (1.0 - step_rate * decay_rate) - step_rate * first_hat / (jnp.sqrt(second_hat) + ADAM_EPS)
    return (first_new, second_new, weight_new)

def reference(noised, targets, timesteps, segments, embedding, out_head, norm_gains, w_qkv, w_out, w_up, w_down, mom_qkv, mom_out, mom_up, mom_down, embed_m, embed_v, head_m, head_v, gains_m, gains_v):
    span_ids = jnp.arange(SPANS).astype(jnp.int32)
    counts = lax.optimization_barrier(jnp.sum((segments[:, None, :] == span_ids[None, :, None]).astype(jnp.int32), axis=2))
    starts = (jnp.cumsum(counts, axis=1) - counts).astype(jnp.int32)
    offsets = (jnp.arange(LEN).astype(jnp.int32)[None, :] - jnp.take_along_axis(starts, segments.astype(jnp.int32), axis=1)).astype(jnp.int32)
    step_time = jnp.take_along_axis(timesteps, segments.astype(jnp.int32), axis=1)
    fixed_part = sinus(step_time, D) + sinus(offsets, D)
    zero_in = jnp.zeros((ROWS, LEN, D), jnp.float32)

    def forward(embed_w, start_in, gain_w, qkv_w, out_w, up_w, down_w, head_w):
        hidden0 = jnp.take(embed_w, noised.astype(jnp.int32), axis=0) + fixed_part + start_in

        def row_step(loss_total, row_data):
            row_loss, hidden2 = row_forward(row_data[0], row_data[1], row_data[2], gain_w, qkv_w, out_w, up_w, down_w, head_w)
            return (loss_total + row_loss, hidden2)
        loss_total, hidden_rows = lax.scan(jax.checkpoint(row_step), jnp.zeros((), jnp.float32), (hidden0, segments, targets))
        return (loss_total, hidden_rows)
    loss_total, pull_back, hidden_rows = jax.vjp(forward, embedding, zero_in, norm_gains, w_qkv, w_out, w_up, w_down, out_head, has_aux=True)
    gradients = pull_back(jnp.ones((), jnp.float32))
    g_embed, input_grad, g_gains, g_qkv, g_out, g_up, g_down, g_head = gradients
    squares = jnp.sum(g_qkv * g_qkv) + jnp.sum(g_out * g_out) + jnp.sum(g_up * g_up) + jnp.sum(g_down * g_down)
    squares = squares + jnp.sum(g_embed * g_embed) + jnp.sum(g_head * g_head) + jnp.sum(g_gains * g_gains)
    grad_norm = jnp.sqrt(squares)
    clip_scale = CLIP_NORM / jnp.maximum(grad_norm, CLIP_NORM)
    mom_qkv_new = MUON_MOMENTUM * mom_qkv + clip_scale * g_qkv
    mom_out_new = MUON_MOMENTUM * mom_out + clip_scale * g_out
    mom_up_new = MUON_MOMENTUM * mom_up + clip_scale * g_up
    mom_down_new = MUON_MOMENTUM * mom_down + clip_scale * g_down
    qkv_new = muon_weight(w_qkv, orthogonalize(mom_qkv_new), 3 * D)
    out_new = muon_weight(w_out, orthogonalize(mom_out_new.T).T, D)
    up_new = muon_weight(w_up, orthogonalize(mom_up_new), max(D, FF))
    down_new = muon_weight(w_down, orthogonalize(mom_down_new.T).T, max(D, FF))
    embed_m_new, embed_v_new, embed_new = adam_step(embedding, clip_scale * g_embed, embed_m, embed_v, EMBED_RATE, WEIGHT_DECAY)
    head_m_new, head_v_new, head_new = adam_step(out_head, clip_scale * g_head, head_m, head_v, HEAD_RATE, WEIGHT_DECAY)
    gains_m_new, gains_v_new, gains_new = adam_step(norm_gains, clip_scale * g_gains, gains_m, gains_v, GAIN_RATE, 0.0)
    return (hidden_rows.astype(jnp.bfloat16), input_grad, grad_norm, mom_qkv_new, qkv_new, mom_out_new, out_new, mom_up_new, up_new, mom_down_new, down_new, embed_m_new, embed_v_new, embed_new, head_m_new, head_v_new, head_new, gains_m_new, gains_v_new, gains_new)
```

```python
from functools import partial
import math

import jax
import jax.numpy as jnp
import numpy as np
from jax import lax
from jax.experimental import pallas as pl
from jax.experimental.pallas import tpu as pltpu
from jax.sharding import PartitionSpec as P

D = 512
HEAD_DIM = 64
PAIR = 2 * HEAD_DIM
FF = 2048
NS_STEPS = 5
STEP = 10
CHUNK = 256
VOCAB_PAD = 32
SPAN_PAD = 16

HIGHEST = lax.Precision.HIGHEST
F32 = jnp.float32
BF16 = jnp.bfloat16
NORM_EPS = 1e-05
MASK_FILL = 1e30
MUON_MOMENTUM = 0.5
MUON_RATE = 0.3
MUON_DECAY = 0.1
SCHULZ_LINEAR = 3.4445
SCHULZ_SQUARE = -4.775
SCHULZ_CUBE = 2.0315
ADAM_BETA_ONE = 0.9
ADAM_BETA_TWO = 0.95
ADAM_EPS = 1e-08
EMBED_RATE = 0.3
HEAD_RATE = 0.02
GAIN_RATE = 0.6
WEIGHT_DECAY = 0.1
CLIP_NORM = 1.0


def nn(left, right, precision=None):
    return lax.dot_general(
        left, right, (((1,), (0,)), ((), ())), preferred_element_type=F32, precision=precision
    )


def nt(left, right, precision=None):
    return lax.dot_general(
        left, right, (((1,), (1,)), ((), ())), preferred_element_type=F32, precision=precision
    )


def tn(left, right, precision=None):
    return lax.dot_general(
        left, right, (((0,), (0,)), ((), ())), preferred_element_type=F32, precision=precision
    )


def halves(values):
    high = values.astype(BF16)
    return high, (values - high.astype(F32)).astype(BF16)


def position_table(length, width):
    half = width // 2
    rates = np.exp(-math.log(10000.0) * np.arange(half) / half)
    angles = np.arange(length)[:, None] * rates[None, :]
    return np.concatenate([np.sin(angles), np.cos(angles)], axis=1).astype(np.float32)


def normed_parts(values):
    centered = values - jnp.mean(values, axis=-1, keepdims=True)
    inv_std = lax.rsqrt(jnp.mean(centered * centered, axis=-1, keepdims=True) + NORM_EPS)
    return centered * inv_std, inv_std


def norm_back(grad_out, source, gain):
    normed, inv_std = normed_parts(source)
    scaled = grad_out * gain
    grad_in = inv_std * (
        scaled
        - jnp.mean(scaled, axis=-1, keepdims=True)
        - normed * jnp.mean(scaled * normed, axis=-1, keepdims=True)
    )
    return grad_in, jnp.sum(grad_out * normed, axis=0, keepdims=True)


def embed_kernel(where_ref, tok_ref, seg_ref, table_ref, emb_ref, gains_ref, h0_ref, a1_ref, aug_ref, rows_ref):
    vocab, width = emb_ref.shape
    half = width // 2
    blocks, size = tok_ref.shape
    spans = SPAN_PAD // 4
    rows_ref[...] = jnp.zeros_like(rows_ref)
    rows_ref[0:vocab, 0:width] = emb_ref[...]
    for span in range(spans):
        at_time = table_ref[pl.ds(where_ref[8 + span], 1), :]
        at_start = table_ref[pl.ds(where_ref[12 + span], 1), :]
        row = VOCAB_PAD + span
        rows_ref[row : row + 1, 0:width] = at_time
        rows_ref[row : row + 1, width : width + half] = at_start[:, half:]
        rows_ref[row : row + 1, width + half :] = at_start[:, :half]
    rows = rows_ref[...]
    high = rows.astype(BF16)
    rest = rows - high.astype(F32)
    middle = rest.astype(BF16)
    low = (rest - middle.astype(F32)).astype(BF16)
    stacked = jnp.concatenate([high, middle, low], axis=0)
    gain = gains_ref[0:1, :]
    for block in range(blocks):
        tok = tok_ref[block : block + 1, :]
        seg = seg_ref[pl.ds(where_ref[block], 1), :]
        hot_tok = (lax.broadcasted_iota(jnp.int32, (VOCAB_PAD, size), 0) == tok).astype(F32)
        hot_seg = (lax.broadcasted_iota(jnp.int32, (SPAN_PAD, size), 0) == seg).astype(F32)
        hot = jnp.concatenate([hot_tok, hot_seg], axis=0).astype(BF16)
        picked = tn(jnp.concatenate([hot, hot, hot], axis=0), stacked)
        table = table_ref[pl.ds(pl.multiple_of(where_ref[4 + block] * size, size), size), :]
        sin_p, cos_p = table[:, :half], table[:, half:]
        cos_s, sin_s = picked[:, width : width + half], picked[:, width + half :]
        place = jnp.concatenate([sin_p * cos_s - cos_p * sin_s, cos_p * cos_s + sin_p * sin_s], axis=1)
        hidden = picked[:, :width] + place
        if block * size < h0_ref.shape[0]:
            h0_ref[block * size : (block + 1) * size, :] = hidden
        a1_ref[block * size : (block + 1) * size, :] = (normed_parts(hidden)[0] * gain).astype(BF16)
        wide = (lax.broadcasted_iota(jnp.int32, (PAIR, size), 0) == seg).astype(F32)
        aug_ref[block * size : (block + 1) * size, :] = jnp.transpose(wide).astype(BF16)


def query_side(aug, own):
    return ((aug[:own].astype(F32) - 1.0) * MASK_FILL).astype(BF16)


def half_mask(values, head):
    lanes = lax.broadcasted_iota(jnp.int32, values.shape, 1)
    keep = (lanes >= head * HEAD_DIM) & (lanes < (head + 1) * HEAD_DIM)
    return jnp.where(keep, values.astype(F32), 0.0).astype(BF16)


def query_side(aug, own):
    return ((aug[:own].astype(F32) - 1.0) * MASK_FILL).astype(BF16)


def half_mask(values, head):
    lanes = lax.broadcasted_iota(jnp.int32, values.shape, 1)
    keep = (lanes >= head * HEAD_DIM) & (lanes < (head + 1) * HEAD_DIM)
    return jnp.where(keep, values.astype(F32), 0.0).astype(BF16)


def heads_apart(rows, back):
    count = rows.shape[0] // HEAD_DIM
    heads = count // 3
    if back:
        index = [j * heads + h for h in range(heads) for j in range(3)]
    else:
        index = [h * 3 + j for j in range(3) for h in range(heads)]
    return jnp.concatenate([rows[i * HEAD_DIM : (i + 1) * HEAD_DIM] for i in index], axis=0)


def attention_weights_kernel(wq_ref, wo_ref, out_ref):
    wide = wq_ref.shape[1]
    out_ref[0:wide, :] = heads_apart(jnp.transpose(wq_ref[...]), False).astype(BF16)
    out_ref[wide:, :] = wo_ref[...].astype(BF16)


def ffn_weights_kernel(wu_ref, wd_ref, out_ref):
    units = wu_ref.shape[1]
    out_ref[0:units, :] = jnp.transpose(wu_ref[...]).astype(BF16)
    out_ref[units:, :] = wd_ref[...].astype(BF16)


def attend_kernel(a1_ref, aug_ref, w0, w1, qkv_ref, ctx_ref, lse_ref):
    own = ctx_ref.shape[1]
    scale = HEAD_DIM**-0.5
    aug = aug_ref[...]
    aug_q = query_side(aug, own)
    for shard, weight in enumerate((w0, w1)):
        qkv = nt(a1_ref[...], weight[0 : 3 * PAIR, :]).astype(BF16)
        qkv_ref[shard] = qkv
        keys = jnp.concatenate([qkv[:, PAIR : 2 * PAIR], aug], axis=1)
        value = qkv[:, 2 * PAIR :]
        query = qkv[:own, :PAIR].astype(F32) * scale
        for head in range(2):
            q_side = jnp.concatenate([half_mask(query, head), aug_q], axis=1)
            scores = nt(keys, q_side)
            top = jnp.max(scores, axis=0, keepdims=True)
            weights = jnp.exp(scores - top)
            total = jnp.sum(weights, axis=0, keepdims=True)
            out = tn(value, weights.astype(BF16))
            at = shard * PAIR + head * HEAD_DIM
            ctx_ref[at : at + HEAD_DIM, :] = out[head * HEAD_DIM : (head + 1) * HEAD_DIM] / total
            lse_ref[2 * shard + head : 2 * shard + head + 1, :] = top + jnp.log(total)


def two_way_slot(across, piece, mine):
    b0, b1 = (piece ^ mine) & 1, lax.shift_right_logical(piece ^ mine, 1) & 1
    if piece < 4:
        return across * 4 + b0 * 2 + b1
    return 8 + b0 * 4 + across * 2 + b1


def one_way_slot(piece, mine):
    return ((piece ^ mine) & 1) * 4 + piece // 2


def gelu_parts(upper):
    size = jnp.abs(upper)
    pdf = jnp.exp(-0.5 * upper * upper) * (1.0 / math.sqrt(2.0 * math.pi))
    turn = 1.0 / (1.0 + 0.2316419 * size)
    series = turn * (
        0.319381530
        + turn * (-0.356563782 + turn * (1.781477937 + turn * (-1.821255978 + turn * 1.330274429)))
    )
    tail = pdf * series
    cdf = jnp.where(upper < 0.0, tail, 1.0 - tail)
    return (upper * cdf).astype(BF16), (cdf + upper * pdf).astype(BF16)


def up_chunks(a2_ref, packs, act_ref, slope_ref, acc_ref, first):
    units = packs[0].shape[0] // 2
    for at, pack in enumerate(packs):

        def step(part, carry, at=at, pack=pack):
            chunk = first + at * (units // CHUNK) + part
            up_rows = pl.ds(pl.multiple_of(part * CHUNK, CHUNK), CHUNK)
            down_rows = pl.ds(pl.multiple_of(units + part * CHUNK, CHUNK), CHUNK)
            act, slope = gelu_parts(nt(a2_ref[...], pack[up_rows, :]))
            act_ref[chunk] = act
            slope_ref[chunk] = slope
            acc_ref[...] += nn(act, pack[down_rows, :])
            return carry

        lax.fori_loop(0, units // CHUNK, step, 0)


def ffn_up_kernel(
    ctx_a_ref, ctx_b_ref, h0_ref, gains_ref, wa0, wa1, wa2, wa3, wb0, wb1,
    h1_ref, acc_ref, a2_ref, act_ref, slope_ref,
):
    hidden1 = h0_ref[...]
    for ctx_ref, first, second in ((ctx_a_ref, wa0, wa1), (ctx_b_ref, wa2, wa3)):
        weight = jnp.concatenate([first[3 * PAIR :, :], second[3 * PAIR :, :]], axis=0)
        hidden1 = hidden1 + tn(ctx_ref[...].astype(BF16), weight)
    h1_ref[...] = hidden1
    acc_ref[...] = hidden1
    a2_ref[...] = (normed_parts(hidden1)[0] * gains_ref[1:2, :]).astype(BF16)
    up_chunks(a2_ref, (wb0, wb1), act_ref, slope_ref, acc_ref, 0)


def ffn_kernel(
    vocab, dp_ref, ctx_a_ref, ctx_b_ref, h1_ref, part_ref, a2_ref, head_ref, gains_ref, tgt_ref, act_a_ref, slope_a_ref,
    wb0, wb1, wb2, wb3,
    out_ref, dh1_ref, dattn_ref, keep_ref, send_ref, small_ref,
    act_ref, slope_ref, acc_ref, dffn_ref,
):
    own, width = h1_ref.shape
    near = act_a_ref.shape[0]
    chunks = 2 * near
    shards = 4
    per_shard = chunks // shards
    unit_rows = per_shard * CHUNK
    mine = dp_ref[0]
    acc_ref[...] = part_ref[...]
    act_ref[0:near] = act_a_ref[...]
    slope_ref[0:near] = slope_a_ref[...]
    up_chunks(a2_ref, (wb2, wb3), act_ref, slope_ref, acc_ref, near)
    hidden2 = acc_ref[...]
    out_ref[...] = hidden2.astype(BF16)
    normed3, _ = normed_parts(hidden2)
    a3 = normed3 * gains_ref[2:3, :]
    head = head_ref[...]
    logits = nt(head, a3, HIGHEST)
    classes = lax.broadcasted_iota(jnp.int32, logits.shape, 0)
    logits = jnp.where(classes < vocab, logits, -MASK_FILL)
    raised = jnp.exp(logits - jnp.max(logits, axis=0, keepdims=True))
    targets = jnp.concatenate([tgt_ref[0:1, :], tgt_ref[1:2, :]], axis=1)
    d_logits = raised / jnp.sum(raised, axis=0, keepdims=True) - (classes == targets).astype(F32)
    small_ref[0:VOCAB_PAD, :] = nn(d_logits, a3, HIGHEST)
    d_h2, g_gain2 = norm_back(tn(d_logits, head, HIGHEST), hidden2, gains_ref[2:3, :])
    dffn_ref[...] = d_h2.astype(BF16)
    acc_ref[...] = jnp.zeros_like(acc_ref)

    def spread(target, across, first, at, values):
        rows = first.stop - first.start
        count = values.shape[0] // rows
        for piece in range(count):
            slot = two_way_slot(across, at + piece, mine)
            target[slot, first, :] = values[piece * rows : (piece + 1) * rows].astype(BF16)

    unit_slice = unit_rows // 8

    for shard, pack in enumerate((wb0, wb1, wb2, wb3)):
        target = send_ref if shard % 2 else keep_ref
        for part in range(per_shard):
            chunk = shard * per_shard + part
            at = part * CHUNK // unit_slice
            up_rows = slice(part * CHUNK, (part + 1) * CHUNK)
            down_rows = slice(unit_rows + part * CHUNK, unit_rows + (part + 1) * CHUNK)
            d_act = nt(dffn_ref[...], pack[down_rows, :])
            d_up = (d_act * slope_ref[chunk].astype(F32)).astype(BF16)
            spread(target, shard // 2, slice(0, unit_slice), at, tn(d_up, a2_ref[...]))
            spread(target, shard // 2, slice(unit_slice, 2 * unit_slice), at, tn(act_ref[chunk], dffn_ref[...]))
            acc_ref[...] += nn(d_up, pack[up_rows, :])
    d_h1_part, g_gain1 = norm_back(acc_ref[...], h1_ref[...], gains_ref[1:2, :])
    d_h1 = d_h2 + d_h1_part
    dh1_ref[...] = d_h1
    d_attn = d_h1.astype(BF16)
    dattn_ref[...] = d_attn
    out_rows = 2 * ctx_a_ref.shape[0] // shards
    for across, ctx_ref in enumerate((ctx_a_ref, ctx_b_ref)):
        g_out = nn(ctx_ref[...].astype(BF16), d_attn)
        for core in range(2):
            spread(
                send_ref if core else keep_ref, across, slice(2 * unit_slice, 2 * unit_slice + out_rows // 8), 0,
                g_out[core * out_rows : (core + 1) * out_rows],
            )
    small_ref[VOCAB_PAD:, :] = jnp.concatenate(
        [jnp.zeros_like(g_gain1), g_gain1, g_gain2, jnp.zeros((5, width), F32)], axis=0
    )


def attend_back_kernel(qkv_ref, aug_ref, ctx_ref, lse_ref, dattn_ref, w0, w1, dq_ref, near_ref, far_ref):
    own = ctx_ref.shape[1]
    scale = HEAD_DIM**-0.5
    aug = aug_ref[...]
    aug_q = query_side(aug, own)
    d_attn = dattn_ref[...]
    for shard, weight_ref in enumerate((w0, w1)):
        weight = weight_ref[3 * PAIR :, :]
        d_ctx = nt(d_attn, weight).astype(BF16)
        d_ctx_t = nt(weight, d_attn).astype(BF16).astype(F32)
        inner = d_ctx_t * ctx_ref[shard * PAIR : (shard + 1) * PAIR, :]
        key = qkv_ref[shard, :, PAIR : 2 * PAIR]
        value = qkv_ref[shard, :, 2 * PAIR :]
        keys = jnp.concatenate([key, aug], axis=1)
        query = qkv_ref[shard, 0:own, 0:PAIR].astype(F32) * scale
        dq_parts = []
        d_key = None
        d_value = None
        for head in range(2):
            mine = slice(head * HEAD_DIM, (head + 1) * HEAD_DIM)
            q_head = half_mask(query, head)
            scores = nt(keys, jnp.concatenate([q_head, aug_q], axis=1))
            probs = jnp.exp(scores - lse_ref[2 * shard + head : 2 * shard + head + 1, :])
            d_ctx_head = half_mask(d_ctx, head)
            d_probs = nt(value, d_ctx_head)
            delta = jnp.sum(inner[mine], axis=0, keepdims=True)
            d_scores = (probs * (d_probs - delta)).astype(BF16)
            d_value_part = nn(probs.astype(BF16), d_ctx_head)
            d_key_part = nn(d_scores, q_head)
            dq_parts.append(tn(key, d_scores)[mine])
            d_key = d_key_part if d_key is None else d_key + d_key_part
            d_value = d_value_part if d_value is None else d_value + d_value_part
        dq_ref[shard] = jnp.transpose(jnp.concatenate(dq_parts, axis=0) * scale).astype(BF16)
        near_ref[shard, :, 0:PAIR] = d_key[:own].astype(BF16)
        near_ref[shard, :, PAIR:] = d_value[:own].astype(BF16)
        far_ref[shard ^ 1, :, 0:PAIR] = d_key[own:].astype(BF16)
        far_ref[shard ^ 1, :, PAIR:] = d_value[own:].astype(BF16)


def qkv_grads(dp_ref, dq_ref, near_ref, far_ref, a1, weights, keep_ref, send_ref, total):
    for shard, weight in enumerate(weights):
        d_kv = (near_ref[shard].astype(F32) + far_ref[shard].astype(F32)).astype(BF16)
        d_qkv = jnp.concatenate([dq_ref[shard], d_kv], axis=1)
        grad = tn(d_qkv, a1)
        target = send_ref if shard else keep_ref
        rows = grad.shape[0] // 8
        for piece in range(8):
            target[one_way_slot(piece, dp_ref[0])] = grad[piece * rows : (piece + 1) * rows].astype(BF16)
        part = nn(d_qkv, weight[0 : 3 * PAIR, :])
        total = part if total is None else total + part
    return total


def input_far_kernel(dp_ref, dq_ref, near_ref, far_ref, a1_ref, w0, w1, total_ref, keep_ref, send_ref):
    own = total_ref.shape[0]
    total_ref[...] = qkv_grads(dp_ref, dq_ref, near_ref, far_ref, a1_ref[0:own, :], (w0, w1), keep_ref, send_ref, None)


def input_kernel(
    dp_ref, dq_ref, near_ref, far_ref, a1_ref, w0, w1, total_ref, h0_ref, dh1_ref, gains_ref, tok_ref, part_ref,
    igrad_ref, keep_ref, send_ref, small_ref, rows_ref,
):
    own, width = h0_ref.shape
    vocab = 27
    d_a1 = qkv_grads(
        dp_ref, dq_ref, near_ref, far_ref, a1_ref[0:own, :], (w0, w1), keep_ref, send_ref, total_ref[...]
    )
    d_h0_part, g_gain0 = norm_back(d_a1, h0_ref[...], gains_ref[0:1, :])
    d_h0 = dh1_ref[...] + d_h0_part
    igrad_ref[...] = d_h0
    high, low = halves(d_h0)
    tok = jnp.concatenate([tok_ref[0:1, :], tok_ref[1:2, :]], axis=1)
    hot = (lax.broadcasted_iota(jnp.int32, (VOCAB_PAD, own), 0) == tok).astype(F32).astype(BF16)
    rows_ref[...] = jnp.zeros_like(rows_ref)
    rows_ref[0:vocab, :] = part_ref[0:vocab, :]
    rows_ref[vocab : 2 * vocab, :] = (nn(hot, high) + nn(hot, low))[0:vocab]
    rows_ref[2 * vocab : 2 * vocab + 1, :] = g_gain0
    rows_ref[2 * vocab + 1 : 2 * vocab + 3, :] = part_ref[VOCAB_PAD + 1 : VOCAB_PAD + 3, :]
    for piece in range(8):
        small_ref[one_way_slot(piece, dp_ref[0])] = rows_ref[piece * 8 : (piece + 1) * 8, :]


def adam_step(weight, grad, first_m, second_m, rate, decay):
    first_new = ADAM_BETA_ONE * first_m + (1.0 - ADAM_BETA_ONE) * grad
    second_new = ADAM_BETA_TWO * second_m + (1.0 - ADAM_BETA_TWO) * grad * grad
    first_hat = first_new / (1.0 - ADAM_BETA_ONE**STEP)
    second_hat = second_new / (1.0 - ADAM_BETA_TWO**STEP)
    weight_new = weight * (1.0 - rate * decay) - rate * first_hat / (jnp.sqrt(second_hat) + ADAM_EPS)
    return first_new, second_new, weight_new


def gram_triangle(store, values, product):
    high, low = halves(values)
    half = store.shape[1]

    def part(side, at):
        return side[at * half : (at + 1) * half, :] if product is nt else side[:, at * half : (at + 1) * half]

    for at, (i, j) in enumerate(((0, 0), (0, 1), (1, 1))):
        store[at * half : (at + 1) * half, :] = (
            product(part(high, i), part(high, j))
            + product(part(high, i), part(low, j))
            + product(part(low, i), part(high, j))
        )


def momentum_kernel(place_ref, clip_ref, *refs):
    g1_refs, g2_refs = refs[0:4], refs[4:6]
    (
        mq_ref, mo_ref, mu_ref, md_ref,
        emb_ref, emb_m_ref, emb_v_ref, head_ref, head_m_ref, head_v_ref, gain_ref, gain_m_ref, gain_v_ref,
        near_ref, far_ref, mq_out, mo_out, mu_out, md_out,
        emb_m_out, emb_v_out, emb_out, head_m_out, head_v_out, head_out, gain_m_out, gain_v_out, gain_out,
        all_ref, rows_ref, pack_ref,
    ) = refs[6:]
    dp, across, core, side = place_ref[0], place_ref[1], place_ref[2], place_ref[3]
    clip = clip_ref[0]
    units = mu_ref.shape[1]
    out_rows = mo_ref.shape[0]
    wide = mq_ref.shape[1]
    parts1 = ((units // 8, 0, 0), (units // 8, units // 8, units), (out_rows // 8, units // 4, 2 * units))
    parts2 = ((wide // 8, 0, 2 * units + out_rows),)

    def place(source, parts, piece):
        for rows, at, base in parts:
            to = pl.ds(pl.multiple_of(base + piece * rows, 8), rows)
            all_ref[to, :] = clip * source[at : at + rows, :].astype(F32)

    for turn in range(4):
        first = turn ^ (dp & 3)
        for high in range(2):
            place(g1_refs[turn].at[high], parts1, 4 * high + first)
    for turn in range(2):
        first = turn ^ (dp & 1)
        for high in range(4):
            piece = 2 * high + first
            place(g2_refs[turn].at[high], parts2, piece)
            tail = g2_refs[turn][high].astype(F32)[wide // 8 :, :]
            rows_ref[pl.ds(pl.multiple_of(piece * 8, 8), 8), :] = clip * tail
    mu_out[...] = MUON_MOMENTUM * mu_ref[...] + jnp.transpose(all_ref[0:units, :])
    md_out[...] = MUON_MOMENTUM * md_ref[...] + all_ref[units : 2 * units, :]
    mo_out[...] = MUON_MOMENTUM * mo_ref[...] + all_ref[2 * units : 2 * units + out_rows, :]
    mq_out[...] = MUON_MOMENTUM * mq_ref[...] + jnp.transpose(
        heads_apart(all_ref[2 * units + out_rows :, :], True)
    )

    def grams(*pair):
        for index, (out_ref, product) in enumerate(pair):
            gram_triangle(pack_ref, out_ref[...], product)
            half = pack_ref.shape[0] // 2
            slot = index ^ across
            near_ref[slot] = pack_ref[pl.ds(pl.multiple_of(core * half, 8), half), :]
            far_ref[slot] = pack_ref[pl.ds(pl.multiple_of((1 - core) * half, 8), half), :]

    @pl.when(side == 0)
    def _():
        grams((mu_out, nt), (mo_out, tn))

    @pl.when(side == 1)
    def _():
        grams((mq_out, nt), (md_out, tn))

    vocab = emb_ref.shape[0]
    head_m_out[...], head_v_out[...], head_out[...] = adam_step(
        head_ref[...], rows_ref[0:vocab, :], head_m_ref[...], head_v_ref[...], HEAD_RATE, WEIGHT_DECAY
    )
    emb_m_out[...], emb_v_out[...], emb_out[...] = adam_step(
        emb_ref[...], rows_ref[vocab : 2 * vocab, :], emb_m_ref[...], emb_v_ref[...], EMBED_RATE, WEIGHT_DECAY
    )
    gain_m_out[...], gain_v_out[...], gain_out[...] = adam_step(
        gain_ref[...], rows_ref[2 * vocab : 2 * vocab + 3, :], gain_m_ref[...], gain_v_ref[...], GAIN_RATE, 0.0
    )


def three(left, right):
    left_high, left_low = halves(left)
    right_high, right_low = halves(right)
    return nn(left_high, right_high) + nn(left_high, right_low) + nn(left_low, right_high)


def once(left, right):
    return nn(left.astype(BF16), right.astype(BF16))


def schulz_kernel(core_ref, mine_ref, other_ref, near_ref, far_ref, pack_ref, poly_ref, gram_ref, tri_ref):
    half, block = mine_ref.shape
    size = 2 * block
    core = core_ref[0]
    pack_ref[pl.ds(pl.multiple_of(core * half, 8), half), :] = mine_ref[...]
    pack_ref[pl.ds(pl.multiple_of((1 - core) * half, 8), half), :] = other_ref[...]
    gram_ref[0:block, 0:block] = pack_ref[0:block, :]
    corner = pack_ref[block:size, :]
    gram_ref[0:block, block:] = corner
    gram_ref[block:, 0:block] = jnp.transpose(corner)
    gram_ref[block:, block:] = pack_ref[size:, :]
    gram = gram_ref[...]
    rows = lax.broadcasted_iota(jnp.int32, gram.shape, 0)
    columns = lax.broadcasted_iota(jnp.int32, gram.shape, 1)
    diagonal = rows == columns
    trace = jnp.sum(jnp.where(diagonal, gram, 0.0))
    inverse = 1.0 / (jnp.sqrt(jnp.full((1, size), trace, F32)) + 1e-07)
    gram = gram * (inverse * inverse)

    def sweep(gram, poly, times, last=False):
        change = SCHULZ_SQUARE * gram + SCHULZ_CUBE * times(gram, gram)
        if poly is None:
            poly_ref[...] = change * inverse + jnp.where(diagonal, SCHULZ_LINEAR * inverse, 0.0)
        else:
            poly_ref[...] = SCHULZ_LINEAR * poly + times(change, poly)
        if not last:
            moved = SCHULZ_LINEAR * gram + times(change, gram)
            gram_ref[...] = SCHULZ_LINEAR * moved + times(moved, change)

    sweep(gram, None, once)
    sweep(gram_ref[...], poly_ref[...], once)
    sweep(gram_ref[...], poly_ref[...], once)
    for index in range(3, NS_STEPS):
        sweep(gram_ref[...], poly_ref[...], three, index == NS_STEPS - 1)
    poly = poly_ref[...]
    spine = jnp.sum(jnp.where(diagonal, poly, 0.0), axis=0, keepdims=True)
    off = jnp.where(diagonal, 0.0, poly).astype(BF16)
    high = spine.astype(BF16).astype(F32)
    low = spine - high
    rest = jnp.zeros((14, block), F32)
    tops = [
        jnp.concatenate([high[:, at], low[:, at], rest], axis=0).astype(BF16)
        for at in (slice(0, block), slice(block, size))
    ]
    part = half - block
    tri_ref[0, 0:block, :] = off[0:block, 0:block]
    tri_ref[0, block:half, :] = off[0:part, block:]
    tri_ref[0, half:, :] = tops[0]
    tri_ref[1, 0 : block - part, :] = off[part:block, block:]
    tri_ref[1, block - part : half, :] = off[block:, block:]
    tri_ref[1, half:, :] = tops[1]
    near_ref[...] = tri_ref[core]
    far_ref[...] = tri_ref[1 - core]


def muon_kernel(
    place_ref, mq_ref, mo_ref, mu_ref, md_ref, near0, near1, near2, near3, far0, far1, far2, far3,
    wq_ref, wo_ref, wu_ref, wd_ref, wq_out, wo_out, wu_out, wd_out, tri_ref,
):
    across, core, side = place_ref[1], place_ref[2], place_ref[3]
    held = 2 * side + across
    for at, (near, far) in enumerate(((near0, far0), (near1, far1), (near2, far2), (near3, far3))):
        tri_ref[at, core] = near[...]
        tri_ref[at, 1 - core] = far[...]
    block = near0.shape[1]
    half = near0.shape[0] - 16
    part = half - block

    def ortho(matrix, values, left):
        slot = matrix ^ held
        first = tri_ref[slot, 0]
        second = tri_ref[slot, 1]
        corner = jnp.concatenate([first[block:half], second[0 : block - part]], axis=0)
        upper = jnp.concatenate([first[0:block], corner], axis=1)
        lower = jnp.concatenate([jnp.transpose(corner), second[block - part : half]], axis=1)
        poly = jnp.concatenate([upper, lower], axis=0)
        spines = [tri[half:].astype(F32) for tri in (first, second)]
        spine = jnp.concatenate([s[0:1] + s[1:2] for s in spines], axis=1)
        if left:
            spine = jnp.transpose(jnp.broadcast_to(spine, (8, 2 * block)))[:, 0:1]
            return nn(poly, values.astype(BF16)) + values * spine
        return nn(values.astype(BF16), poly) + values * spine

    def moved(weight, ortho, longest):
        return weight * (1.0 - MUON_RATE * MUON_DECAY) - MUON_RATE * 0.2 * math.sqrt(longest) * ortho

    wu_out[...] = moved(wu_ref[...], ortho(0, mu_ref[...], True), max(D, FF))
    wo_out[...] = moved(wo_ref[...], ortho(1, mo_ref[...], False), D)
    wq_out[...] = moved(wq_ref[...], ortho(2, mq_ref[...], True), 3 * D)
    wd_out[...] = moved(wd_ref[...], ortho(3, md_ref[...], False), max(D, FF))


VMEM = pl.BlockSpec(memory_space=pltpu.VMEM)
SMEM = pl.BlockSpec(memory_space=pltpu.SMEM)
VMEM_LIMIT = 30 * 1024 * 1024


def call(body, name, ins, outs, scratch=(), scalars=0, plain=(), far=(), micros=1):
    shapes = [
        jax.ShapeDtypeStruct(shape, dtype) if at in far else pltpu.VMEM(shape, dtype)
        for at, (shape, dtype) in enumerate(outs)
    ]
    held = [
        value if at < scalars or at in plain else pltpu.with_memory_space_constraint(value, pltpu.VMEM)
        for at, value in enumerate(ins)
    ]
    return pl.pallas_call(
        body,
        name=name,
        out_shape=shapes,
        in_specs=[SMEM] * scalars + [VMEM] * (len(ins) - scalars),
        out_specs=[VMEM] * len(shapes),
        scratch_shapes=list(scratch),
        compiler_params=pltpu.CompilerParams(vmem_limit_bytes=VMEM_LIMIT),
        cost_estimate=pl.CostEstimate(flops=micros * 10**8, bytes_accessed=0, transcendentals=0),
    )(*held)


def swap(values, bit):
    return lax.ppermute(values, "tensor", [(i, i ^ bit) for i in range(4)])


def swap_dp(values, bit):
    return lax.ppermute(values, "dp", [(i, i ^ bit) for i in range(lax.axis_size("dp"))])


def swap_both(values, bit, dp_bit):
    width = lax.axis_size("tensor")
    pairs = [
        (p * width + t, (p ^ dp_bit) * width + (t ^ bit)) for p in range(lax.axis_size("dp")) for t in range(width)
    ]
    return lax.ppermute(values, ("dp", "tensor"), pairs)


def add(left, right):
    return (left.astype(F32) + right.astype(F32)).astype(BF16)


def after(values, done):
    return lax.optimization_barrier((values, done))[0]


def over_rest(piece):
    bit = 8
    while bit < lax.axis_size("dp"):
        piece = add(piece, swap_dp(piece, bit))
        bit *= 2
    return piece


def on_device(
    noised, targets, timesteps, segments, embedding, out_head, norm_gains,
    w_qkv, w_out, w_up, w_down, mom_qkv, mom_out, mom_up, mom_down,
    embed_m, embed_v, head_m, head_v, gains_m, gains_v,
):
    place = lax.axis_index("tensor")
    group = lax.axis_index("dp") & 7
    row = place // 2
    core = place % 2
    size = noised.shape[1]
    length = segments.shape[1]
    own = 2 * size
    vocab = embedding.shape[0]
    order = jnp.stack([place, place ^ 2, place ^ 1, place ^ 3])
    group_ref = group.reshape(1).astype(jnp.int32)
    places = jnp.stack([group, row, core, group & 1]).astype(jnp.int32)

    ids = jnp.stack([noised, targets])
    mine = lax.dynamic_index_in_dim(ids, row, 1, keepdims=False)
    got = swap(lax.dynamic_index_in_dim(ids, 1 - row, 1, keepdims=False), 2)
    own_ids = jnp.stack([mine, got], axis=1)
    tok = jnp.concatenate([own_ids[0], swap(own_ids[0], 1)], axis=0)
    seg_row = lax.dynamic_index_in_dim(segments, row, 0, keepdims=False)
    span_ids = jnp.arange(timesteps.shape[1], dtype=jnp.int32)
    starts = jnp.sum((seg_row[None, :] < span_ids[:, None]).astype(jnp.int32), axis=1)
    times = lax.dynamic_index_in_dim(timesteps, row, 0, keepdims=False)
    where = jnp.concatenate([row * 4 + order, order, times, starts]).astype(jnp.int32)
    table = jnp.asarray(position_table(max(length, 1000), D))

    unit_rows = w_up.shape[1]
    out_rows = w_out.shape[0]
    (wa_mine,) = call(
        attention_weights_kernel, "attention_weights", [w_qkv, w_out], [((3 * PAIR + out_rows, D), BF16)], plain=(0, 1)
    )
    wa_across = swap(after(wa_mine, got), 2)

    hidden0, a1, aug = call(
        embed_kernel, "embed",
        [where, tok, segments.reshape(-1, size), table, embedding, norm_gains],
        [((own, D), F32), ((length, D), BF16), ((length, PAIR), BF16)],
        [pltpu.VMEM((VOCAB_PAD + SPAN_PAD, 2 * D), F32)],
        scalars=1, plain=(2, 3, 4, 5), micros=4,
    )

    def attend(first, second):
        return call(
            attend_kernel, "attend", [a1, aug, first, second],
            [((2, length, 3 * PAIR), BF16), ((2 * PAIR, own), F32), ((4, own), F32)], micros=7,
    )

    (wb_mine,) = call(
        ffn_weights_kernel, "ffn_weights", [after(w_up, a1), w_down], [((2 * unit_rows, D), BF16)], plain=(0, 1)
    )
    wb_across = swap(wb_mine, 2)
    wa = [wa_mine, swap(wa_mine, 1)]
    qkv_a, ctx_a, lse_a = attend(*wa)
    wa_across = after(wa_across, ctx_a)
    wa += [wa_across, swap(wa_across, 1)]
    qkv_b, ctx_b, lse_b = attend(*wa[2:])
    wb = [wb_mine, swap(wb_mine, 1)]
    head_t = jnp.pad(out_head.T, ((0, VOCAB_PAD - vocab), (0, 0)))
    half_chunks = FF // CHUNK // 2
    hidden1, partial2, a2, act_a, slope_a = call(
        ffn_up_kernel, "ffn_up", [ctx_a, ctx_b, hidden0, norm_gains, *wa, *wb],
        [((own, D), F32), ((own, D), F32), ((own, D), BF16)] + [((half_chunks, own, CHUNK), BF16)] * 2,
        plain=(3,), micros=7,
    )
    wb_across = after(wb_across, a2)
    wb += [wb_across, swap(wb_across, 1)]
    rows1 = (2 * unit_rows + out_rows) // 8
    hidden2, d_h1, d_attn, keep1, send1, part = call(
        partial(ffn_kernel, vocab), "ffn",
        [group_ref, ctx_a, ctx_b, hidden1, partial2, a2, head_t, norm_gains, own_ids[1], act_a, slope_a, *wb],
        [
            ((own, D), BF16), ((own, D), F32), ((own, D), BF16),
            ((16, rows1, D), BF16), ((16, rows1, D), BF16), ((VOCAB_PAD + 8, D), F32),
        ],
        [
            pltpu.VMEM((2 * half_chunks, own, CHUNK), BF16),
            pltpu.VMEM((2 * half_chunks, own, CHUNK), BF16),
            pltpu.VMEM((own, D), F32),
            pltpu.VMEM((own, D), BF16),
        ],
        scalars=1, plain=(7,), micros=17,
    )

    def back(qkv, ctx, lse, d_attn, weights):
        return call(
            attend_back_kernel, "attend_back", [qkv, aug, ctx, lse, d_attn, *weights],
            [((2, own, PAIR), BF16), ((2, own, 2 * PAIR), BF16), ((2, own, 2 * PAIR), BF16)], micros=10,
    )

    got1 = swap(send1, 1)
    dq_b, near_b, far_b = back(qkv_b, ctx_b, lse_b, d_attn, wa[2:])
    got1 = after(got1, dq_b)
    send_x = add(keep1[4:8], got1[4:8])
    send_y = add(keep1[12:16], got1[12:16])
    got_x, got_y = swap(send_x, 2), swap_dp(send_y, 1)
    far_b = swap(far_b, 1)
    dq_a, near_a, far_a = back(qkv_a, ctx_a, lse_a, after(d_attn, (send_x, send_y)), wa[:2])
    far_a = swap(far_a, 1)
    grads = [((own, D), F32), ((8, 48, D), BF16), ((8, 48, D), BF16)]
    d_a1, keep2_b, send2_b = call(
        input_far_kernel, "input_far", [group_ref, dq_b, near_b, far_b, a1, *wa[2:]], grads, scalars=1, micros=4
    )
    got2_b = swap(send2_b, 1)
    got_x, got_y, d_a1 = lax.optimization_barrier((got_x, got_y, d_a1))
    half_a = add(add(keep1[0:4], got1[0:4]), got_x)
    half_b = add(add(keep1[8:12], got1[8:12]), got_y)
    d_a1 = after(d_a1, (half_a, half_b))
    got_y, got_x = swap_dp(half_a[2:4], 1), swap(half_b[2:4], 2)
    igrad, keep2, send2, small = call(
        input_kernel, "input_grad",
        [group_ref, dq_a, near_a, far_a, a1, *wa[:2], d_a1, hidden0, d_h1, norm_gains, tok, part],
        grads + [((8, 8, D), F32)], [pltpu.VMEM((64, D), F32)], scalars=1, plain=(10,), micros=5,
    )
    got_x, got_y, send2, small = lax.optimization_barrier((got_x, got_y, send2, small))
    got2 = swap(send2, 1)
    small = small.astype(BF16)
    got_small = swap(small, 1)
    got2_b = after(got2_b, igrad)
    send2_x = jnp.concatenate([add(keep2_b, got2_b), add(small, got_small)], axis=1)
    got2_x = swap(send2_x, 2)
    half_a = add(half_a[0:2], got_y)
    half_b = add(half_b[0:2], got_x)
    rows2 = jnp.concatenate([keep2.astype(F32) + got2.astype(F32), add(small, got_small).astype(F32)], axis=1)
    rows2 = rows2 + got2_x.astype(F32)
    rows2 = (rows2[0:4] + swap_dp(rows2[4:8].astype(BF16), 1).astype(F32)).astype(BF16)
    quarter = add(jnp.stack([half_a[0], half_b[0]]), swap_dp(jnp.stack([half_a[1], half_b[1]]), 2))
    rows2 = add(rows2, swap_dp(rows2, 2))
    quarter = over_rest(add(quarter, swap_dp(quarter, 4)))
    rows2 = over_rest(add(rows2, swap_dp(rows2, 4)))
    quarter_z = swap_dp(quarter, 2)
    g1 = [quarter, swap_dp(quarter, 1), quarter_z, swap_dp(quarter_z, 1)]
    g2 = [rows2, swap_dp(rows2, 1)]

    out_got = swap(after(hidden2[size:], igrad), 2)
    igrad_got = swap(igrad[size:].astype(BF16), 2)

    def squares(values):
        return jnp.sum(jnp.square(values.astype(F32)))

    square = squares(quarter) + squares(quarter_z) + squares(rows2[:, 0:48]) + 0.25 * squares(rows2[:, 48:])
    square = after(jnp.full((8, 128), square, F32), g1[1])
    square = square + swap(square, 1)
    square = square + swap(square, 2)
    square = square + swap_dp(square, 1)
    grad_norm = jnp.sqrt(square[0, 0])
    clip = CLIP_NORM / jnp.maximum(grad_norm, CLIP_NORM)

    def rows_of(kept, got):
        return jnp.where(row == 0, jnp.stack([kept, got]), jnp.stack([got, kept]))

    block_out = rows_of(hidden2[:size], out_got)
    input_grad = rows_of(igrad[:size], igrad_got.astype(F32))

    def like(*arrays):
        return [(a.shape, F32) for a in arrays]

    heads = [out_head.T, head_m.T, head_v.T]
    triangle = ((2, 3 * D // 4, D // 2), F32)
    outs = call(
        momentum_kernel, "momentum",
        [
            places, clip.reshape(1), *g1, *g2, mom_qkv, mom_out, mom_up, mom_down,
            embedding, embed_m, embed_v, *heads, norm_gains, gains_m, gains_v,
        ],
        [triangle, triangle]
        + like(mom_qkv, mom_out, mom_up, mom_down, embed_m, embed_v, embedding)
        + like(*heads, gains_m, gains_v, norm_gains),
        [pltpu.VMEM((8 * rows1 + 3 * PAIR, D), F32), pltpu.VMEM((64, D), F32), pltpu.VMEM((3 * D // 2, D // 2), F32)],
        scalars=2, plain=range(12, 21), far=range(2, 15), micros=7,
    )
    near, far = outs[:2]
    moms = outs[2:6]
    mom_qkv_new, mom_out_new, mom_up_new, mom_down_new = moms
    embed_new, head_new, gains_new = outs[6:9], [h.T for h in outs[9:12]], outs[12:15]
    far = swap(far, 1)
    half = (near[0] + far[0]) + swap(near[1] + far[1], 2)
    poly = [((16 + 3 * D // 4, D // 2), BF16)] * 2
    near, far = call(
        schulz_kernel, "schulz", [core.reshape(1).astype(jnp.int32), half, swap(half, 1)], poly,
        [pltpu.VMEM((3 * D // 2, D // 2), F32), pltpu.VMEM((D, D), F32), pltpu.VMEM((D, D), F32),
         pltpu.VMEM((2, 16 + 3 * D // 4, D // 2), BF16)],
        scalars=1, micros=10,
    )
    near_x, near_y = swap(near, 2), swap_dp(near, 1)
    nears = [near, near_x, near_y, swap_both(near, 2, 1)]
    fars = [far] + [swap(values, 1) for values in nears[1:]]
    qkv_new, out_new, up_new, down_new = call(
        muon_kernel, "muon",
        [places, *moms, *nears, *fars, w_qkv, w_out, w_up, w_down],
        like(w_qkv, w_out, w_up, w_down),
        [pltpu.VMEM((4, 2, 16 + 3 * D // 4, D // 2), BF16)],
        scalars=1, plain=(1, 2, 3, 4), far=range(4), micros=5,
    )
    return (
        block_out, input_grad, grad_norm,
        mom_qkv_new, qkv_new, mom_out_new, out_new, mom_up_new, up_new, mom_down_new, down_new,
        *embed_new, *head_new, *gains_new,
    )


def solution(mesh):
    columns, rows = P(None, "tensor"), P("tensor", None)
    matrices = (columns, rows, columns, rows)
    in_specs = (
        (P("dp", "tensor"), P("dp", "tensor"), P("dp", None), P("dp", None), P(), P(), P())
        + matrices + matrices + (P(),) * 6
    )
    out_specs = (
        (P("dp", "tensor", None), P("dp", "tensor", None), P())
        + (columns, columns, rows, rows, columns, columns, rows, rows) + (P(),) * 9
    )
    return jax.shard_map(on_device, mesh=mesh, in_specs=in_specs, out_specs=out_specs, check_vma=False)
```

```python
import math

import jax
import jax.numpy as jnp
import numpy as np
from jax import lax
from jax.experimental import pallas as pl
from jax.experimental.pallas import tpu as pltpu
from jax.sharding import PartitionSpec as P

D = 512
HEAD_DIM = 64
PAIR = 2 * HEAD_DIM
FF = 2048
NS_STEPS = 5
STEP = 10
CHUNK = 256
VOCAB_PAD = 32
SPAN_PAD = 16
GROUP, ROW, CORE, SIDE = 16, 17, 18, 19

HIGHEST = lax.Precision.HIGHEST
F32 = jnp.float32
BF16 = jnp.bfloat16
NORM_EPS = 1e-05
MASK_FILL = 1e30
MUON_MOMENTUM = 0.5
MUON_RATE = 0.3
MUON_DECAY = 0.1
SCHULZ_LINEAR = 3.4445
SCHULZ_SQUARE = -4.775
SCHULZ_CUBE = 2.0315
ADAM_BETA_ONE = 0.9
ADAM_BETA_TWO = 0.95
ADAM_EPS = 1e-08
EMBED_RATE = 0.3
HEAD_RATE = 0.02
GAIN_RATE = 0.6
WEIGHT_DECAY = 0.1
CLIP_NORM = 1.0


def nn(left, right, precision=None):
    return lax.dot_general(
        left, right, (((1,), (0,)), ((), ())), preferred_element_type=F32, precision=precision
    )


def nt(left, right, precision=None):
    return lax.dot_general(
        left, right, (((1,), (1,)), ((), ())), preferred_element_type=F32, precision=precision
    )


def tn(left, right, precision=None):
    return lax.dot_general(
        left, right, (((0,), (0,)), ((), ())), preferred_element_type=F32, precision=precision
    )


def halves(values):
    high = values.astype(BF16)
    return high, (values - high.astype(F32)).astype(BF16)


def position_table(length, width):
    half = width // 2
    rates = np.exp(-math.log(10000.0) * np.arange(half) / half)
    angles = np.arange(length)[:, None] * rates[None, :]
    return np.concatenate([np.sin(angles), np.cos(angles)], axis=1).astype(np.float32)


def normed_parts(values):
    centered = values - jnp.mean(values, axis=-1, keepdims=True)
    inv_std = lax.rsqrt(jnp.mean(centered * centered, axis=-1, keepdims=True) + NORM_EPS)
    return centered * inv_std, inv_std


def norm_back(grad_out, source, gain):
    normed, inv_std = normed_parts(source)
    scaled = grad_out * gain
    grad_in = inv_std * (
        scaled
        - jnp.mean(scaled, axis=-1, keepdims=True)
        - normed * jnp.mean(scaled * normed, axis=-1, keepdims=True)
    )
    return grad_in, jnp.sum(grad_out * normed, axis=0, keepdims=True)


def embed_kernel(where_ref, tok_ref, seg_ref, table_ref, emb_ref, gains_ref, h0_ref, a1_ref, aug_ref, rows_ref):
    vocab, width = emb_ref.shape
    half = width // 2
    blocks, size = tok_ref.shape
    spans = SPAN_PAD // 4
    rows_ref[...] = jnp.zeros_like(rows_ref)
    rows_ref[0:vocab, 0:width] = emb_ref[...]
    for span in range(spans):
        at_time = table_ref[pl.ds(where_ref[8 + span], 1), :]
        at_start = table_ref[pl.ds(where_ref[12 + span], 1), :]
        row = VOCAB_PAD + span
        rows_ref[row : row + 1, 0:width] = at_time
        rows_ref[row : row + 1, width : width + half] = at_start[:, half:]
        rows_ref[row : row + 1, width + half :] = at_start[:, :half]
    rows = rows_ref[...]
    high = rows.astype(BF16)
    rest = rows - high.astype(F32)
    middle = rest.astype(BF16)
    low = (rest - middle.astype(F32)).astype(BF16)
    stacked = jnp.concatenate([high, middle, low], axis=0)
    gain = gains_ref[0:1, :]
    for block in range(blocks):
        tok = tok_ref[block : block + 1, :]
        seg = seg_ref[pl.ds(where_ref[block], 1), :]
        hot_tok = (lax.broadcasted_iota(jnp.int32, (VOCAB_PAD, size), 0) == tok).astype(F32)
        hot_seg = (lax.broadcasted_iota(jnp.int32, (SPAN_PAD, size), 0) == seg).astype(F32)
        hot = jnp.concatenate([hot_tok, hot_seg], axis=0).astype(BF16)
        picked = tn(jnp.concatenate([hot, hot, hot], axis=0), stacked)
        table = table_ref[pl.ds(pl.multiple_of(where_ref[4 + block] * size, size), size), :]
        sin_p, cos_p = table[:, :half], table[:, half:]
        cos_s, sin_s = picked[:, width : width + half], picked[:, width + half :]
        place = jnp.concatenate([sin_p * cos_s - cos_p * sin_s, cos_p * cos_s + sin_p * sin_s], axis=1)
        hidden = picked[:, :width] + place
        if block * size < h0_ref.shape[0]:
            h0_ref[block * size : (block + 1) * size, :] = hidden
        a1_ref[block * size : (block + 1) * size, :] = (normed_parts(hidden)[0] * gain).astype(BF16)
        wide = (lax.broadcasted_iota(jnp.int32, (PAIR, size), 0) == seg).astype(F32)
        aug_ref[block * size : (block + 1) * size, :] = jnp.transpose(wide).astype(BF16)


def query_side(aug, own):
    return ((aug[:own].astype(F32) - 1.0) * MASK_FILL).astype(BF16)


def half_mask(values, head):
    lanes = lax.broadcasted_iota(jnp.int32, values.shape, 1)
    keep = (lanes >= head * HEAD_DIM) & (lanes < (head + 1) * HEAD_DIM)
    return jnp.where(keep, values.astype(F32), 0.0).astype(BF16)


def query_side(aug, own):
    return ((aug[:own].astype(F32) - 1.0) * MASK_FILL).astype(BF16)


def half_mask(values, head):
    lanes = lax.broadcasted_iota(jnp.int32, values.shape, 1)
    keep = (lanes >= head * HEAD_DIM) & (lanes < (head + 1) * HEAD_DIM)
    return jnp.where(keep, values.astype(F32), 0.0).astype(BF16)


def heads_apart(rows, back):
    count = rows.shape[0] // HEAD_DIM
    heads = count // 3
    if back:
        index = [j * heads + h for h in range(heads) for j in range(3)]
    else:
        index = [h * 3 + j for j in range(3) for h in range(heads)]
    return jnp.concatenate([rows[i * HEAD_DIM : (i + 1) * HEAD_DIM] for i in index], axis=0)


def attention_weights_kernel(wq_ref, wo_ref, out_ref):
    wide = wq_ref.shape[1]
    out_ref[0:wide, :] = heads_apart(jnp.transpose(wq_ref[...]), False).astype(BF16)
    out_ref[wide:, :] = wo_ref[...].astype(BF16)


def ffn_weights_kernel(wu_ref, wd_ref, out_ref):
    units = wu_ref.shape[1]
    out_ref[0:units, :] = jnp.transpose(wu_ref[...]).astype(BF16)
    out_ref[units:, :] = wd_ref[...].astype(BF16)


def attend_kernel(a1_ref, aug_ref, w0, w1, qkv_ref, ctx_ref, weights_ref, inverse_ref):
    own = ctx_ref.shape[1]
    scale = HEAD_DIM**-0.5
    aug = aug_ref[...]
    aug_q = query_side(aug, own)
    inverse_ref[...] = jnp.zeros_like(inverse_ref)
    for shard, weight in enumerate((w0, w1)):
        qkv = nt(a1_ref[...], weight[0 : 3 * PAIR, :]).astype(BF16)
        qkv_ref[shard] = qkv
        keys = jnp.concatenate([qkv[:, PAIR : 2 * PAIR], aug], axis=1)
        value = qkv[:, 2 * PAIR :]
        query = qkv[:own, :PAIR].astype(F32) * scale
        for head in range(2):
            q_side = jnp.concatenate([half_mask(query, head), aug_q], axis=1)
            scores = nt(keys, q_side)
            top = jnp.max(scores, axis=0, keepdims=True)
            raised = jnp.exp(scores - top)
            inverse = 1.0 / jnp.sum(raised, axis=0, keepdims=True)
            weights = raised.astype(BF16)
            weights_ref[2 * shard + head] = weights
            out = tn(value, weights)
            at = shard * PAIR + head * HEAD_DIM
            ctx_ref[at : at + HEAD_DIM, :] = out[head * HEAD_DIM : (head + 1) * HEAD_DIM] * inverse
            inverse_ref[2 * shard + head : 2 * shard + head + 1, :] = inverse


def low_bits(piece, mine):
    return (piece ^ mine) & 1, lax.shift_right_logical(piece ^ mine, 1) & 1


def gelu_parts(upper):
    size = jnp.abs(upper)
    pdf = jnp.exp(-0.5 * upper * upper) * (1.0 / math.sqrt(2.0 * math.pi))
    turn = 1.0 / (1.0 + 0.2316419 * size)
    series = turn * (
        0.319381530
        + turn * (-0.356563782 + turn * (1.781477937 + turn * (-1.821255978 + turn * 1.330274429)))
    )
    tail = pdf * series
    cdf = jnp.where(upper < 0.0, tail, 1.0 - tail)
    return (upper * cdf).astype(BF16), (cdf + upper * pdf).astype(BF16)


def up_chunks(a2_ref, packs, act_ref, slope_ref, acc_ref, first):
    units = packs[0].shape[0] // 2
    for at, pack in enumerate(packs):
        for part in range(units // CHUNK):
            chunk = first + at * (units // CHUNK) + part
            act, slope = gelu_parts(nt(a2_ref[...], pack[part * CHUNK : (part + 1) * CHUNK, :]))
            act_ref[chunk] = act
            slope_ref[chunk] = slope
            acc_ref[...] += nn(act, pack[units + part * CHUNK : units + (part + 1) * CHUNK, :])


def ffn_up_kernel(
    ctx_a_ref, ctx_b_ref, h0_ref, gains_ref, wa0, wa1, wa2, wa3, wb0, wb1,
    h1_ref, acc_ref, a2_ref, act_ref, slope_ref,
):
    hidden1 = h0_ref[...]
    for ctx_ref, first, second in ((ctx_a_ref, wa0, wa1), (ctx_b_ref, wa2, wa3)):
        weight = jnp.concatenate([first[3 * PAIR :, :], second[3 * PAIR :, :]], axis=0)
        hidden1 = hidden1 + tn(ctx_ref[...].astype(BF16), weight)
    h1_ref[...] = hidden1
    acc_ref[...] = hidden1
    a2_ref[...] = (normed_parts(hidden1)[0] * gains_ref[1:2, :]).astype(BF16)
    up_chunks(a2_ref, (wb0, wb1), act_ref, slope_ref, acc_ref, 0)


def back_chunk(d_ffn, act, slope, up, down, a2_ref, acc_ref):
    d_up = (nt(d_ffn, down) * slope.astype(F32)).astype(BF16)
    acc_ref[...] += nn(d_up, up)
    return tn(d_up, a2_ref[...]), tn(act, d_ffn)


def chunk_rows(pack, part):
    units = pack.shape[0] // 2
    at = part * CHUNK
    return pack[at : at + CHUNK, :], pack[units + at : units + at + CHUNK, :]


def ffn_kernel(
    where_ref, part_ref, a2_ref, head_ref, gains_ref, tgt_ref, act_a_ref, slope_a_ref, wb0, wb1, wb2, wb3,
    out_ref, dh2_ref, dffn_ref, acc_ref, act_b_ref, slope_b_ref, keep_ref, send_ref, small_ref,
    act_ref, slope_ref, pad_ref,
):
    vocab = head_ref.shape[0]
    width = out_ref.shape[1]
    mine = where_ref[GROUP]
    pad_ref[...] = jnp.zeros_like(pad_ref)
    pad_ref[0:vocab, :] = head_ref[...]
    acc_ref[...] = part_ref[...]
    up_chunks(a2_ref, (wb2, wb3), act_ref, slope_ref, acc_ref, 0)
    hidden2 = acc_ref[...]
    out_ref[...] = hidden2.astype(BF16)
    normed3, _ = normed_parts(hidden2)
    a3 = normed3 * gains_ref[2:3, :]
    head = pad_ref[...]
    logits = nt(head, a3, HIGHEST)
    classes = lax.broadcasted_iota(jnp.int32, logits.shape, 0)
    logits = jnp.where(classes < vocab, logits, -MASK_FILL)
    raised = jnp.exp(logits - jnp.max(logits, axis=0, keepdims=True))
    targets = jnp.concatenate([tgt_ref[0:1, :], tgt_ref[1:2, :]], axis=1)
    d_logits = raised / jnp.sum(raised, axis=0, keepdims=True) - (classes == targets).astype(F32)
    small_ref[0:VOCAB_PAD, :] = nn(d_logits, a3, HIGHEST)
    d_h2, g_gain2 = norm_back(tn(d_logits, head, HIGHEST), hidden2, gains_ref[2:3, :])
    small_ref[VOCAB_PAD:, :] = jnp.concatenate([g_gain2, jnp.zeros((7, width), F32)], axis=0)
    dh2_ref[...] = d_h2
    d_ffn = d_h2.astype(BF16)
    dffn_ref[...] = d_ffn
    acc_ref[...] = jnp.zeros_like(acc_ref)
    rows = CHUNK // 4
    for shard, pack in enumerate((wb0, wb1, wb2, wb3)):
        target = send_ref if shard % 2 else keep_ref
        chunk = 2 * (shard % 2)
        act, slope = (act_a_ref, slope_a_ref) if shard < 2 else (act_ref, slope_ref)
        up, down = chunk_rows(pack, 0)
        g_up, g_down = back_chunk(d_ffn, act[chunk], slope[chunk], up, down, a2_ref, acc_ref)
        for piece in range(4):
            b0, b1 = low_bits(piece, mine)
            slot = 4 * (shard // 2) + 2 * b0 + b1
            target[slot, 0:rows, :] = g_up[piece * rows : (piece + 1) * rows].astype(BF16)
            target[slot, rows:, :] = g_down[piece * rows : (piece + 1) * rows].astype(BF16)
        if shard >= 2:
            act_b_ref[shard - 2] = act_ref[chunk + 1]
            slope_b_ref[shard - 2] = slope_ref[chunk + 1]


def ffn_end_kernel(
    where_ref, ctx_a_ref, ctx_b_ref, h1_ref, dh2_ref, dffn_ref, part_ref, a2_ref, gains_ref,
    act_a_ref, slope_a_ref, act_b_ref, slope_b_ref, wb0, wb1, wb2, wb3,
    dh1_ref, dattn_ref, keep_ref, send_ref, gain_ref, acc_ref,
):
    mine = where_ref[GROUP]
    d_ffn = dffn_ref[...]
    acc_ref[...] = part_ref[...]
    rows = CHUNK // 4
    for shard, pack in enumerate((wb0, wb1, wb2, wb3)):
        target = send_ref if shard % 2 else keep_ref
        act, slope = (act_a_ref[2 * shard + 1], slope_a_ref[2 * shard + 1]) if shard < 2 else (
            act_b_ref[shard - 2], slope_b_ref[shard - 2]
        )
        up, down = chunk_rows(pack, 1)
        g_up, g_down = back_chunk(d_ffn, act, slope, up, down, a2_ref, acc_ref)
        for piece in range(4):
            b0, b1 = low_bits(piece, mine)
            slot = 4 * b0 + 2 * (shard // 2) + b1
            target[slot, 0:rows, :] = g_up[piece * rows : (piece + 1) * rows].astype(BF16)
            target[slot, rows : 2 * rows, :] = g_down[piece * rows : (piece + 1) * rows].astype(BF16)
    d_h1_part, g_gain1 = norm_back(acc_ref[...], h1_ref[...], gains_ref[1:2, :])
    d_h1 = dh2_ref[...] + d_h1_part
    dh1_ref[...] = d_h1
    d_attn = d_h1.astype(BF16)
    dattn_ref[...] = d_attn
    gain_ref[...] = jnp.broadcast_to(g_gain1, gain_ref.shape)
    out_rows = ctx_a_ref.shape[0] // 2
    for across, ctx_ref in enumerate((ctx_a_ref, ctx_b_ref)):
        g_out = nn(ctx_ref[...].astype(BF16), d_attn)
        for core in range(2):
            target = send_ref if core else keep_ref
            for piece in range(4):
                b0, b1 = low_bits(piece, mine)
                at = core * out_rows + piece * (out_rows // 4)
                target[4 * b0 + 2 * across + b1, 2 * rows :, :] = g_out[at : at + out_rows // 4].astype(BF16)


def attend_back_kernel(qkv_ref, weights_ref, ctx_ref, inverse_ref, dattn_ref, w0, w1, dq_ref, near_ref, far_ref):
    own = ctx_ref.shape[1]
    scale = HEAD_DIM**-0.5
    d_attn = dattn_ref[...]
    columns = jnp.transpose(inverse_ref[...])
    for shard, weight_ref in enumerate((w0, w1)):
        weight = weight_ref[3 * PAIR :, :]
        d_ctx = nt(d_attn, weight).astype(BF16).astype(F32)
        d_ctx_t = nt(weight, d_attn).astype(BF16).astype(F32)
        inner = d_ctx_t * ctx_ref[shard * PAIR : (shard + 1) * PAIR, :]
        key = qkv_ref[shard, :, PAIR : 2 * PAIR]
        value = qkv_ref[shard, :, 2 * PAIR :]
        query = qkv_ref[shard, 0:own, 0:PAIR].astype(F32) * scale
        dq_parts = []
        d_key = None
        d_value = None
        for head in range(2):
            mine = slice(head * HEAD_DIM, (head + 1) * HEAD_DIM)
            at = 2 * shard + head
            q_head = half_mask(query, head)
            d_ctx_head = half_mask(d_ctx * columns[:, at : at + 1], head)
            delta = jnp.sum(inner[mine], axis=0, keepdims=True) * inverse_ref[at : at + 1, :]
            weights = weights_ref[at]
            d_scores = (weights.astype(F32) * (nt(value, d_ctx_head) - delta)).astype(BF16)
            d_value_part = nn(weights, d_ctx_head)
            d_key_part = nn(d_scores, q_head)
            dq_parts.append(tn(key, d_scores)[mine])
            d_key = d_key_part if d_key is None else d_key + d_key_part
            d_value = d_value_part if d_value is None else d_value + d_value_part
        dq_ref[shard] = jnp.transpose(jnp.concatenate(dq_parts, axis=0) * scale).astype(BF16)
        near_ref[shard, :, 0:PAIR] = d_key[:own].astype(BF16)
        near_ref[shard, :, PAIR:] = d_value[:own].astype(BF16)
        far_ref[shard ^ 1, :, 0:PAIR] = d_key[own:].astype(BF16)
        far_ref[shard ^ 1, :, PAIR:] = d_value[own:].astype(BF16)


def qkv_grads(where_ref, dq_ref, near_ref, far_ref, a1, weights, keep_ref, send_ref, total):
    for shard, weight in enumerate(weights):
        d_kv = (near_ref[shard].astype(F32) + far_ref[shard].astype(F32)).astype(BF16)
        d_qkv = jnp.concatenate([dq_ref[shard], d_kv], axis=1)
        grad = tn(d_qkv, a1)
        target = send_ref if shard else keep_ref
        rows = grad.shape[0] // 8
        for piece in range(8):
            b0, b1 = low_bits(piece, where_ref[GROUP])
            target[4 * b0 + 2 * b1 + piece // 4] = grad[piece * rows : (piece + 1) * rows].astype(BF16)
        part = nn(d_qkv, weight[0 : 3 * PAIR, :])
        total = part if total is None else total + part
    return total


def input_far_kernel(where_ref, dq_ref, near_ref, far_ref, a1_ref, w0, w1, total_ref, keep_ref, send_ref):
    own = total_ref.shape[0]
    total_ref[...] = qkv_grads(where_ref, dq_ref, near_ref, far_ref, a1_ref[0:own, :], (w0, w1), keep_ref, send_ref, None)


def input_kernel(
    where_ref, dq_ref, near_ref, far_ref, a1_ref, w0, w1, total_ref, h0_ref, dh1_ref, gains_ref, tok_ref, part_ref, gain1_ref,
    igrad_ref, keep_ref, send_ref, small_ref, rows_ref,
):
    own, width = h0_ref.shape
    vocab = 27
    d_a1 = qkv_grads(
        where_ref, dq_ref, near_ref, far_ref, a1_ref[0:own, :], (w0, w1), keep_ref, send_ref, total_ref[...]
    )
    d_h0_part, g_gain0 = norm_back(d_a1, h0_ref[...], gains_ref[0:1, :])
    d_h0 = dh1_ref[...] + d_h0_part
    igrad_ref[...] = d_h0
    high, low = halves(d_h0)
    tok = jnp.concatenate([tok_ref[0:1, :], tok_ref[1:2, :]], axis=1)
    hot = (lax.broadcasted_iota(jnp.int32, (VOCAB_PAD, own), 0) == tok).astype(F32).astype(BF16)
    rows_ref[...] = jnp.zeros_like(rows_ref)
    rows_ref[0:vocab, :] = part_ref[0:vocab, :]
    rows_ref[vocab : 2 * vocab, :] = (nn(hot, high) + nn(hot, low))[0:vocab]
    rows_ref[2 * vocab : 2 * vocab + 1, :] = g_gain0
    rows_ref[2 * vocab + 1 : 2 * vocab + 2, :] = gain1_ref[0:1, :]
    rows_ref[2 * vocab + 2 : 2 * vocab + 3, :] = part_ref[VOCAB_PAD : VOCAB_PAD + 1, :]
    for piece in range(8):
        b0, b1 = low_bits(piece, where_ref[GROUP])
        small_ref[4 * b0 + 2 * b1 + piece // 4] = rows_ref[piece * 8 : (piece + 1) * 8, :]


def adam_step(weight, grad, first_m, second_m, rate, decay):
    first_new = ADAM_BETA_ONE * first_m + (1.0 - ADAM_BETA_ONE) * grad
    second_new = ADAM_BETA_TWO * second_m + (1.0 - ADAM_BETA_TWO) * grad * grad
    first_hat = first_new / (1.0 - ADAM_BETA_ONE**STEP)
    second_hat = second_new / (1.0 - ADAM_BETA_TWO**STEP)
    weight_new = weight * (1.0 - rate * decay) - rate * first_hat / (jnp.sqrt(second_hat) + ADAM_EPS)
    return first_new, second_new, weight_new


def gram_triangle(store, values, product):
    high, low = halves(values)
    half = store.shape[1]

    def part(side, at):
        return side[at * half : (at + 1) * half, :] if product is nt else side[:, at * half : (at + 1) * half]

    for at, (i, j) in enumerate(((0, 0), (0, 1), (1, 1))):
        store[at * half : (at + 1) * half, :] = (
            product(part(high, i), part(high, j))
            + product(part(high, i), part(low, j))
            + product(part(low, i), part(high, j))
        )


def momentum_kernel(where_ref, square_ref, *refs):
    g1_refs, g2_refs = refs[0:4], refs[4:8]
    (
        mq_ref, mo_ref, mu_ref, md_ref,
        emb_ref, emb_m_ref, emb_v_ref, head_ref, head_m_ref, head_v_ref, gain_ref, gain_m_ref, gain_v_ref,
        near_ref, far_ref, norm_ref, mq_out, mo_out, mu_out, md_out,
        emb_m_out, emb_v_out, emb_out, head_m_out, head_v_out, head_out, gain_m_out, gain_v_out, gain_out,
        all_ref, rows_ref, pack_ref,
    ) = refs[8:]
    dp, across, core, side = where_ref[GROUP], where_ref[ROW], where_ref[CORE], where_ref[SIDE]
    norm = jnp.sqrt(square_ref[...])
    norm_ref[...] = norm
    clip = jnp.max(CLIP_NORM / jnp.maximum(norm, CLIP_NORM))
    units = mu_ref.shape[1]
    out_rows = mo_ref.shape[0]
    wide = mq_ref.shape[1]
    eighth, quarter = units // 8, out_rows // 4

    def place(source, at, rows, to):
        all_ref[pl.ds(pl.multiple_of(to, 8), rows), :] = clip * source[at : at + rows, :].astype(F32)

    for turn in range(4):
        low = turn ^ (dp & 3)
        for high in range(2):
            piece = 4 * high + low
            place(g1_refs[turn], 2 * eighth * high, eighth, piece * eighth)
            place(g1_refs[turn], 2 * eighth * high + eighth, eighth, units + piece * eighth)
            rows = wide // 8
            values = g2_refs[turn][high].astype(F32)
            all_ref[pl.ds(pl.multiple_of(2 * units + out_rows + piece * rows, 8), rows), :] = clip * values[0:rows]
            rows_ref[pl.ds(pl.multiple_of(piece * 8, 8), 8), :] = clip * values[rows:]
        place(g1_refs[turn], 4 * eighth, quarter, 2 * units + low * quarter)
    mu_out[...] = MUON_MOMENTUM * mu_ref[...] + jnp.transpose(all_ref[0:units, :])
    md_out[...] = MUON_MOMENTUM * md_ref[...] + all_ref[units : 2 * units, :]
    mo_out[...] = MUON_MOMENTUM * mo_ref[...] + all_ref[2 * units : 2 * units + out_rows, :]
    mq_out[...] = MUON_MOMENTUM * mq_ref[...] + jnp.transpose(
        heads_apart(all_ref[2 * units + out_rows :, :], True)
    )

    def grams(*pair):
        for index, (out_ref, product) in enumerate(pair):
            gram_triangle(pack_ref, out_ref[...], product)
            half = pack_ref.shape[0] // 2
            slot = index ^ across
            near_ref[slot] = pack_ref[pl.ds(pl.multiple_of(core * half, 8), half), :]
            far_ref[slot] = pack_ref[pl.ds(pl.multiple_of((1 - core) * half, 8), half), :]

    @pl.when(side == 0)
    def _():
        grams((mu_out, nt), (mo_out, tn))

    @pl.when(side == 1)
    def _():
        grams((mq_out, nt), (md_out, tn))

    vocab = emb_ref.shape[0]
    head_m_out[...], head_v_out[...], head_out[...] = adam_step(
        head_ref[...], rows_ref[0:vocab, :], head_m_ref[...], head_v_ref[...], HEAD_RATE, WEIGHT_DECAY
    )
    emb_m_out[...], emb_v_out[...], emb_out[...] = adam_step(
        emb_ref[...], rows_ref[vocab : 2 * vocab, :], emb_m_ref[...], emb_v_ref[...], EMBED_RATE, WEIGHT_DECAY
    )
    gain_m_out[...], gain_v_out[...], gain_out[...] = adam_step(
        gain_ref[...], rows_ref[2 * vocab : 2 * vocab + 3, :], gain_m_ref[...], gain_v_ref[...], GAIN_RATE, 0.0
    )


def rows_kernel(where_ref, out_ref, out_got_ref, grad_ref, grad_got_ref, block_ref, input_ref):
    row = where_ref[ROW]
    size = out_got_ref.shape[0]
    block_ref[row] = out_ref[0:size, :]
    block_ref[1 - row] = out_got_ref[...]
    input_ref[row] = grad_ref[0:size, :]
    input_ref[1 - row] = grad_got_ref[...].astype(F32)


def squares_kernel(quarter_ref, quarter_z_ref, rows_ref, rows_z_ref, out_ref):
    wide = 3 * PAIR // 8
    total = 0.0
    for ref in (quarter_ref, quarter_z_ref):
        values = ref[...].astype(F32)
        total = total + jnp.sum(values * values)
    for ref in (rows_ref, rows_z_ref):
        for at in range(ref.shape[0]):
            values = ref[at].astype(F32)
            total = total + jnp.sum(values[0:wide] * values[0:wide]) + 0.25 * jnp.sum(values[wide:] * values[wide:])
    out_ref[...] = jnp.full(out_ref.shape, total, F32)


def three(left, right):
    left_high, left_low = halves(left)
    right_high, right_low = halves(right)
    return nn(left_high, right_high) + nn(left_high, right_low) + nn(left_low, right_high)


def once(left, right):
    return nn(left.astype(BF16), right.astype(BF16))


def schulz_kernel(where_ref, mine_ref, other_ref, near_ref, far_ref, pack_ref, poly_ref, gram_ref, tri_ref):
    half, block = mine_ref.shape
    size = 2 * block
    core = where_ref[CORE]
    pack_ref[pl.ds(pl.multiple_of(core * half, 8), half), :] = mine_ref[...]
    pack_ref[pl.ds(pl.multiple_of((1 - core) * half, 8), half), :] = other_ref[...]
    gram_ref[0:block, 0:block] = pack_ref[0:block, :]
    corner = pack_ref[block:size, :]
    gram_ref[0:block, block:] = corner
    gram_ref[block:, 0:block] = jnp.transpose(corner)
    gram_ref[block:, block:] = pack_ref[size:, :]
    gram = gram_ref[...]
    rows = lax.broadcasted_iota(jnp.int32, gram.shape, 0)
    columns = lax.broadcasted_iota(jnp.int32, gram.shape, 1)
    diagonal = rows == columns
    trace = jnp.sum(jnp.where(diagonal, gram, 0.0))
    inverse = 1.0 / (jnp.sqrt(jnp.full((1, size), trace, F32)) + 1e-07)
    gram = gram * (inverse * inverse)

    def sweep(gram, poly, times, last=False):
        change = SCHULZ_SQUARE * gram + SCHULZ_CUBE * times(gram, gram)
        if poly is None:
            poly_ref[...] = change * inverse + jnp.where(diagonal, SCHULZ_LINEAR * inverse, 0.0)
        else:
            poly_ref[...] = SCHULZ_LINEAR * poly + times(change, poly)
        if not last:
            moved = SCHULZ_LINEAR * gram + times(change, gram)
            gram_ref[...] = SCHULZ_LINEAR * moved + times(moved, change)

    sweep(gram, None, once)
    sweep(gram_ref[...], poly_ref[...], once)
    sweep(gram_ref[...], poly_ref[...], once)
    for index in range(3, NS_STEPS):
        sweep(gram_ref[...], poly_ref[...], three, index == NS_STEPS - 1)
    poly = poly_ref[...]
    spine = jnp.sum(jnp.where(diagonal, poly, 0.0), axis=0, keepdims=True)
    off = jnp.where(diagonal, 0.0, poly).astype(BF16)
    high = spine.astype(BF16).astype(F32)
    low = spine - high
    rest = jnp.zeros((14, block), F32)
    tops = [
        jnp.concatenate([high[:, at], low[:, at], rest], axis=0).astype(BF16)
        for at in (slice(0, block), slice(block, size))
    ]
    part = half - block
    tri_ref[0, 0:block, :] = off[0:block, 0:block]
    tri_ref[0, block:half, :] = off[0:part, block:]
    tri_ref[0, half:, :] = tops[0]
    tri_ref[1, 0 : block - part, :] = off[part:block, block:]
    tri_ref[1, block - part : half, :] = off[block:, block:]
    tri_ref[1, half:, :] = tops[1]
    near_ref[...] = tri_ref[core]
    far_ref[...] = tri_ref[1 - core]


def muon_kernel(
    where_ref, mq_ref, mo_ref, mu_ref, md_ref, near0, near1, near2, near3, far0, far1, far2, far3,
    wq_ref, wo_ref, wu_ref, wd_ref, wq_out, wo_out, wu_out, wd_out, tri_ref,
):
    across, core, side = where_ref[ROW], where_ref[CORE], where_ref[SIDE]
    held = 2 * side + across
    for at, (near, far) in enumerate(((near0, far0), (near1, far1), (near2, far2), (near3, far3))):
        tri_ref[at, core] = near[...]
        tri_ref[at, 1 - core] = far[...]
    block = near0.shape[1]
    half = near0.shape[0] - 16
    part = half - block

    def ortho(matrix, values, left):
        slot = matrix ^ held
        first = tri_ref[slot, 0]
        second = tri_ref[slot, 1]
        corner = jnp.concatenate([first[block:half], second[0 : block - part]], axis=0)
        upper = jnp.concatenate([first[0:block], corner], axis=1)
        lower = jnp.concatenate([jnp.transpose(corner), second[block - part : half]], axis=1)
        poly = jnp.concatenate([upper, lower], axis=0)
        spines = [tri[half:].astype(F32) for tri in (first, second)]
        spine = jnp.concatenate([s[0:1] + s[1:2] for s in spines], axis=1)
        if left:
            spine = jnp.transpose(jnp.broadcast_to(spine, (8, 2 * block)))[:, 0:1]
            return nn(poly, values.astype(BF16)) + values * spine
        return nn(values.astype(BF16), poly) + values * spine

    def moved(weight, ortho, longest):
        return weight * (1.0 - MUON_RATE * MUON_DECAY) - MUON_RATE * 0.2 * math.sqrt(longest) * ortho

    wu_out[...] = moved(wu_ref[...], ortho(0, mu_ref[...], True), max(D, FF))
    wo_out[...] = moved(wo_ref[...], ortho(1, mo_ref[...], False), D)
    wq_out[...] = moved(wq_ref[...], ortho(2, mq_ref[...], True), 3 * D)
    wd_out[...] = moved(wd_ref[...], ortho(3, md_ref[...], False), max(D, FF))


VMEM = pl.BlockSpec(memory_space=pltpu.VMEM)
SMEM = pl.BlockSpec(memory_space=pltpu.SMEM)
VMEM_LIMIT = 14 * 1024 * 1024


def call(body, name, ins, outs, scratch=(), scalars=0, plain=(), far=(), micros=1):
    shapes = [
        (pltpu.HBM if at in far else pltpu.VMEM)(shape, dtype)
        for at, (shape, dtype) in enumerate(outs)
    ]
    held = [
        value if at < scalars else pltpu.with_memory_space_constraint(value, pltpu.HBM if at in plain else pltpu.VMEM)
        for at, value in enumerate(ins)
    ]
    return pl.pallas_call(
        body,
        name=name,
        out_shape=shapes,
        in_specs=[SMEM] * scalars + [VMEM] * (len(ins) - scalars),
        out_specs=[VMEM] * len(shapes),
        scratch_shapes=list(scratch),
        compiler_params=pltpu.CompilerParams(vmem_limit_bytes=VMEM_LIMIT),
        cost_estimate=pl.CostEstimate(flops=micros * 10**8, bytes_accessed=0, transcendentals=0),
    )(*held)


def swap(values, bit):
    return lax.ppermute(values, "tensor", [(i, i ^ bit) for i in range(4)])


def swap_dp(values, bit):
    return lax.ppermute(values, "dp", [(i, i ^ bit) for i in range(lax.axis_size("dp"))])


def swap_both(values, bit, dp_bit):
    width = lax.axis_size("tensor")
    pairs = [
        (p * width + t, (p ^ dp_bit) * width + (t ^ bit)) for p in range(lax.axis_size("dp")) for t in range(width)
    ]
    return lax.ppermute(values, ("dp", "tensor"), pairs)


def add(left, right):
    return (left.astype(F32) + right.astype(F32)).astype(BF16)


def after(values, done):
    return lax.optimization_barrier((values, done))[0]


def over_rest(piece):
    bit = 8
    while bit < lax.axis_size("dp"):
        piece = add(piece, swap_dp(piece, bit))
        bit *= 2
    return piece


def on_device(
    noised, targets, timesteps, segments, embedding, out_head, norm_gains,
    w_qkv, w_out, w_up, w_down, mom_qkv, mom_out, mom_up, mom_down,
    embed_m, embed_v, head_m, head_v, gains_m, gains_v,
):
    place = lax.axis_index("tensor")
    group = lax.axis_index("dp") & 7
    row = place // 2
    core = place % 2
    size = noised.shape[1]
    length = segments.shape[1]
    own = 2 * size
    order = jnp.stack([place, place ^ 2, place ^ 1, place ^ 3])

    ids = jnp.stack([noised, targets])
    mine = lax.dynamic_index_in_dim(ids, row, 1, keepdims=False)
    send_ids = lax.dynamic_index_in_dim(ids, 1 - row, 1, keepdims=False)
    got = swap(send_ids, 2)
    own_ids = jnp.stack([mine, got], axis=1)
    tok = jnp.concatenate([own_ids[0], swap(own_ids[0], 1)], axis=0)
    seg_row = lax.dynamic_index_in_dim(segments, row, 0, keepdims=False)
    span_ids = jnp.arange(timesteps.shape[1], dtype=jnp.int32)
    starts = jnp.sum((seg_row[None, :] < span_ids[:, None]).astype(jnp.int32), axis=1)
    times = lax.dynamic_index_in_dim(timesteps, row, 0, keepdims=False)
    stand = jnp.stack([group, row, core, group & 1])
    where = jnp.concatenate([row * 4 + order, order, times, starts, stand]).astype(jnp.int32)
    table = jnp.asarray(position_table(max(length, 1000), D))

    unit_rows = w_up.shape[1]
    out_rows = w_out.shape[0]
    (wa_mine,) = call(
        attention_weights_kernel, "attention_weights", [after(w_qkv, send_ids), w_out], [((3 * PAIR + out_rows, D), BF16)], plain=(0, 1)
    )
    wa_across = swap(wa_mine, 2)

    hidden0, a1, aug = call(
        embed_kernel, "embed",
        [where, tok, segments.reshape(-1, size), table, embedding, norm_gains],
        [((own, D), F32), ((length, D), BF16), ((length, PAIR), BF16)],
        [pltpu.VMEM((VOCAB_PAD + SPAN_PAD, 2 * D), F32)],
        scalars=1, plain=(2, 3, 4, 5), micros=4,
    )

    def attend(first, second):
        return call(
            attend_kernel, "attend", [a1, aug, first, second],
            [((2, length, 3 * PAIR), BF16), ((2 * PAIR, own), F32), ((4, length, own), BF16), ((8, own), F32)],
            micros=5,
        )

    (wb_mine,) = call(
        ffn_weights_kernel, "ffn_weights", [after(w_up, a1), w_down], [((2 * unit_rows, D), BF16)], plain=(0, 1)
    )
    wb_across = swap(wb_mine, 2)
    wa = [wa_mine, swap(wa_mine, 1)]
    qkv_a, ctx_a, weights_a, inverse_a = attend(*wa)
    wa_across = after(wa_across, ctx_a)
    wa += [wa_across, swap(wa_across, 1)]
    qkv_b, ctx_b, weights_b, inverse_b = attend(*wa[2:])
    wb = [wb_mine, swap(wb_mine, 1)]
    half_chunks = FF // CHUNK // 2
    hidden1, partial2, a2, act_a, slope_a = call(
        ffn_up_kernel, "ffn_up", [ctx_a, ctx_b, hidden0, norm_gains, *wa, *wb],
        [((own, D), F32), ((own, D), F32), ((own, D), BF16)] + [((half_chunks, own, CHUNK), BF16)] * 2,
        plain=(3,), micros=7,
    )
    wb_across = after(wb_across, a2)
    wb += [wb_across, swap(wb_across, 1)]
    slices = unit_rows // 4
    rows2 = slices + out_rows // 4
    hidden2, d_h2, d_ffn, d_a2, act_b, slope_b, keep_a, send_a, part = call(
        ffn_kernel, "ffn",
        [where, partial2, a2, out_head.T, norm_gains, own_ids[1], act_a, slope_a, *wb],
        [((own, D), BF16), ((own, D), F32), ((own, D), BF16), ((own, D), F32)]
        + [((2, own, CHUNK), BF16)] * 2 + [((8, slices, D), BF16)] * 2 + [((VOCAB_PAD + 8, D), F32)],
        [
            pltpu.VMEM((half_chunks, own, CHUNK), BF16),
            pltpu.VMEM((half_chunks, own, CHUNK), BF16),
            pltpu.VMEM((VOCAB_PAD, D), F32),
        ],
        scalars=1, plain=(3, 4), far=(0,), micros=10,
    )
    got_a = swap(send_a, 1)
    d_h1, d_attn, keep_b, send_b, gain1 = call(
        ffn_end_kernel, "ffn_end",
        [where, ctx_a, ctx_b, hidden1, d_h2, d_ffn, d_a2, a2, norm_gains, act_a, slope_a, act_b, slope_b, *wb],
        [((own, D), F32), ((own, D), BF16), ((8, rows2, D), BF16), ((8, rows2, D), BF16), ((8, D), F32)],
        [pltpu.VMEM((own, D), F32)], scalars=1, plain=(8,), micros=5,
    )
    got_b = swap(send_b, 1)

    def back(qkv, weights, ctx, inverse, d_attn, packs):
        return call(
            attend_back_kernel, "attend_back", [qkv, weights, ctx, inverse, d_attn, *packs],
            [((2, own, PAIR), BF16), ((2, own, 2 * PAIR), BF16), ((2, own, 2 * PAIR), BF16)], micros=5,
        )

    keep_x, send_x = add(keep_a[0:4], got_a[0:4]), add(keep_a[4:8], got_a[4:8])
    got_x = swap(send_x, 2)
    got_b = after(got_b, send_x)
    keep_y, send_y = add(keep_b[0:4], got_b[0:4]), add(keep_b[4:8], got_b[4:8])
    got_y = swap_dp(send_y, 1)
    d_attn = after(d_attn, (send_x, send_y))
    dq_b, near_b, far_b = back(qkv_b, weights_b, ctx_b, inverse_b, d_attn, wa[2:])
    far_b = swap(far_b, 1)
    dq_a, near_a, far_a = back(qkv_a, weights_a, ctx_a, inverse_a, after(d_attn, dq_b), wa[:2])
    far_a = swap(far_a, 1)
    got_x, dq_b = lax.optimization_barrier((got_x, dq_b))
    half_a = add(keep_x, got_x)
    near_b = after(near_b, half_a)
    grads = [((own, D), F32), ((8, 48, D), BF16), ((8, 48, D), BF16)]
    d_a1, keep2_b, send2_b = call(
        input_far_kernel, "input_far", [where, dq_b, near_b, far_b, a1, *wa[2:]], grads, scalars=1, micros=4
    )
    got2_b = swap(send2_b, 1)
    got_y, d_a1 = lax.optimization_barrier((got_y, d_a1))
    half_b = add(keep_y, got_y)
    d_a1 = after(d_a1, (half_a, half_b))
    got_y, got_x = swap_dp(half_a[2:4], 1), swap(half_b[2:4], 2)
    igrad, keep2, send2, small = call(
        input_kernel, "input_grad",
        [where, dq_a, near_a, far_a, a1, *wa[:2], d_a1, hidden0, d_h1, norm_gains, tok, part, gain1],
        grads + [((8, 8, D), F32)], [pltpu.VMEM((64, D), F32)], scalars=1, plain=(10,), micros=5,
    )
    got_x, got_y, send2, small = lax.optimization_barrier((got_x, got_y, send2, small))
    got2 = swap(send2, 1)
    small = small.astype(BF16)
    got_small = swap(small, 1)

    def join(*parts):
        return jnp.concatenate(parts, axis=-2)

    half_a, half_b = add(half_a[0:2], got_y), add(half_b[0:2], got_x)
    send_z = join(half_a[1], half_b[1])
    got_z = swap_dp(send_z, 2)
    near2, far2 = (values.reshape(2, 4, 48, D) for values in (add(keep2, got2), add(keep2_b, after(got2_b, send_z))))
    small = add(small, got_small).reshape(2, 4, 8, D)

    send2_y = join(near2[1, 2:4], small[1, 2:4], far2[1, 2:4])
    got2_y = swap_dp(send2_y, 1)
    got2_x = swap(after(join(far2[:, 0:2], small[:, 0:2]), send2_y), 2)
    quarter = add(join(half_a[0], half_b[0]), after(got_z, got2_x))
    first = add(join(near2[:, 0:2], small[:, 0:2]), got2_x)
    second = add(join(near2[0, 2:4], small[0, 2:4], far2[0, 2:4]), got2_y)
    got2_y = swap_dp(first[1], 1)
    got2_x = swap(join(second[:, 56:104], second[:, 48:56]), 2)
    first, second = add(first[0], got2_y), add(second[:, 0:56], got2_x)
    rows = add(first, swap_dp(second, 2))
    quarter = over_rest(add(quarter, swap_dp(quarter, 4)))
    rows = over_rest(add(rows, swap_dp(rows, 4)))
    quarter_z, quarter_y = swap_dp(quarter, 2), swap_dp(quarter, 1)
    rows_z, rows_y = swap_dp(rows, 2), swap_dp(rows, 1)
    g1 = [quarter, quarter_y, quarter_z, swap_dp(quarter_z, 1)]
    g2 = [rows, rows_y, rows_z, swap_dp(rows_z, 1)]

    out_got = swap(after(hidden2[size:], igrad), 2)
    igrad_got = swap(igrad[size:].astype(BF16), 2)

    block_out, input_grad = call(
        rows_kernel, "rows", [where, hidden2, out_got, igrad, igrad_got],
        [((2, size, D), BF16), ((2, size, D), F32)], scalars=1, plain=(1,), far=(0, 1),
    )
    (square,) = call(squares_kernel, "squares", [after(quarter, (quarter_y, rows_y, block_out)), quarter_z, rows, rows_z], [((8, 128), F32)])
    square = square + swap(square, 1)
    square = (square + swap(square, 2)) + (swap_dp(square, 1) + swap_both(square, 2, 1))


    def like(*arrays):
        return [(a.shape, F32) for a in arrays]

    heads = [out_head.T, head_m.T, head_v.T]
    triangle = ((2, 3 * D // 4, D // 2), F32)
    outs = call(
        momentum_kernel, "momentum",
        [
            where, square, *g1, *g2, mom_qkv, mom_out, mom_up, mom_down,
            embedding, embed_m, embed_v, *heads, norm_gains, gains_m, gains_v,
        ],
        [triangle, triangle, ((8, 128), F32)]
        + like(mom_qkv, mom_out, mom_up, mom_down, embed_m, embed_v, embedding)
        + like(*heads, gains_m, gains_v, norm_gains),
        [pltpu.VMEM((2 * unit_rows + out_rows + 3 * PAIR, D), F32), pltpu.VMEM((64, D), F32), pltpu.VMEM((3 * D // 2, D // 2), F32)],
        scalars=1, plain=range(14, 23), far=range(2, 16), micros=7,
    )
    near, far, norm = outs[:3]
    moms = outs[3:7]
    mom_qkv_new, mom_out_new, mom_up_new, mom_down_new = moms
    embed_new, head_new, gains_new = outs[7:10], [h.T for h in outs[10:13]], outs[13:16]
    grad_norm = norm[0, 0]
    far = swap(far, 1)
    half = (near[0] + far[0]) + swap(near[1] + far[1], 2)
    poly = [((16 + 3 * D // 4, D // 2), BF16)] * 2
    near, far = call(
        schulz_kernel, "schulz", [where, half, swap(half, 1)], poly,
        [pltpu.VMEM((3 * D // 2, D // 2), F32), pltpu.VMEM((D, D), F32), pltpu.VMEM((D, D), F32),
         pltpu.VMEM((2, 16 + 3 * D // 4, D // 2), BF16)],
        scalars=1, micros=10,
    )
    near_x, near_y = swap(near, 2), swap_dp(near, 1)
    nears = [near, near_x, near_y, swap_both(near, 2, 1)]
    fars = [far] + [swap(values, 1) for values in nears[1:]]
    qkv_new, out_new, up_new, down_new = call(
        muon_kernel, "muon",
        [where, *moms, *nears, *fars, w_qkv, w_out, w_up, w_down],
        like(w_qkv, w_out, w_up, w_down),
        [pltpu.VMEM((4, 2, 16 + 3 * D // 4, D // 2), BF16)],
        scalars=1, plain=(1, 2, 3, 4), far=range(4), micros=5,
    )
    return (
        block_out, input_grad, grad_norm,
        mom_qkv_new, qkv_new, mom_out_new, out_new, mom_up_new, up_new, mom_down_new, down_new,
        *embed_new, *head_new, *gains_new,
    )


def solution(mesh):
    columns, rows = P(None, "tensor"), P("tensor", None)
    matrices = (columns, rows, columns, rows)
    in_specs = (
        (P("dp", "tensor"), P("dp", "tensor"), P("dp", None), P("dp", None), P(), P(), P())
        + matrices + matrices + (P(),) * 6
    )
    out_specs = (
        (P("dp", "tensor", None), P("dp", "tensor", None), P())
        + (columns, columns, rows, rows, columns, columns, rows, rows) + (P(),) * 9
    )
    return jax.shard_map(on_device, mesh=mesh, in_specs=in_specs, out_specs=out_specs, check_vma=False)
```

```python
import math

import jax
import jax.numpy as jnp
import numpy as np
from jax import lax
from jax.experimental import pallas as pl
from jax.experimental.pallas import tpu as pltpu
from jax.sharding import PartitionSpec as P

D = 512
HEAD_DIM = 64
PAIR = 2 * HEAD_DIM
FF = 2048
NS_STEPS = 5
STEP = 10
CHUNK = 256
VOCAB_PAD = 32
SPAN_PAD = 16
GROUP, ROW, CORE, SIDE = 16, 17, 18, 19

HIGHEST = lax.Precision.HIGHEST
F32 = jnp.float32
BF16 = jnp.bfloat16
NORM_EPS = 1e-05
MASK_FILL = 1e30
MUON_MOMENTUM = 0.5
MUON_RATE = 0.3
MUON_DECAY = 0.1
SCHULZ_LINEAR = 3.4445
SCHULZ_SQUARE = -4.775
SCHULZ_CUBE = 2.0315
ADAM_BETA_ONE = 0.9
ADAM_BETA_TWO = 0.95
ADAM_EPS = 1e-08
EMBED_RATE = 0.3
HEAD_RATE = 0.02
GAIN_RATE = 0.6
WEIGHT_DECAY = 0.1
CLIP_NORM = 1.0


def nn(left, right, precision=None):
    return lax.dot_general(
        left, right, (((1,), (0,)), ((), ())), preferred_element_type=F32, precision=precision
    )


def nt(left, right, precision=None):
    return lax.dot_general(
        left, right, (((1,), (1,)), ((), ())), preferred_element_type=F32, precision=precision
    )


def tn(left, right, precision=None):
    return lax.dot_general(
        left, right, (((0,), (0,)), ((), ())), preferred_element_type=F32, precision=precision
    )


def halves(values):
    high = values.astype(BF16)
    return high, (values - high.astype(F32)).astype(BF16)


def position_table(length, width):
    half = width // 2
    rates = np.exp(-math.log(10000.0) * np.arange(half) / half)
    angles = np.arange(length)[:, None] * rates[None, :]
    return np.concatenate([np.sin(angles), np.cos(angles)], axis=1).astype(np.float32)


def normed_parts(values):
    centered = values - jnp.mean(values, axis=-1, keepdims=True)
    inv_std = lax.rsqrt(jnp.mean(centered * centered, axis=-1, keepdims=True) + NORM_EPS)
    return centered * inv_std, inv_std


def norm_back(grad_out, source, gain):
    normed, inv_std = normed_parts(source)
    scaled = grad_out * gain
    grad_in = inv_std * (
        scaled
        - jnp.mean(scaled, axis=-1, keepdims=True)
        - normed * jnp.mean(scaled * normed, axis=-1, keepdims=True)
    )
    return grad_in, jnp.sum(grad_out * normed, axis=0, keepdims=True)


def embed_kernel(where_ref, tok_ref, seg_ref, table_ref, emb_ref, gains_ref, h0_ref, a1_ref, aug_ref, rows_ref):
    vocab, width = emb_ref.shape
    half = width // 2
    blocks, size = tok_ref.shape
    spans = SPAN_PAD // 4
    rows_ref[...] = jnp.zeros_like(rows_ref)
    rows_ref[0:vocab, 0:width] = emb_ref[...]
    for span in range(spans):
        at_time = table_ref[pl.ds(where_ref[8 + span], 1), :]
        at_start = table_ref[pl.ds(where_ref[12 + span], 1), :]
        row = VOCAB_PAD + span
        rows_ref[row : row + 1, 0:width] = at_time
        rows_ref[row : row + 1, width : width + half] = at_start[:, half:]
        rows_ref[row : row + 1, width + half :] = at_start[:, :half]
    rows = rows_ref[...]
    high = rows.astype(BF16)
    rest = rows - high.astype(F32)
    middle = rest.astype(BF16)
    low = (rest - middle.astype(F32)).astype(BF16)
    stacked = jnp.concatenate([high, middle, low], axis=0)
    gain = gains_ref[0:1, :]
    for block in range(blocks):
        tok = tok_ref[block : block + 1, :]
        seg = seg_ref[pl.ds(where_ref[block], 1), :]
        hot_tok = (lax.broadcasted_iota(jnp.int32, (VOCAB_PAD, size), 0) == tok).astype(F32)
        hot_seg = (lax.broadcasted_iota(jnp.int32, (SPAN_PAD, size), 0) == seg).astype(F32)
        hot = jnp.concatenate([hot_tok, hot_seg], axis=0).astype(BF16)
        picked = tn(jnp.concatenate([hot, hot, hot], axis=0), stacked)
        table = table_ref[pl.ds(pl.multiple_of(where_ref[4 + block] * size, size), size), :]
        sin_p, cos_p = table[:, :half], table[:, half:]
        cos_s, sin_s = picked[:, width : width + half], picked[:, width + half :]
        place = jnp.concatenate([sin_p * cos_s - cos_p * sin_s, cos_p * cos_s + sin_p * sin_s], axis=1)
        hidden = picked[:, :width] + place
        if block * size < h0_ref.shape[0]:
            h0_ref[block * size : (block + 1) * size, :] = hidden
        a1_ref[block * size : (block + 1) * size, :] = (normed_parts(hidden)[0] * gain).astype(BF16)
        wide = (lax.broadcasted_iota(jnp.int32, (PAIR, size), 0) == seg).astype(F32)
        aug_ref[block * size : (block + 1) * size, :] = jnp.transpose(wide).astype(BF16)


def query_side(aug, own):
    return ((aug[:own].astype(F32) - 1.0) * MASK_FILL).astype(BF16)


def half_mask(values, head):
    lanes = lax.broadcasted_iota(jnp.int32, values.shape, 1)
    keep = (lanes >= head * HEAD_DIM) & (lanes < (head + 1) * HEAD_DIM)
    return jnp.where(keep, values.astype(F32), 0.0).astype(BF16)


def query_side(aug, own):
    return ((aug[:own].astype(F32) - 1.0) * MASK_FILL).astype(BF16)


def half_mask(values, head):
    lanes = lax.broadcasted_iota(jnp.int32, values.shape, 1)
    keep = (lanes >= head * HEAD_DIM) & (lanes < (head + 1) * HEAD_DIM)
    return jnp.where(keep, values.astype(F32), 0.0).astype(BF16)


def heads_apart(rows, back):
    count = rows.shape[0] // HEAD_DIM
    heads = count // 3
    if back:
        index = [j * heads + h for h in range(heads) for j in range(3)]
    else:
        index = [h * 3 + j for j in range(3) for h in range(heads)]
    return jnp.concatenate([rows[i * HEAD_DIM : (i + 1) * HEAD_DIM] for i in index], axis=0)


def attention_weights_kernel(wq_ref, wo_ref, out_ref):
    wide = wq_ref.shape[1]
    out_ref[0:wide, :] = heads_apart(jnp.transpose(wq_ref[...]), False).astype(BF16)
    out_ref[wide:, :] = wo_ref[...].astype(BF16)


def ffn_weights_kernel(wu_ref, wd_ref, out_ref):
    units = wu_ref.shape[1]
    out_ref[0:units, :] = jnp.transpose(wu_ref[...]).astype(BF16)
    out_ref[units:, :] = wd_ref[...].astype(BF16)


def attend_kernel(a1_ref, aug_ref, w0, w1, qkv_ref, ctx_ref, weights_ref, inverse_ref):
    own = ctx_ref.shape[1]
    scale = HEAD_DIM**-0.5
    aug = aug_ref[...]
    aug_q = query_side(aug, own)
    inverse_ref[...] = jnp.zeros_like(inverse_ref)
    for shard, weight in enumerate((w0, w1)):
        qkv = nt(a1_ref[...], weight[0 : 3 * PAIR, :]).astype(BF16)
        qkv_ref[shard] = qkv
        keys = jnp.concatenate([qkv[:, PAIR : 2 * PAIR], aug], axis=1)
        value = qkv[:, 2 * PAIR :]
        query = qkv[:own, :PAIR].astype(F32) * scale
        for head in range(2):
            q_side = jnp.concatenate([half_mask(query, head), aug_q], axis=1)
            scores = nt(keys, q_side)
            top = jnp.max(scores, axis=0, keepdims=True)
            raised = jnp.exp(scores - top)
            inverse = 1.0 / jnp.sum(raised, axis=0, keepdims=True)
            weights = raised.astype(BF16)
            weights_ref[2 * shard + head] = weights
            out = tn(value, weights)
            at = shard * PAIR + head * HEAD_DIM
            ctx_ref[at : at + HEAD_DIM, :] = out[head * HEAD_DIM : (head + 1) * HEAD_DIM] * inverse
            inverse_ref[2 * shard + head : 2 * shard + head + 1, :] = inverse


def low_bits(piece, mine):
    return (piece ^ mine) & 1, lax.shift_right_logical(piece ^ mine, 1) & 1


def gelu_parts(upper):
    size = jnp.abs(upper)
    pdf = jnp.exp(-0.5 * upper * upper) * (1.0 / math.sqrt(2.0 * math.pi))
    turn = 1.0 / (1.0 + 0.2316419 * size)
    series = turn * (
        0.319381530
        + turn * (-0.356563782 + turn * (1.781477937 + turn * (-1.821255978 + turn * 1.330274429)))
    )
    tail = pdf * series
    cdf = jnp.where(upper < 0.0, tail, 1.0 - tail)
    return (upper * cdf).astype(BF16), (cdf + upper * pdf).astype(BF16)


def up_chunks(a2_ref, packs, act_ref, slope_ref, acc_ref, first):
    units = packs[0].shape[0] // 2
    for at, pack in enumerate(packs):
        for part in range(units // CHUNK):
            chunk = first + at * (units // CHUNK) + part
            act, slope = gelu_parts(nt(a2_ref[...], pack[part * CHUNK : (part + 1) * CHUNK, :]))
            act_ref[chunk] = act
            slope_ref[chunk] = slope
            acc_ref[...] += nn(act, pack[units + part * CHUNK : units + (part + 1) * CHUNK, :])


def ffn_up_kernel(
    ctx_a_ref, ctx_b_ref, h0_ref, gains_ref, wa0, wa1, wa2, wa3, wb0, wb1,
    h1_ref, acc_ref, a2_ref, act_ref, slope_ref,
):
    hidden1 = h0_ref[...]
    for ctx_ref, first, second in ((ctx_a_ref, wa0, wa1), (ctx_b_ref, wa2, wa3)):
        weight = jnp.concatenate([first[3 * PAIR :, :], second[3 * PAIR :, :]], axis=0)
        hidden1 = hidden1 + tn(ctx_ref[...].astype(BF16), weight)
    h1_ref[...] = hidden1
    acc_ref[...] = hidden1
    a2_ref[...] = (normed_parts(hidden1)[0] * gains_ref[1:2, :]).astype(BF16)
    up_chunks(a2_ref, (wb0, wb1), act_ref, slope_ref, acc_ref, 0)


def back_chunk(d_ffn, act, slope, up, down, a2_ref, acc_ref):
    d_up = (nt(d_ffn, down) * slope.astype(F32)).astype(BF16)
    acc_ref[...] += nn(d_up, up)
    return tn(d_up, a2_ref[...]), tn(act, d_ffn)


def chunk_rows(pack, part):
    units = pack.shape[0] // 2
    at = part * CHUNK
    return pack[at : at + CHUNK, :], pack[units + at : units + at + CHUNK, :]


def ffn_kernel(
    where_ref, part_ref, a2_ref, head_ref, gains_ref, tgt_ref, act_a_ref, slope_a_ref, wb0, wb1, wb2, wb3,
    out_ref, dh2_ref, dffn_ref, acc_ref, act_b_ref, slope_b_ref, keep_ref, send_ref, small_ref,
    act_ref, slope_ref, pad_ref,
):
    vocab = head_ref.shape[0]
    width = out_ref.shape[1]
    mine = where_ref[GROUP]
    pad_ref[...] = jnp.zeros_like(pad_ref)
    pad_ref[0:vocab, :] = head_ref[...]
    acc_ref[...] = part_ref[...]
    up_chunks(a2_ref, (wb2, wb3), act_ref, slope_ref, acc_ref, 0)
    hidden2 = acc_ref[...]
    out_ref[...] = hidden2.astype(BF16)
    normed3, _ = normed_parts(hidden2)
    a3 = normed3 * gains_ref[2:3, :]
    head = pad_ref[...]
    logits = nt(head, a3, HIGHEST)
    classes = lax.broadcasted_iota(jnp.int32, logits.shape, 0)
    logits = jnp.where(classes < vocab, logits, -MASK_FILL)
    raised = jnp.exp(logits - jnp.max(logits, axis=0, keepdims=True))
    targets = jnp.concatenate([tgt_ref[0:1, :], tgt_ref[1:2, :]], axis=1)
    d_logits = raised / jnp.sum(raised, axis=0, keepdims=True) - (classes == targets).astype(F32)
    small_ref[0:VOCAB_PAD, :] = nn(d_logits, a3, HIGHEST)
    d_h2, g_gain2 = norm_back(tn(d_logits, head, HIGHEST), hidden2, gains_ref[2:3, :])
    small_ref[VOCAB_PAD:, :] = jnp.concatenate([g_gain2, jnp.zeros((7, width), F32)], axis=0)
    dh2_ref[...] = d_h2
    d_ffn = d_h2.astype(BF16)
    dffn_ref[...] = d_ffn
    acc_ref[...] = jnp.zeros_like(acc_ref)
    rows = CHUNK // 4
    for shard, pack in enumerate((wb0, wb1, wb2, wb3)):
        target = send_ref if shard % 2 else keep_ref
        chunk = 2 * (shard % 2)
        act, slope = (act_a_ref, slope_a_ref) if shard < 2 else (act_ref, slope_ref)
        up, down = chunk_rows(pack, 0)
        g_up, g_down = back_chunk(d_ffn, act[chunk], slope[chunk], up, down, a2_ref, acc_ref)
        for piece in range(4):
            b0, b1 = low_bits(piece, mine)
            slot = 4 * (shard // 2) + 2 * b0 + b1
            target[slot, 0:rows, :] = g_up[piece * rows : (piece + 1) * rows].astype(BF16)
            target[slot, rows:, :] = g_down[piece * rows : (piece + 1) * rows].astype(BF16)
        if shard >= 2:
            act_b_ref[shard - 2] = act_ref[chunk + 1]
            slope_b_ref[shard - 2] = slope_ref[chunk + 1]


def ffn_end_kernel(
    where_ref, ctx_a_ref, ctx_b_ref, h1_ref, dh2_ref, dffn_ref, part_ref, a2_ref, gains_ref,
    act_a_ref, slope_a_ref, act_b_ref, slope_b_ref, wb0, wb1, wb2, wb3,
    dh1_ref, dattn_ref, keep_ref, send_ref, gain_ref, acc_ref,
):
    mine = where_ref[GROUP]
    d_ffn = dffn_ref[...]
    acc_ref[...] = part_ref[...]
    rows = CHUNK // 4
    for shard, pack in enumerate((wb0, wb1, wb2, wb3)):
        target = send_ref if shard % 2 else keep_ref
        act, slope = (act_a_ref[2 * shard + 1], slope_a_ref[2 * shard + 1]) if shard < 2 else (
            act_b_ref[shard - 2], slope_b_ref[shard - 2]
        )
        up, down = chunk_rows(pack, 1)
        g_up, g_down = back_chunk(d_ffn, act, slope, up, down, a2_ref, acc_ref)
        for piece in range(4):
            b0, b1 = low_bits(piece, mine)
            slot = 4 * b0 + 2 * (shard // 2) + b1
            target[slot, 0:rows, :] = g_up[piece * rows : (piece + 1) * rows].astype(BF16)
            target[slot, rows : 2 * rows, :] = g_down[piece * rows : (piece + 1) * rows].astype(BF16)
    d_h1_part, g_gain1 = norm_back(acc_ref[...], h1_ref[...], gains_ref[1:2, :])
    d_h1 = dh2_ref[...] + d_h1_part
    dh1_ref[...] = d_h1
    d_attn = d_h1.astype(BF16)
    dattn_ref[...] = d_attn
    gain_ref[...] = jnp.broadcast_to(g_gain1, gain_ref.shape)
    out_rows = ctx_a_ref.shape[0] // 2
    for across, ctx_ref in enumerate((ctx_a_ref, ctx_b_ref)):
        g_out = nn(ctx_ref[...].astype(BF16), d_attn)
        for core in range(2):
            target = send_ref if core else keep_ref
            for piece in range(4):
                b0, b1 = low_bits(piece, mine)
                at = core * out_rows + piece * (out_rows // 4)
                target[4 * b0 + 2 * across + b1, 2 * rows :, :] = g_out[at : at + out_rows // 4].astype(BF16)


def attend_back_kernel(qkv_ref, weights_ref, ctx_ref, inverse_ref, dattn_ref, w0, w1, dq_ref, near_ref, far_ref):
    own = ctx_ref.shape[1]
    scale = HEAD_DIM**-0.5
    d_attn = dattn_ref[...]
    columns = jnp.transpose(inverse_ref[...])
    for shard, weight_ref in enumerate((w0, w1)):
        weight = weight_ref[3 * PAIR :, :]
        d_ctx = nt(d_attn, weight).astype(BF16).astype(F32)
        d_ctx_t = nt(weight, d_attn).astype(BF16).astype(F32)
        inner = d_ctx_t * ctx_ref[shard * PAIR : (shard + 1) * PAIR, :]
        key = qkv_ref[shard, :, PAIR : 2 * PAIR]
        value = qkv_ref[shard, :, 2 * PAIR :]
        query = qkv_ref[shard, 0:own, 0:PAIR].astype(F32) * scale
        dq_parts = []
        d_key = None
        d_value = None
        for head in range(2):
            mine = slice(head * HEAD_DIM, (head + 1) * HEAD_DIM)
            at = 2 * shard + head
            q_head = half_mask(query, head)
            d_ctx_head = half_mask(d_ctx * columns[:, at : at + 1], head)
            delta = jnp.sum(inner[mine], axis=0, keepdims=True) * inverse_ref[at : at + 1, :]
            weights = weights_ref[at]
            d_scores = (weights.astype(F32) * (nt(value, d_ctx_head) - delta)).astype(BF16)
            d_value_part = nn(weights, d_ctx_head)
            d_key_part = nn(d_scores, q_head)
            dq_parts.append(tn(key, d_scores)[mine])
            d_key = d_key_part if d_key is None else d_key + d_key_part
            d_value = d_value_part if d_value is None else d_value + d_value_part
        dq_ref[shard] = jnp.transpose(jnp.concatenate(dq_parts, axis=0) * scale).astype(BF16)
        near_ref[shard, :, 0:PAIR] = d_key[:own].astype(BF16)
        near_ref[shard, :, PAIR:] = d_value[:own].astype(BF16)
        far_ref[shard ^ 1, :, 0:PAIR] = d_key[own:].astype(BF16)
        far_ref[shard ^ 1, :, PAIR:] = d_value[own:].astype(BF16)


def qkv_grads(where_ref, dq_ref, near_ref, far_ref, a1, weights, keep_ref, send_ref, total):
    for shard, weight in enumerate(weights):
        d_kv = (near_ref[shard].astype(F32) + far_ref[shard].astype(F32)).astype(BF16)
        d_qkv = jnp.concatenate([dq_ref[shard], d_kv], axis=1)
        grad = tn(d_qkv, a1)
        target = send_ref if shard else keep_ref
        rows = grad.shape[0] // 8
        for piece in range(8):
            b0, b1 = low_bits(piece, where_ref[GROUP])
            target[4 * b0 + 2 * b1 + piece // 4] = grad[piece * rows : (piece + 1) * rows].astype(BF16)
        part = nn(d_qkv, weight[0 : 3 * PAIR, :])
        total = part if total is None else total + part
    return total


def input_far_kernel(where_ref, dq_ref, near_ref, far_ref, a1_ref, w0, w1, total_ref, keep_ref, send_ref):
    own = total_ref.shape[0]
    total_ref[...] = qkv_grads(where_ref, dq_ref, near_ref, far_ref, a1_ref[0:own, :], (w0, w1), keep_ref, send_ref, None)


def input_kernel(
    where_ref, dq_ref, near_ref, far_ref, a1_ref, w0, w1, total_ref, h0_ref, dh1_ref, gains_ref, tok_ref, part_ref, gain1_ref,
    igrad_ref, keep_ref, send_ref, small_ref, rows_ref,
):
    own, width = h0_ref.shape
    vocab = 27
    d_a1 = qkv_grads(
        where_ref, dq_ref, near_ref, far_ref, a1_ref[0:own, :], (w0, w1), keep_ref, send_ref, total_ref[...]
    )
    d_h0_part, g_gain0 = norm_back(d_a1, h0_ref[...], gains_ref[0:1, :])
    d_h0 = dh1_ref[...] + d_h0_part
    igrad_ref[...] = d_h0
    high, low = halves(d_h0)
    tok = jnp.concatenate([tok_ref[0:1, :], tok_ref[1:2, :]], axis=1)
    hot = (lax.broadcasted_iota(jnp.int32, (VOCAB_PAD, own), 0) == tok).astype(F32).astype(BF16)
    rows_ref[...] = jnp.zeros_like(rows_ref)
    rows_ref[0:vocab, :] = part_ref[0:vocab, :]
    rows_ref[vocab : 2 * vocab, :] = (nn(hot, high) + nn(hot, low))[0:vocab]
    rows_ref[2 * vocab : 2 * vocab + 1, :] = g_gain0
    rows_ref[2 * vocab + 1 : 2 * vocab + 2, :] = gain1_ref[0:1, :]
    rows_ref[2 * vocab + 2 : 2 * vocab + 3, :] = part_ref[VOCAB_PAD : VOCAB_PAD + 1, :]
    for piece in range(8):
        b0, b1 = low_bits(piece, where_ref[GROUP])
        small_ref[4 * b0 + 2 * b1 + piece // 4] = rows_ref[piece * 8 : (piece + 1) * 8, :]


def adam_step(weight, grad, first_m, second_m, rate, decay):
    first_new = ADAM_BETA_ONE * first_m + (1.0 - ADAM_BETA_ONE) * grad
    second_new = ADAM_BETA_TWO * second_m + (1.0 - ADAM_BETA_TWO) * grad * grad
    first_hat = first_new / (1.0 - ADAM_BETA_ONE**STEP)
    second_hat = second_new / (1.0 - ADAM_BETA_TWO**STEP)
    weight_new = weight * (1.0 - rate * decay) - rate * first_hat / (jnp.sqrt(second_hat) + ADAM_EPS)
    return first_new, second_new, weight_new


def gram_triangle(store, values, product):
    high, low = halves(values)
    half = store.shape[1]

    def part(side, at):
        return side[at * half : (at + 1) * half, :] if product is nt else side[:, at * half : (at + 1) * half]

    for at, (i, j) in enumerate(((0, 0), (0, 1), (1, 1))):
        store[at * half : (at + 1) * half, :] = (
            product(part(high, i), part(high, j))
            + product(part(high, i), part(low, j))
            + product(part(low, i), part(high, j))
        )


def sort_rows(quarter_ref, rows_ref, up_ref, down_ref):
    slices = (quarter_ref.shape[0] - 32) // 4
    wide = 3 * PAIR // 8
    for high in range(2):
        at = slice(high * slices, (high + 1) * slices)
        up_ref[at, :] = quarter_ref[2 * high * slices : (2 * high + 1) * slices, :]
        down_ref[at, :] = quarter_ref[(2 * high + 1) * slices : (2 * high + 2) * slices, :]
        values = rows_ref[high].astype(F32)
        down_ref[2 * slices + high * wide : 2 * slices + (high + 1) * wide, :] = values[0:wide].astype(BF16)
    up_ref[2 * slices : 2 * slices + 32, :] = quarter_ref[4 * slices :, :]
    up_ref[2 * slices + 32 : 2 * slices + 2 * wide, :] = jnp.zeros((2 * wide - 32, up_ref.shape[1]), BF16)
    return jnp.concatenate([rows_ref[high].astype(F32)[wide:] for high in range(2)], axis=0).astype(BF16)


def choose_kernel(where_ref, quarter_ref, rows_ref, first_ref, rest_ref, sorted_ref):
    side = where_ref[SIDE]
    main = first_ref.shape[0]
    small = sort_rows(quarter_ref, rows_ref, sorted_ref.at[0], sorted_ref.at[1])
    first_ref[...] = sorted_ref[1 - side]
    rest_ref[0:main, :] = sorted_ref[side]
    rest_ref[main:, :] = small


def put(all_ref, scale, sources, low, base_rows, matrix):
    for high, (ref, at) in enumerate(sources):
        piece = 4 * high + low
        to = pl.ds(pl.multiple_of(matrix + piece * base_rows, 8), base_rows)
        all_ref[to, :] = scale * ref[at : at + base_rows, :].astype(F32)


def gram_kernel(
    where_ref, square_ref, q0_ref, r0_ref, q1_ref, r1_ref, y0_ref, y1_ref, mq_ref, mo_ref, mu_ref, md_ref,
    near_ref, far_ref, all_ref, pack_ref, sorted_ref,
):
    dp, across, core, side = where_ref[GROUP], where_ref[ROW], where_ref[CORE], where_ref[SIDE]
    clip = jnp.max(CLIP_NORM / jnp.maximum(jnp.sqrt(square_ref[...]), CLIP_NORM))
    units, wide = mu_ref.shape[1], mq_ref.shape[1]
    slices = units // 8
    for turn, (quarter, rows) in enumerate(((q0_ref, r0_ref), (q1_ref, r1_ref))):
        sort_rows(quarter, rows, sorted_ref.at[2 * turn], sorted_ref.at[2 * turn + 1])

    def gather(type_index, put_rows):
        for turn, got in enumerate((y0_ref, y1_ref)):
            put_rows(sorted_ref.at[2 * turn + type_index], (2 * turn) ^ (dp & 3))
            put_rows(got, (2 * turn + 1) ^ (dp & 3))

    def grams(*pair):
        for index, (values, product) in enumerate(pair):
            gram_triangle(pack_ref, values, product)
            half = pack_ref.shape[0] // 2
            slot = index ^ across
            near_ref[slot] = pack_ref[pl.ds(pl.multiple_of(core * half, 8), half), :]
            far_ref[slot] = pack_ref[pl.ds(pl.multiple_of((1 - core) * half, 8), half), :]

    @pl.when(side == 0)
    def _():
        def up_out(ref, low):
            put(all_ref, clip, ((ref, 0), (ref, slices)), low, slices, 0)
            all_ref[pl.ds(pl.multiple_of(units + low * 32, 8), 32), :] = clip * ref[
                2 * slices : 2 * slices + 32, :
            ].astype(F32)

        gather(0, up_out)
        up = MUON_MOMENTUM * mu_ref[...] + jnp.transpose(all_ref[0:units, :])
        out = MUON_MOMENTUM * mo_ref[...] + all_ref[units : units + mo_ref.shape[0], :]
        grams((up, nt), (out, tn))

    @pl.when(side == 1)
    def _():
        def down_qkv(ref, low):
            put(all_ref, clip, ((ref, 0), (ref, slices)), low, slices, 0)
            put(all_ref, clip, ((ref, 2 * slices), (ref, 2 * slices + wide // 8)), low, wide // 8, units)

        gather(1, down_qkv)
        qkv = MUON_MOMENTUM * mq_ref[...] + jnp.transpose(heads_apart(all_ref[units : units + wide, :], True))
        down = MUON_MOMENTUM * md_ref[...] + all_ref[0:units, :]
        grams((qkv, nt), (down, tn))


def momentum_kernel(
    where_ref, square_ref, q0_ref, r0_ref, q1_ref, r1_ref, y0_ref, y1_ref, rest0_ref, rest1_ref,
    mq_ref, mo_ref, mu_ref, md_ref,
    emb_ref, emb_m_ref, emb_v_ref, head_ref, head_m_ref, head_v_ref, gain_ref, gain_m_ref, gain_v_ref,
    norm_ref, mq_out, mo_out, mu_out, md_out,
    emb_m_out, emb_v_out, emb_out, head_m_out, head_v_out, head_out, gain_m_out, gain_v_out, gain_out,
    all_ref, rows_ref, sorted_ref, got_ref,
):
    dp, side = where_ref[GROUP], where_ref[SIDE]
    norm = jnp.sqrt(square_ref[...])
    norm_ref[...] = norm
    clip = jnp.max(CLIP_NORM / jnp.maximum(norm, CLIP_NORM))
    units, wide, out_rows = mu_ref.shape[1], mq_ref.shape[1], mo_ref.shape[0]
    slices = units // 8
    main = y0_ref.shape[0]
    qkv_at, out_at = 2 * units + out_rows, 2 * units

    def place(up_ref, down_ref, small, low):
        put(all_ref, clip, ((up_ref, 0), (up_ref, slices)), low, slices, 0)
        put(all_ref, clip, ((down_ref, 0), (down_ref, slices)), low, slices, units)
        put(all_ref, clip, ((down_ref, 2 * slices), (down_ref, 2 * slices + wide // 8)), low, wide // 8, qkv_at)
        all_ref[pl.ds(pl.multiple_of(out_at + low * 32, 8), 32), :] = clip * up_ref[
            2 * slices : 2 * slices + 32, :
        ].astype(F32)
        for high in range(2):
            to = pl.ds(pl.multiple_of((4 * high + low) * 8, 8), 8)
            rows_ref[to, :] = clip * small.astype(F32)[8 * high : 8 * high + 8]

    for turn, (quarter, rows, first, rest) in enumerate(
        ((q0_ref, r0_ref, y0_ref, rest0_ref), (q1_ref, r1_ref, y1_ref, rest1_ref))
    ):
        small = sort_rows(quarter, rows, sorted_ref.at[0], sorted_ref.at[1])
        place(sorted_ref.at[0], sorted_ref.at[1], small, (2 * turn) ^ (dp & 3))
        got_ref[side] = first[...]
        got_ref[1 - side] = rest[0:main, :]
        place(got_ref.at[0], got_ref.at[1], rest[main:, :], (2 * turn + 1) ^ (dp & 3))
    mu_out[...] = MUON_MOMENTUM * mu_ref[...] + jnp.transpose(all_ref[0:units, :])
    md_out[...] = MUON_MOMENTUM * md_ref[...] + all_ref[units : 2 * units, :]
    mo_out[...] = MUON_MOMENTUM * mo_ref[...] + all_ref[out_at:qkv_at, :]
    mq_out[...] = MUON_MOMENTUM * mq_ref[...] + jnp.transpose(heads_apart(all_ref[qkv_at:, :], True))
    vocab = emb_ref.shape[0]
    head_m_out[...], head_v_out[...], head_out[...] = adam_step(
        head_ref[...], rows_ref[0:vocab, :], head_m_ref[...], head_v_ref[...], HEAD_RATE, WEIGHT_DECAY
    )
    emb_m_out[...], emb_v_out[...], emb_out[...] = adam_step(
        emb_ref[...], rows_ref[vocab : 2 * vocab, :], emb_m_ref[...], emb_v_ref[...], EMBED_RATE, WEIGHT_DECAY
    )
    gain_m_out[...], gain_v_out[...], gain_out[...] = adam_step(
        gain_ref[...], rows_ref[2 * vocab : 2 * vocab + 3, :], gain_m_ref[...], gain_v_ref[...], GAIN_RATE, 0.0
    )


def rows_kernel(where_ref, out_ref, out_got_ref, grad_ref, grad_got_ref, block_ref, input_ref):
    row = where_ref[ROW]
    size = out_got_ref.shape[0]
    block_ref[row] = out_ref[0:size, :]
    block_ref[1 - row] = out_got_ref[...]
    input_ref[row] = grad_ref[0:size, :]
    input_ref[1 - row] = grad_got_ref[...].astype(F32)


def squares_kernel(quarter_ref, quarter_z_ref, rows_ref, rows_z_ref, out_ref):
    wide = 3 * PAIR // 8
    total = 0.0
    for ref in (quarter_ref, quarter_z_ref):
        values = ref[...].astype(F32)
        total = total + jnp.sum(values * values)
    for ref in (rows_ref, rows_z_ref):
        for at in range(ref.shape[0]):
            values = ref[at].astype(F32)
            total = total + jnp.sum(values[0:wide] * values[0:wide]) + 0.25 * jnp.sum(values[wide:] * values[wide:])
    out_ref[...] = jnp.full(out_ref.shape, total, F32)


def three(left, right):
    left_high, left_low = halves(left)
    right_high, right_low = halves(right)
    return nn(left_high, right_high) + nn(left_high, right_low) + nn(left_low, right_high)


def once(left, right):
    return nn(left.astype(BF16), right.astype(BF16))


def schulz_kernel(where_ref, mine_ref, other_ref, near_ref, far_ref, pack_ref, poly_ref, gram_ref, tri_ref):
    half, block = mine_ref.shape
    size = 2 * block
    core = where_ref[CORE]
    pack_ref[pl.ds(pl.multiple_of(core * half, 8), half), :] = mine_ref[...]
    pack_ref[pl.ds(pl.multiple_of((1 - core) * half, 8), half), :] = other_ref[...]
    gram_ref[0:block, 0:block] = pack_ref[0:block, :]
    corner = pack_ref[block:size, :]
    gram_ref[0:block, block:] = corner
    gram_ref[block:, 0:block] = jnp.transpose(corner)
    gram_ref[block:, block:] = pack_ref[size:, :]
    gram = gram_ref[...]
    rows = lax.broadcasted_iota(jnp.int32, gram.shape, 0)
    columns = lax.broadcasted_iota(jnp.int32, gram.shape, 1)
    diagonal = rows == columns
    trace = jnp.sum(jnp.where(diagonal, gram, 0.0))
    inverse = 1.0 / (jnp.sqrt(jnp.full((1, size), trace, F32)) + 1e-07)
    gram = gram * (inverse * inverse)

    def sweep(gram, poly, times, last=False):
        change = SCHULZ_SQUARE * gram + SCHULZ_CUBE * times(gram, gram)
        if poly is None:
            poly_ref[...] = change * inverse + jnp.where(diagonal, SCHULZ_LINEAR * inverse, 0.0)
        else:
            poly_ref[...] = SCHULZ_LINEAR * poly + times(change, poly)
        if not last:
            moved = SCHULZ_LINEAR * gram + times(change, gram)
            gram_ref[...] = SCHULZ_LINEAR * moved + times(moved, change)

    sweep(gram, None, once)
    sweep(gram_ref[...], poly_ref[...], once)
    sweep(gram_ref[...], poly_ref[...], once)
    for index in range(3, NS_STEPS):
        sweep(gram_ref[...], poly_ref[...], three, index == NS_STEPS - 1)
    poly = poly_ref[...]
    spine = jnp.sum(jnp.where(diagonal, poly, 0.0), axis=0, keepdims=True)
    off = jnp.where(diagonal, 0.0, poly).astype(BF16)
    high = spine.astype(BF16).astype(F32)
    low = spine - high
    rest = jnp.zeros((14, block), F32)
    tops = [
        jnp.concatenate([high[:, at], low[:, at], rest], axis=0).astype(BF16)
        for at in (slice(0, block), slice(block, size))
    ]
    part = half - block
    tri_ref[0, 0:block, :] = off[0:block, 0:block]
    tri_ref[0, block:half, :] = off[0:part, block:]
    tri_ref[0, half:, :] = tops[0]
    tri_ref[1, 0 : block - part, :] = off[part:block, block:]
    tri_ref[1, block - part : half, :] = off[block:, block:]
    tri_ref[1, half:, :] = tops[1]
    near_ref[...] = tri_ref[core]
    far_ref[...] = tri_ref[1 - core]


def muon_kernel(
    where_ref, mq_ref, mo_ref, mu_ref, md_ref, near0, near1, near2, near3, far0, far1, far2, far3,
    wq_ref, wo_ref, wu_ref, wd_ref, wq_out, wo_out, wu_out, wd_out, tri_ref,
):
    across, core, side = where_ref[ROW], where_ref[CORE], where_ref[SIDE]
    held = 2 * side + across
    for at, (near, far) in enumerate(((near0, far0), (near1, far1), (near2, far2), (near3, far3))):
        tri_ref[at, core] = near[...]
        tri_ref[at, 1 - core] = far[...]
    block = near0.shape[1]
    half = near0.shape[0] - 16
    part = half - block

    def ortho(matrix, values, left):
        slot = matrix ^ held
        first = tri_ref[slot, 0]
        second = tri_ref[slot, 1]
        corner = jnp.concatenate([first[block:half], second[0 : block - part]], axis=0)
        upper = jnp.concatenate([first[0:block], corner], axis=1)
        lower = jnp.concatenate([jnp.transpose(corner), second[block - part : half]], axis=1)
        poly = jnp.concatenate([upper, lower], axis=0)
        spines = [tri[half:].astype(F32) for tri in (first, second)]
        spine = jnp.concatenate([s[0:1] + s[1:2] for s in spines], axis=1)
        if left:
            spine = jnp.transpose(jnp.broadcast_to(spine, (8, 2 * block)))[:, 0:1]
            return nn(poly, values.astype(BF16)) + values * spine
        return nn(values.astype(BF16), poly) + values * spine

    def moved(weight, ortho, longest):
        return weight * (1.0 - MUON_RATE * MUON_DECAY) - MUON_RATE * 0.2 * math.sqrt(longest) * ortho

    wu_out[...] = moved(wu_ref[...], ortho(0, mu_ref[...], True), max(D, FF))
    wo_out[...] = moved(wo_ref[...], ortho(1, mo_ref[...], False), D)
    wq_out[...] = moved(wq_ref[...], ortho(2, mq_ref[...], True), 3 * D)
    wd_out[...] = moved(wd_ref[...], ortho(3, md_ref[...], False), max(D, FF))


VMEM = pl.BlockSpec(memory_space=pltpu.VMEM)
SMEM = pl.BlockSpec(memory_space=pltpu.SMEM)
VMEM_LIMIT = 14 * 1024 * 1024


def call(body, name, ins, outs, scratch=(), scalars=0, plain=(), far=(), micros=1):
    shapes = [
        (pltpu.HBM if at in far else pltpu.VMEM)(shape, dtype)
        for at, (shape, dtype) in enumerate(outs)
    ]
    held = [
        value if at < scalars else pltpu.with_memory_space_constraint(value, pltpu.HBM if at in plain else pltpu.VMEM)
        for at, value in enumerate(ins)
    ]
    return pl.pallas_call(
        body,
        name=name,
        out_shape=shapes,
        in_specs=[SMEM] * scalars + [VMEM] * (len(ins) - scalars),
        out_specs=[VMEM] * len(shapes),
        scratch_shapes=list(scratch),
        compiler_params=pltpu.CompilerParams(vmem_limit_bytes=VMEM_LIMIT),
        cost_estimate=pl.CostEstimate(flops=micros * 10**8, bytes_accessed=0, transcendentals=0),
    )(*held)


def swap(values, bit):
    return lax.ppermute(values, "tensor", [(i, i ^ bit) for i in range(4)])


def swap_dp(values, bit):
    return lax.ppermute(values, "dp", [(i, i ^ bit) for i in range(lax.axis_size("dp"))])


def swap_both(values, bit, dp_bit):
    width = lax.axis_size("tensor")
    pairs = [
        (p * width + t, (p ^ dp_bit) * width + (t ^ bit)) for p in range(lax.axis_size("dp")) for t in range(width)
    ]
    return lax.ppermute(values, ("dp", "tensor"), pairs)


def add(left, right):
    return (left.astype(F32) + right.astype(F32)).astype(BF16)


def after(values, done):
    return lax.optimization_barrier((values, done))[0]


def over_rest(piece):
    bit = 8
    while bit < lax.axis_size("dp"):
        piece = add(piece, swap_dp(piece, bit))
        bit *= 2
    return piece


def on_device(
    noised, targets, timesteps, segments, embedding, out_head, norm_gains,
    w_qkv, w_out, w_up, w_down, mom_qkv, mom_out, mom_up, mom_down,
    embed_m, embed_v, head_m, head_v, gains_m, gains_v,
):
    place = lax.axis_index("tensor")
    group = lax.axis_index("dp") & 7
    row = place // 2
    core = place % 2
    size = noised.shape[1]
    length = segments.shape[1]
    own = 2 * size
    order = jnp.stack([place, place ^ 2, place ^ 1, place ^ 3])

    ids = jnp.stack([noised, targets])
    mine = lax.dynamic_index_in_dim(ids, row, 1, keepdims=False)
    send_ids = lax.dynamic_index_in_dim(ids, 1 - row, 1, keepdims=False)
    got = swap(send_ids, 2)
    own_ids = jnp.stack([mine, got], axis=1)
    tok = jnp.concatenate([own_ids[0], swap(own_ids[0], 1)], axis=0)
    seg_row = lax.dynamic_index_in_dim(segments, row, 0, keepdims=False)
    span_ids = jnp.arange(timesteps.shape[1], dtype=jnp.int32)
    starts = jnp.sum((seg_row[None, :] < span_ids[:, None]).astype(jnp.int32), axis=1)
    times = lax.dynamic_index_in_dim(timesteps, row, 0, keepdims=False)
    stand = jnp.stack([group, row, core, group & 1])
    where = jnp.concatenate([row * 4 + order, order, times, starts, stand]).astype(jnp.int32)
    table = jnp.asarray(position_table(max(length, 1000), D))

    unit_rows = w_up.shape[1]
    out_rows = w_out.shape[0]
    (wa_mine,) = call(
        attention_weights_kernel, "attention_weights", [after(w_qkv, send_ids), w_out], [((3 * PAIR + out_rows, D), BF16)], plain=(0, 1)
    )
    wa_across = swap(wa_mine, 2)

    hidden0, a1, aug = call(
        embed_kernel, "embed",
        [where, tok, segments.reshape(-1, size), table, embedding, norm_gains],
        [((own, D), F32), ((length, D), BF16), ((length, PAIR), BF16)],
        [pltpu.VMEM((VOCAB_PAD + SPAN_PAD, 2 * D), F32)],
        scalars=1, plain=(2, 3, 4, 5), micros=4,
    )

    def attend(first, second):
        return call(
            attend_kernel, "attend", [a1, aug, first, second],
            [((2, length, 3 * PAIR), BF16), ((2 * PAIR, own), F32), ((4, length, own), BF16), ((8, own), F32)],
            micros=5,
        )

    (wb_mine,) = call(
        ffn_weights_kernel, "ffn_weights", [after(w_up, a1), w_down], [((2 * unit_rows, D), BF16)], plain=(0, 1)
    )
    wb_across = swap(wb_mine, 2)
    wa = [wa_mine, swap(wa_mine, 1)]
    qkv_a, ctx_a, weights_a, inverse_a = attend(*wa)
    wa_across = after(wa_across, ctx_a)
    wa += [wa_across, swap(wa_across, 1)]
    qkv_b, ctx_b, weights_b, inverse_b = attend(*wa[2:])
    wb = [wb_mine, swap(wb_mine, 1)]
    half_chunks = FF // CHUNK // 2
    hidden1, partial2, a2, act_a, slope_a = call(
        ffn_up_kernel, "ffn_up", [ctx_a, ctx_b, hidden0, norm_gains, *wa, *wb],
        [((own, D), F32), ((own, D), F32), ((own, D), BF16)] + [((half_chunks, own, CHUNK), BF16)] * 2,
        plain=(3,), micros=7,
    )
    wb_across = after(wb_across, a2)
    wb += [wb_across, swap(wb_across, 1)]
    slices = unit_rows // 4
    rows2 = slices + out_rows // 4
    hidden2, d_h2, d_ffn, d_a2, act_b, slope_b, keep_a, send_a, part = call(
        ffn_kernel, "ffn",
        [where, partial2, a2, out_head.T, norm_gains, own_ids[1], act_a, slope_a, *wb],
        [((own, D), BF16), ((own, D), F32), ((own, D), BF16), ((own, D), F32)]
        + [((2, own, CHUNK), BF16)] * 2 + [((8, slices, D), BF16)] * 2 + [((VOCAB_PAD + 8, D), F32)],
        [
            pltpu.VMEM((half_chunks, own, CHUNK), BF16),
            pltpu.VMEM((half_chunks, own, CHUNK), BF16),
            pltpu.VMEM((VOCAB_PAD, D), F32),
        ],
        scalars=1, plain=(3, 4), far=(0,), micros=10,
    )
    got_a = swap(send_a, 1)
    d_h1, d_attn, keep_b, send_b, gain1 = call(
        ffn_end_kernel, "ffn_end",
        [where, ctx_a, ctx_b, hidden1, d_h2, d_ffn, d_a2, a2, norm_gains, act_a, slope_a, act_b, slope_b, *wb],
        [((own, D), F32), ((own, D), BF16), ((8, rows2, D), BF16), ((8, rows2, D), BF16), ((8, D), F32)],
        [pltpu.VMEM((own, D), F32)], scalars=1, plain=(8,), micros=5,
    )
    got_b = swap(send_b, 1)

    def back(qkv, weights, ctx, inverse, d_attn, packs):
        return call(
            attend_back_kernel, "attend_back", [qkv, weights, ctx, inverse, d_attn, *packs],
            [((2, own, PAIR), BF16), ((2, own, 2 * PAIR), BF16), ((2, own, 2 * PAIR), BF16)], micros=5,
        )

    keep_x, send_x = add(keep_a[0:4], got_a[0:4]), add(keep_a[4:8], got_a[4:8])
    got_x = swap(send_x, 2)
    got_b = after(got_b, send_x)
    keep_y, send_y = add(keep_b[0:4], got_b[0:4]), add(keep_b[4:8], got_b[4:8])
    got_y = swap_dp(send_y, 1)
    d_attn = after(d_attn, (send_x, send_y))
    dq_b, near_b, far_b = back(qkv_b, weights_b, ctx_b, inverse_b, d_attn, wa[2:])
    far_b = swap(far_b, 1)
    dq_a, near_a, far_a = back(qkv_a, weights_a, ctx_a, inverse_a, after(d_attn, dq_b), wa[:2])
    far_a = swap(far_a, 1)
    got_x, dq_b = lax.optimization_barrier((got_x, dq_b))
    half_a = add(keep_x, got_x)
    near_b = after(near_b, half_a)
    grads = [((own, D), F32), ((8, 48, D), BF16), ((8, 48, D), BF16)]
    d_a1, keep2_b, send2_b = call(
        input_far_kernel, "input_far", [where, dq_b, near_b, far_b, a1, *wa[2:]], grads, scalars=1, micros=4
    )
    got2_b = swap(send2_b, 1)
    got_y, d_a1 = lax.optimization_barrier((got_y, d_a1))
    half_b = add(keep_y, got_y)
    d_a1 = after(d_a1, (half_a, half_b))
    got_y, got_x = swap_dp(half_a[2:4], 1), swap(half_b[2:4], 2)
    igrad, keep2, send2, small = call(
        input_kernel, "input_grad",
        [where, dq_a, near_a, far_a, a1, *wa[:2], d_a1, hidden0, d_h1, norm_gains, tok, part, gain1],
        grads + [((8, 8, D), F32)], [pltpu.VMEM((64, D), F32)], scalars=1, plain=(10,), micros=5,
    )
    got_x, got_y, send2, small = lax.optimization_barrier((got_x, got_y, send2, small))
    got2 = swap(send2, 1)
    small = small.astype(BF16)
    got_small = swap(small, 1)

    def join(*parts):
        return jnp.concatenate(parts, axis=-2)

    half_a, half_b = add(half_a[0:2], got_y), add(half_b[0:2], got_x)
    send_z = join(half_a[1], half_b[1])
    got_z = swap_dp(send_z, 2)
    near2, far2 = (values.reshape(2, 4, 48, D) for values in (add(keep2, got2), add(keep2_b, after(got2_b, send_z))))
    small = add(small, got_small).reshape(2, 4, 8, D)

    send2_y = join(near2[1, 2:4], small[1, 2:4], far2[1, 2:4])
    got2_y = swap_dp(send2_y, 1)
    got2_x = swap(after(join(far2[:, 0:2], small[:, 0:2]), send2_y), 2)
    quarter = add(join(half_a[0], half_b[0]), after(got_z, got2_x))
    first = add(join(near2[:, 0:2], small[:, 0:2]), got2_x)
    second = add(join(near2[0, 2:4], small[0, 2:4], far2[0, 2:4]), got2_y)
    got2_y = swap_dp(first[1], 1)
    got2_x = swap(join(second[:, 56:104], second[:, 48:56]), 2)
    first, second = add(first[0], got2_y), add(second[:, 0:56], got2_x)
    rows = add(first, swap_dp(second, 2))
    got_z = swap_dp(quarter, 4)
    igrad_got = swap(after(igrad, got2_x)[size:].astype(BF16), 2)
    out_got = swap(after(hidden2, got2_x)[size:], 2)

    block_out, input_grad = call(
        rows_kernel, "rows", [where, hidden2, out_got, igrad, igrad_got],
        [((2, size, D), BF16), ((2, size, D), F32)], scalars=1, plain=(1,), far=(0, 1),
    )
    quarter = over_rest(add(quarter, after(got_z, block_out)))
    rows = over_rest(add(rows, swap_dp(rows, 4)))
    quarter_z, rows_z = swap_dp(quarter, 2), swap_dp(rows, 2)
    main = 2 * slices // 2 + 3 * PAIR // 4

    def choose(quarter, rows):
        return call(
            choose_kernel, "choose", [where, quarter, rows], [((main, D), BF16), ((main + 16, D), BF16)],
            [pltpu.VMEM((2, main, D), BF16)], scalars=1,
        )

    first0, rest0 = choose(quarter, rows)
    first0 = swap_dp(first0, 1)
    first1, rest1 = choose(quarter_z, rows_z)
    first1 = swap_dp(first1, 1)
    (square,) = call(squares_kernel, "squares", [quarter, quarter_z, rows, rows_z], [((8, 128), F32)])
    square = square + swap(square, 1)
    square = (square + swap(square, 2)) + (swap_dp(square, 1) + swap_both(square, 2, 1))
    rest0, rest1 = (swap_dp(rest, 1) for rest in after((rest0, rest1), square))

    def like(*arrays):
        return [(a.shape, F32) for a in arrays]

    heads = [out_head.T, head_m.T, head_v.T]
    triangle = ((2, 3 * D // 4, D // 2), F32)
    sums = [where, square, quarter, rows, quarter_z, rows_z, first0, first1]
    moments = [mom_qkv, mom_out, mom_up, mom_down]
    sorted_rows = pltpu.VMEM((4, main, D), BF16)
    near, far = call(
        gram_kernel, "gram", sums + moments, [triangle, triangle],
        [pltpu.VMEM((2 * unit_rows, D), F32), pltpu.VMEM((3 * D // 2, D // 2), F32), sorted_rows], scalars=1, micros=3,
    )
    far = swap(far, 1)
    half = after(near[0] + far[0], rest0) + swap(near[1] + far[1], 2)
    poly = [((16 + 3 * D // 4, D // 2), BF16)] * 2
    near, far = call(
        schulz_kernel, "schulz", [where, half, swap(half, 1)], poly,
        [pltpu.VMEM((3 * D // 2, D // 2), F32), pltpu.VMEM((D, D), F32), pltpu.VMEM((D, D), F32),
         pltpu.VMEM((2, 16 + 3 * D // 4, D // 2), BF16)],
        scalars=1, micros=10,
    )
    near, far = after((near, far), rest1)
    outs = call(
        momentum_kernel, "momentum",
        [where, after(square, near)] + sums[2:] + [rest0, rest1] + moments
        + [embedding, embed_m, embed_v, *heads, norm_gains, gains_m, gains_v],
        [((8, 128), F32)] + like(mom_qkv, mom_out, mom_up, mom_down, embed_m, embed_v, embedding)
        + like(*heads, gains_m, gains_v, norm_gains),
        [
            pltpu.VMEM((2 * unit_rows + out_rows + 3 * PAIR, D), F32), pltpu.VMEM((64, D), F32),
            pltpu.VMEM((2, main, D), BF16), pltpu.VMEM((2, main, D), BF16),
        ],
        scalars=1, plain=range(14, 23), far=range(14), micros=5,
    )
    norm = outs[0]
    moms = outs[1:5]
    mom_qkv_new, mom_out_new, mom_up_new, mom_down_new = moms
    embed_new, head_new, gains_new = outs[5:8], [h.T for h in outs[8:11]], outs[11:14]
    grad_norm = norm[0, 0]
    near_x, near_y = swap(near, 2), swap_dp(near, 1)
    nears = [near, *after((near_x, near_y, swap_both(near, 2, 1)), moms)]
    fars = [far] + [swap(values, 1) for values in nears[1:]]
    qkv_new, out_new, up_new, down_new = call(
        muon_kernel, "muon",
        [where, *moms, *nears, *fars, w_qkv, w_out, w_up, w_down],
        like(w_qkv, w_out, w_up, w_down),
        [pltpu.VMEM((4, 2, 16 + 3 * D // 4, D // 2), BF16)],
        scalars=1, plain=(1, 2, 3, 4), far=range(4), micros=5,
    )
    return (
        block_out, input_grad, grad_norm,
        mom_qkv_new, qkv_new, mom_out_new, out_new, mom_up_new, up_new, mom_down_new, down_new,
        *embed_new, *head_new, *gains_new,
    )


def solution(mesh):
    columns, rows = P(None, "tensor"), P("tensor", None)
    matrices = (columns, rows, columns, rows)
    in_specs = (
        (P("dp", "tensor"), P("dp", "tensor"), P("dp", None), P("dp", None), P(), P(), P())
        + matrices + matrices + (P(),) * 6
    )
    out_specs = (
        (P("dp", "tensor", None), P("dp", "tensor", None), P())
        + (columns, columns, rows, rows, columns, columns, rows, rows) + (P(),) * 9
    )
    return jax.shard_map(on_device, mesh=mesh, in_specs=in_specs, out_specs=out_specs, check_vma=False)
```

```python
import math

import jax
import jax.numpy as jnp
import numpy as np
from jax import lax
from jax.experimental import pallas as pl
from jax.experimental.pallas import tpu as pltpu
from jax.sharding import PartitionSpec as P

D = 512
HEAD_DIM = 64
PAIR = 2 * HEAD_DIM
FF = 2048
NS_STEPS = 5
STEP = 10
CHUNK = 256
VOCAB_PAD = 32
SPAN_PAD = 16
GROUP, ROW, CORE, SIDE = 16, 17, 18, 19

HIGHEST = lax.Precision.HIGHEST
F32 = jnp.float32
BF16 = jnp.bfloat16
NORM_EPS = 1e-05
MASK_FILL = 1e30
MUON_MOMENTUM = 0.5
MUON_RATE = 0.3
MUON_DECAY = 0.1
SCHULZ_LINEAR = 3.4445
SCHULZ_SQUARE = -4.775
SCHULZ_CUBE = 2.0315
ADAM_BETA_ONE = 0.9
ADAM_BETA_TWO = 0.95
ADAM_EPS = 1e-08
EMBED_RATE = 0.3
HEAD_RATE = 0.02
GAIN_RATE = 0.6
WEIGHT_DECAY = 0.1
CLIP_NORM = 1.0


def nn(left, right, precision=None):
    return lax.dot_general(
        left, right, (((1,), (0,)), ((), ())), preferred_element_type=F32, precision=precision
    )


def nt(left, right, precision=None):
    return lax.dot_general(
        left, right, (((1,), (1,)), ((), ())), preferred_element_type=F32, precision=precision
    )


def tn(left, right, precision=None):
    return lax.dot_general(
        left, right, (((0,), (0,)), ((), ())), preferred_element_type=F32, precision=precision
    )


def halves(values):
    high = values.astype(BF16)
    return high, (values - high.astype(F32)).astype(BF16)


def position_table(length, width):
    half = width // 2
    rates = np.exp(-math.log(10000.0) * np.arange(half) / half)
    angles = np.arange(length)[:, None] * rates[None, :]
    return np.concatenate([np.sin(angles), np.cos(angles)], axis=1).astype(np.float32)


def normed_parts(values):
    centered = values - jnp.mean(values, axis=-1, keepdims=True)
    inv_std = lax.rsqrt(jnp.mean(centered * centered, axis=-1, keepdims=True) + NORM_EPS)
    return centered * inv_std, inv_std


def norm_back(grad_out, source, gain):
    normed, inv_std = normed_parts(source)
    scaled = grad_out * gain
    grad_in = inv_std * (
        scaled
        - jnp.mean(scaled, axis=-1, keepdims=True)
        - normed * jnp.mean(scaled * normed, axis=-1, keepdims=True)
    )
    return grad_in, jnp.sum(grad_out * normed, axis=0, keepdims=True)


def embed_kernel(where_ref, tok_ref, seg_ref, table_ref, emb_ref, gains_ref, h0_ref, a1_ref, aug_ref, rows_ref):
    vocab, width = emb_ref.shape
    half = width // 2
    blocks, size = tok_ref.shape
    spans = SPAN_PAD // 4
    rows_ref[...] = jnp.zeros_like(rows_ref)
    rows_ref[0:vocab, 0:width] = emb_ref[...]
    for span in range(spans):
        at_time = table_ref[pl.ds(where_ref[8 + span], 1), :]
        at_start = table_ref[pl.ds(where_ref[12 + span], 1), :]
        row = VOCAB_PAD + span
        rows_ref[row : row + 1, 0:width] = at_time
        rows_ref[row : row + 1, width : width + half] = at_start[:, half:]
        rows_ref[row : row + 1, width + half :] = at_start[:, :half]
    rows = rows_ref[...]
    high = rows.astype(BF16)
    rest = rows - high.astype(F32)
    middle = rest.astype(BF16)
    low = (rest - middle.astype(F32)).astype(BF16)
    stacked = jnp.concatenate([high, middle, low], axis=0)
    gain = gains_ref[0:1, :]
    for block in range(blocks):
        tok = tok_ref[block : block + 1, :]
        seg = seg_ref[pl.ds(where_ref[block], 1), :]
        hot_tok = (lax.broadcasted_iota(jnp.int32, (VOCAB_PAD, size), 0) == tok).astype(F32)
        hot_seg = (lax.broadcasted_iota(jnp.int32, (SPAN_PAD, size), 0) == seg).astype(F32)
        hot = jnp.concatenate([hot_tok, hot_seg], axis=0).astype(BF16)
        picked = tn(jnp.concatenate([hot, hot, hot], axis=0), stacked)
        table = table_ref[pl.ds(pl.multiple_of(where_ref[4 + block] * size, size), size), :]
        sin_p, cos_p = table[:, :half], table[:, half:]
        cos_s, sin_s = picked[:, width : width + half], picked[:, width + half :]
        place = jnp.concatenate([sin_p * cos_s - cos_p * sin_s, cos_p * cos_s + sin_p * sin_s], axis=1)
        hidden = picked[:, :width] + place
        if block * size < h0_ref.shape[0]:
            h0_ref[block * size : (block + 1) * size, :] = hidden
        a1_ref[block * size : (block + 1) * size, :] = (normed_parts(hidden)[0] * gain).astype(BF16)
        wide = (lax.broadcasted_iota(jnp.int32, (PAIR, size), 0) == seg).astype(F32)
        aug_ref[block * size : (block + 1) * size, :] = jnp.transpose(wide).astype(BF16)


def query_side(aug, own):
    return ((aug[:own].astype(F32) - 1.0) * MASK_FILL).astype(BF16)


def half_mask(values, head):
    lanes = lax.broadcasted_iota(jnp.int32, values.shape, 1)
    keep = (lanes >= head * HEAD_DIM) & (lanes < (head + 1) * HEAD_DIM)
    return jnp.where(keep, values.astype(F32), 0.0).astype(BF16)


def query_side(aug, own):
    return ((aug[:own].astype(F32) - 1.0) * MASK_FILL).astype(BF16)


def half_mask(values, head):
    lanes = lax.broadcasted_iota(jnp.int32, values.shape, 1)
    keep = (lanes >= head * HEAD_DIM) & (lanes < (head + 1) * HEAD_DIM)
    return jnp.where(keep, values.astype(F32), 0.0).astype(BF16)


def heads_apart(rows, back):
    count = rows.shape[0] // HEAD_DIM
    heads = count // 3
    if back:
        index = [j * heads + h for h in range(heads) for j in range(3)]
    else:
        index = [h * 3 + j for j in range(3) for h in range(heads)]
    return jnp.concatenate([rows[i * HEAD_DIM : (i + 1) * HEAD_DIM] for i in index], axis=0)


def attention_weights_kernel(side_ref, wq_ref, wo_ref, out_ref, part_ref):
    wide = wq_ref.shape[1]
    out_ref[0:wide, :] = heads_apart(jnp.transpose(wq_ref[...]), False).astype(BF16)
    out_ref[wide:, :] = wo_ref[...].astype(BF16)
    half = part_ref.shape[0]
    part_ref[...] = out_ref[pl.ds(pl.multiple_of(side_ref[0] * half, half), half), :]


def join_kernel(where_ref, mine_ref, got_ref, out_ref):
    side = where_ref[SIDE]
    out_ref[side] = mine_ref[...]
    out_ref[1 - side] = got_ref[...]


def ffn_weights_kernel(wu_ref, wd_ref, out_ref):
    units = wu_ref.shape[1]
    out_ref[0:units, :] = jnp.transpose(wu_ref[...]).astype(BF16)
    out_ref[units:, :] = wd_ref[...].astype(BF16)


def attend_kernel(a1_ref, aug_ref, w0, w1, qkv_ref, ctx_ref, weights_ref, inverse_ref):
    own = ctx_ref.shape[1]
    scale = HEAD_DIM**-0.5
    aug = aug_ref[...]
    aug_q = query_side(aug, own)
    inverse_ref[...] = jnp.zeros_like(inverse_ref)
    for shard, weight in enumerate((w0, w1)):
        qkv = nt(a1_ref[...], weight[0 : 3 * PAIR, :]).astype(BF16)
        qkv_ref[shard] = qkv
        keys = jnp.concatenate([qkv[:, PAIR : 2 * PAIR], aug], axis=1)
        value = qkv[:, 2 * PAIR :]
        query = qkv[:own, :PAIR].astype(F32) * scale
        for head in range(2):
            q_side = jnp.concatenate([half_mask(query, head), aug_q], axis=1)
            scores = nt(keys, q_side)
            top = jnp.max(scores, axis=0, keepdims=True)
            raised = jnp.exp(scores - top)
            inverse = 1.0 / jnp.sum(raised, axis=0, keepdims=True)
            weights = raised.astype(BF16)
            weights_ref[2 * shard + head] = weights
            out = tn(value, weights)
            at = shard * PAIR + head * HEAD_DIM
            ctx_ref[at : at + HEAD_DIM, :] = out[head * HEAD_DIM : (head + 1) * HEAD_DIM] * inverse
            inverse_ref[2 * shard + head : 2 * shard + head + 1, :] = inverse


def low_bits(piece, mine):
    return (piece ^ mine) & 1, lax.shift_right_logical(piece ^ mine, 1) & 1


def gelu_parts(upper):
    size = jnp.abs(upper)
    pdf = jnp.exp(-0.5 * upper * upper) * (1.0 / math.sqrt(2.0 * math.pi))
    turn = 1.0 / (1.0 + 0.2316419 * size)
    series = turn * (
        0.319381530
        + turn * (-0.356563782 + turn * (1.781477937 + turn * (-1.821255978 + turn * 1.330274429)))
    )
    tail = pdf * series
    cdf = jnp.where(upper < 0.0, tail, 1.0 - tail)
    return (upper * cdf).astype(BF16), (cdf + upper * pdf).astype(BF16)


def up_chunks(a2_ref, packs, act_ref, slope_ref, acc_ref, first):
    units = packs[0].shape[0] // 2
    for at, pack in enumerate(packs):
        for part in range(units // CHUNK):
            chunk = first + at * (units // CHUNK) + part
            act, slope = gelu_parts(nt(a2_ref[...], pack[part * CHUNK : (part + 1) * CHUNK, :]))
            act_ref[chunk] = act
            slope_ref[chunk] = slope
            acc_ref[...] += nn(act, pack[units + part * CHUNK : units + (part + 1) * CHUNK, :])


def ffn_up_kernel(
    ctx_a_ref, ctx_b_ref, h0_ref, gains_ref, wa0, wa1, wa2, wa3, wb0, wb1,
    h1_ref, acc_ref, a2_ref, act_ref, slope_ref,
):
    hidden1 = h0_ref[...]
    for ctx_ref, first, second in ((ctx_a_ref, wa0, wa1), (ctx_b_ref, wa2, wa3)):
        weight = jnp.concatenate([first[3 * PAIR :, :], second[3 * PAIR :, :]], axis=0)
        hidden1 = hidden1 + tn(ctx_ref[...].astype(BF16), weight)
    h1_ref[...] = hidden1
    acc_ref[...] = hidden1
    a2_ref[...] = (normed_parts(hidden1)[0] * gains_ref[1:2, :]).astype(BF16)
    up_chunks(a2_ref, (wb0, wb1), act_ref, slope_ref, acc_ref, 0)


def back_chunk(d_ffn, act, slope, up, down, a2_ref, acc_ref):
    d_up = (nt(d_ffn, down) * slope.astype(F32)).astype(BF16)
    acc_ref[...] += nn(d_up, up)
    return tn(d_up, a2_ref[...]), tn(act, d_ffn)


def chunk_rows(pack, part):
    units = pack.shape[0] // 2
    at = part * CHUNK
    return pack[at : at + CHUNK, :], pack[units + at : units + at + CHUNK, :]


def ffn_kernel(
    where_ref, part_ref, a2_ref, head_ref, gains_ref, tgt_ref, act_a_ref, slope_a_ref, wb0, wb1, wb2, wb3,
    out_ref, dh2_ref, dffn_ref, acc_ref, act_b_ref, slope_b_ref, keep_ref, send_ref, small_ref,
    act_ref, slope_ref, pad_ref,
):
    vocab = head_ref.shape[0]
    width = out_ref.shape[1]
    mine = where_ref[GROUP]
    pad_ref[...] = jnp.zeros_like(pad_ref)
    pad_ref[0:vocab, :] = head_ref[...]
    acc_ref[...] = part_ref[...]
    up_chunks(a2_ref, (wb2, wb3), act_ref, slope_ref, acc_ref, 0)
    hidden2 = acc_ref[...]
    out_ref[...] = hidden2.astype(BF16)
    normed3, _ = normed_parts(hidden2)
    a3 = normed3 * gains_ref[2:3, :]
    head = pad_ref[...]
    a3_high, a3_low = halves(a3)
    head_high, head_low = halves(head)
    both = nt(jnp.concatenate([head_high, head_low], axis=0), a3_high)
    logits = both[0:VOCAB_PAD] + both[VOCAB_PAD:] + nt(head_high, a3_low)
    classes = lax.broadcasted_iota(jnp.int32, logits.shape, 0)
    logits = jnp.where(classes < vocab, logits, -MASK_FILL)
    raised = jnp.exp(logits - jnp.max(logits, axis=0, keepdims=True))
    targets = jnp.concatenate([tgt_ref[0:1, :], tgt_ref[1:2, :]], axis=1)
    d_logits = raised / jnp.sum(raised, axis=0, keepdims=True) - (classes == targets).astype(F32)
    d_high, d_low = halves(d_logits)
    both = nn(jnp.concatenate([d_high, d_low], axis=0), a3_high)
    small_ref[0:VOCAB_PAD, :] = both[0:VOCAB_PAD] + both[VOCAB_PAD:] + nn(d_high, a3_low)
    d_a3 = tn(
        jnp.concatenate([d_high, d_low, d_high], axis=0), jnp.concatenate([head_high, head_high, head_low], axis=0)
    )
    d_h2, g_gain2 = norm_back(d_a3, hidden2, gains_ref[2:3, :])
    small_ref[VOCAB_PAD:, :] = jnp.concatenate([g_gain2, jnp.zeros((7, width), F32)], axis=0)
    dh2_ref[...] = d_h2
    d_ffn = d_h2.astype(BF16)
    dffn_ref[...] = d_ffn
    acc_ref[...] = jnp.zeros_like(acc_ref)
    rows = CHUNK // 4
    for shard, pack in enumerate((wb0, wb1, wb2, wb3)):
        target = send_ref if shard % 2 else keep_ref
        chunk = 2 * (shard % 2)
        act, slope = (act_a_ref, slope_a_ref) if shard < 2 else (act_ref, slope_ref)
        up, down = chunk_rows(pack, 0)
        g_up, g_down = back_chunk(d_ffn, act[chunk], slope[chunk], up, down, a2_ref, acc_ref)
        for piece in range(4):
            b0, b1 = low_bits(piece, mine)
            slot = 4 * (shard // 2) + 2 * b0 + b1
            target[slot, 0:rows, :] = g_up[piece * rows : (piece + 1) * rows].astype(BF16)
            target[slot, rows:, :] = g_down[piece * rows : (piece + 1) * rows].astype(BF16)
        if shard >= 2:
            act_b_ref[shard - 2] = act_ref[chunk + 1]
            slope_b_ref[shard - 2] = slope_ref[chunk + 1]


def ffn_end_kernel(
    where_ref, ctx_a_ref, ctx_b_ref, h1_ref, dh2_ref, dffn_ref, part_ref, a2_ref, gains_ref,
    act_a_ref, slope_a_ref, act_b_ref, slope_b_ref, wb0, wb1, wb2, wb3,
    dh1_ref, dattn_ref, keep_ref, send_ref, keep_out_ref, send_out_ref, gain_ref, acc_ref,
):
    mine = where_ref[GROUP]
    d_ffn = dffn_ref[...]
    acc_ref[...] = part_ref[...]
    rows = CHUNK // 4
    for shard, pack in enumerate((wb0, wb1, wb2, wb3)):
        target = send_ref if shard % 2 else keep_ref
        act, slope = (act_a_ref[2 * shard + 1], slope_a_ref[2 * shard + 1]) if shard < 2 else (
            act_b_ref[shard - 2], slope_b_ref[shard - 2]
        )
        up, down = chunk_rows(pack, 1)
        g_up, g_down = back_chunk(d_ffn, act, slope, up, down, a2_ref, acc_ref)
        for piece in range(4):
            b0, b1 = low_bits(piece, mine)
            slot = 4 * b0 + 2 * (shard // 2) + b1
            target[slot, 0:rows, :] = g_up[piece * rows : (piece + 1) * rows].astype(BF16)
            target[slot, rows : 2 * rows, :] = g_down[piece * rows : (piece + 1) * rows].astype(BF16)
    d_h1_part, g_gain1 = norm_back(acc_ref[...], h1_ref[...], gains_ref[1:2, :])
    d_h1 = dh2_ref[...] + d_h1_part
    dh1_ref[...] = d_h1
    d_attn = d_h1.astype(BF16)
    dattn_ref[...] = d_attn
    gain_ref[...] = jnp.broadcast_to(g_gain1, gain_ref.shape)
    out_rows = ctx_a_ref.shape[0] // 2
    for across, ctx_ref in enumerate((ctx_a_ref, ctx_b_ref)):
        g_out = nn(ctx_ref[...].astype(BF16), d_attn)
        for core in range(2):
            target = send_out_ref if core else keep_out_ref
            for piece in range(4):
                b0, b1 = low_bits(piece, mine)
                at = core * out_rows + piece * (out_rows // 4)
                target[4 * across + 2 * b0 + b1] = g_out[at : at + out_rows // 4].astype(BF16)


def attend_back_kernel(qkv_ref, weights_ref, ctx_ref, inverse_ref, dattn_ref, w0, w1, dq_ref, near_ref, far_ref):
    own = ctx_ref.shape[1]
    scale = HEAD_DIM**-0.5
    d_attn = dattn_ref[...]
    columns = jnp.transpose(inverse_ref[...])
    for shard, weight_ref in enumerate((w0, w1)):
        weight = weight_ref[3 * PAIR :, :]
        d_ctx = nt(d_attn, weight).astype(BF16).astype(F32)
        d_ctx_t = nt(weight, d_attn).astype(BF16).astype(F32)
        inner = d_ctx_t * ctx_ref[shard * PAIR : (shard + 1) * PAIR, :]
        key = qkv_ref[shard, :, PAIR : 2 * PAIR]
        value = qkv_ref[shard, :, 2 * PAIR :]
        query = qkv_ref[shard, 0:own, 0:PAIR].astype(F32) * scale
        dq_parts = []
        d_key = None
        d_value = None
        for head in range(2):
            mine = slice(head * HEAD_DIM, (head + 1) * HEAD_DIM)
            at = 2 * shard + head
            q_head = half_mask(query, head)
            d_ctx_head = half_mask(d_ctx * columns[:, at : at + 1], head)
            delta = jnp.sum(inner[mine], axis=0, keepdims=True) * inverse_ref[at : at + 1, :]
            weights = weights_ref[at]
            d_scores = (weights.astype(F32) * (nt(value, d_ctx_head) - delta)).astype(BF16)
            d_value_part = nn(weights, d_ctx_head)
            d_key_part = nn(d_scores, q_head)
            dq_parts.append(tn(key, d_scores)[mine])
            d_key = d_key_part if d_key is None else d_key + d_key_part
            d_value = d_value_part if d_value is None else d_value + d_value_part
        dq_ref[shard] = jnp.transpose(jnp.concatenate(dq_parts, axis=0) * scale).astype(BF16)
        near_ref[shard, :, 0:PAIR] = d_key[:own].astype(BF16)
        near_ref[shard, :, PAIR:] = d_value[:own].astype(BF16)
        far_ref[shard ^ 1, :, 0:PAIR] = d_key[own:].astype(BF16)
        far_ref[shard ^ 1, :, PAIR:] = d_value[own:].astype(BF16)


def qkv_grads(where_ref, dq_ref, near_ref, far_ref, a1, weights, keep_ref, send_ref, total):
    for shard, weight in enumerate(weights):
        d_kv = (near_ref[shard].astype(F32) + far_ref[shard].astype(F32)).astype(BF16)
        d_qkv = jnp.concatenate([dq_ref[shard], d_kv], axis=1)
        grad = tn(d_qkv, a1)
        target = send_ref if shard else keep_ref
        rows = grad.shape[0] // 8
        for piece in range(8):
            b0, b1 = low_bits(piece, where_ref[GROUP])
            target[4 * b0 + 2 * b1 + piece // 4] = grad[piece * rows : (piece + 1) * rows].astype(BF16)
        part = nn(d_qkv, weight[0 : 3 * PAIR, :])
        total = part if total is None else total + part
    return total


def input_far_kernel(where_ref, dq_ref, near_ref, far_ref, a1_ref, w0, w1, total_ref, keep_ref, send_ref):
    own = total_ref.shape[0]
    total_ref[...] = qkv_grads(where_ref, dq_ref, near_ref, far_ref, a1_ref[0:own, :], (w0, w1), keep_ref, send_ref, None)


def input_kernel(
    where_ref, dq_ref, near_ref, far_ref, a1_ref, w0, w1, total_ref, h0_ref, dh1_ref, gains_ref, tok_ref, part_ref, gain1_ref,
    igrad_ref, keep_ref, send_ref, small_ref, rows_ref,
):
    own, width = h0_ref.shape
    vocab = 27
    d_a1 = qkv_grads(
        where_ref, dq_ref, near_ref, far_ref, a1_ref[0:own, :], (w0, w1), keep_ref, send_ref, total_ref[...]
    )
    d_h0_part, g_gain0 = norm_back(d_a1, h0_ref[...], gains_ref[0:1, :])
    d_h0 = dh1_ref[...] + d_h0_part
    igrad_ref[...] = d_h0
    high, low = halves(d_h0)
    tok = jnp.concatenate([tok_ref[0:1, :], tok_ref[1:2, :]], axis=1)
    hot = (lax.broadcasted_iota(jnp.int32, (VOCAB_PAD, own), 0) == tok).astype(F32).astype(BF16)
    rows_ref[...] = jnp.zeros_like(rows_ref)
    rows_ref[0:vocab, :] = part_ref[0:vocab, :]
    rows_ref[vocab : 2 * vocab, :] = (nn(hot, high) + nn(hot, low))[0:vocab]
    rows_ref[2 * vocab : 2 * vocab + 1, :] = g_gain0
    rows_ref[2 * vocab + 1 : 2 * vocab + 2, :] = gain1_ref[0:1, :]
    rows_ref[2 * vocab + 2 : 2 * vocab + 3, :] = part_ref[VOCAB_PAD : VOCAB_PAD + 1, :]
    for piece in range(8):
        b0, b1 = low_bits(piece, where_ref[GROUP])
        small_ref[4 * b0 + 2 * b1 + piece // 4] = rows_ref[piece * 8 : (piece + 1) * 8, :]


def adam_step(weight, grad, first_m, second_m, rate, decay):
    first_new = ADAM_BETA_ONE * first_m + (1.0 - ADAM_BETA_ONE) * grad
    second_new = ADAM_BETA_TWO * second_m + (1.0 - ADAM_BETA_TWO) * grad * grad
    first_hat = first_new / (1.0 - ADAM_BETA_ONE**STEP)
    second_hat = second_new / (1.0 - ADAM_BETA_TWO**STEP)
    weight_new = weight * (1.0 - rate * decay) - rate * first_hat / (jnp.sqrt(second_hat) + ADAM_EPS)
    return first_new, second_new, weight_new


def gram_triangle(store, values, product):
    high, low = halves(values)
    half = store.shape[1]

    def part(side, at):
        return side[at * half : (at + 1) * half, :] if product is nt else side[:, at * half : (at + 1) * half]

    for at, (i, j) in enumerate(((0, 0), (0, 1), (1, 1))):
        store[at * half : (at + 1) * half, :] = (
            product(part(high, i), part(high, j))
            + product(part(high, i), part(low, j))
            + product(part(low, i), part(high, j))
        )


def sort_rows(quarter_ref, rows_ref, up_ref, down_ref):
    slices = (quarter_ref.shape[0] - 32) // 4
    wide = 3 * PAIR // 8
    for high in range(2):
        at = slice(high * slices, (high + 1) * slices)
        first = high * (2 * slices + 32)
        up_ref[at, :] = quarter_ref[first : first + slices, :]
        down_ref[at, :] = quarter_ref[first + slices : first + 2 * slices, :]
        values = rows_ref[high].astype(F32)
        down_ref[2 * slices + high * wide : 2 * slices + (high + 1) * wide, :] = values[0:wide].astype(BF16)
    up_ref[2 * slices : 2 * slices + 32, :] = quarter_ref[2 * slices : 2 * slices + 32, :]
    up_ref[2 * slices + 32 : 2 * slices + 2 * wide, :] = jnp.zeros((2 * wide - 32, up_ref.shape[1]), BF16)
    return jnp.concatenate([rows_ref[high].astype(F32)[wide:] for high in range(2)], axis=0).astype(BF16)


def choose_kernel(where_ref, quarter_ref, rows_ref, first_ref, rest_ref, sorted_ref):
    side = where_ref[SIDE]
    main = first_ref.shape[0]
    small = sort_rows(quarter_ref, rows_ref, sorted_ref.at[0], sorted_ref.at[1])
    first_ref[...] = sorted_ref[1 - side]
    rest_ref[0:main, :] = sorted_ref[side]
    rest_ref[main:, :] = small


def put(all_ref, scale, sources, low, base_rows, matrix):
    for high, (ref, at) in enumerate(sources):
        piece = 4 * high + low
        to = pl.ds(pl.multiple_of(matrix + piece * base_rows, 8), base_rows)
        all_ref[to, :] = scale * ref[at : at + base_rows, :].astype(F32)


def gram_kernel(
    where_ref, square_ref, q0_ref, r0_ref, q1_ref, r1_ref, y0_ref, y1_ref, mq_ref, mo_ref, mu_ref, md_ref,
    near_ref, far_ref, all_ref, pack_ref, sorted_ref,
):
    dp, across, core, side = where_ref[GROUP], where_ref[ROW], where_ref[CORE], where_ref[SIDE]
    clip = jnp.max(CLIP_NORM / jnp.maximum(jnp.sqrt(square_ref[...]), CLIP_NORM))
    units, wide = mu_ref.shape[1], mq_ref.shape[1]
    slices = units // 8
    for turn, (quarter, rows) in enumerate(((q0_ref, r0_ref), (q1_ref, r1_ref))):
        sort_rows(quarter, rows, sorted_ref.at[2 * turn], sorted_ref.at[2 * turn + 1])

    def gather(type_index, put_rows):
        for turn, got in enumerate((y0_ref, y1_ref)):
            put_rows(sorted_ref.at[2 * turn + type_index], (2 * turn) ^ (dp & 3))
            put_rows(got, (2 * turn + 1) ^ (dp & 3))

    def grams(*pair):
        for index, (values, product) in enumerate(pair):
            gram_triangle(pack_ref, values, product)
            half = pack_ref.shape[0] // 2
            slot = index ^ across
            near_ref[slot] = pack_ref[pl.ds(pl.multiple_of(core * half, 8), half), :]
            far_ref[slot] = pack_ref[pl.ds(pl.multiple_of((1 - core) * half, 8), half), :]

    @pl.when(side == 0)
    def _():
        def up_out(ref, low):
            put(all_ref, clip, ((ref, 0), (ref, slices)), low, slices, 0)
            all_ref[pl.ds(pl.multiple_of(units + low * 32, 8), 32), :] = clip * ref[
                2 * slices : 2 * slices + 32, :
            ].astype(F32)

        gather(0, up_out)
        up = MUON_MOMENTUM * mu_ref[...] + jnp.transpose(all_ref[0:units, :])
        out = MUON_MOMENTUM * mo_ref[...] + all_ref[units : units + mo_ref.shape[0], :]
        grams((up, nt), (out, tn))

    @pl.when(side == 1)
    def _():
        def down_qkv(ref, low):
            put(all_ref, clip, ((ref, 0), (ref, slices)), low, slices, 0)
            put(all_ref, clip, ((ref, 2 * slices), (ref, 2 * slices + wide // 8)), low, wide // 8, units)

        gather(1, down_qkv)
        qkv = MUON_MOMENTUM * mq_ref[...] + jnp.transpose(heads_apart(all_ref[units : units + wide, :], True))
        down = MUON_MOMENTUM * md_ref[...] + all_ref[0:units, :]
        grams((qkv, nt), (down, tn))


def momentum_kernel(
    where_ref, square_ref, q0_ref, r0_ref, q1_ref, r1_ref, y0_ref, y1_ref, rest0_ref, rest1_ref,
    mq_ref, mo_ref, mu_ref, md_ref,
    emb_ref, emb_m_ref, emb_v_ref, head_ref, head_m_ref, head_v_ref, gain_ref, gain_m_ref, gain_v_ref,
    norm_ref, mq_out, mo_out, mu_out, md_out,
    emb_m_out, emb_v_out, emb_out, head_m_out, head_v_out, head_out, gain_m_out, gain_v_out, gain_out,
    all_ref, rows_ref, sorted_ref, got_ref,
):
    dp, side = where_ref[GROUP], where_ref[SIDE]
    norm = jnp.sqrt(square_ref[...])
    norm_ref[...] = norm
    clip = jnp.max(CLIP_NORM / jnp.maximum(norm, CLIP_NORM))
    units, wide, out_rows = mu_ref.shape[1], mq_ref.shape[1], mo_ref.shape[0]
    slices = units // 8
    main = y0_ref.shape[0]
    qkv_at, out_at = 2 * units + out_rows, 2 * units

    def place(up_ref, down_ref, small, low):
        put(all_ref, clip, ((up_ref, 0), (up_ref, slices)), low, slices, 0)
        put(all_ref, clip, ((down_ref, 0), (down_ref, slices)), low, slices, units)
        put(all_ref, clip, ((down_ref, 2 * slices), (down_ref, 2 * slices + wide // 8)), low, wide // 8, qkv_at)
        all_ref[pl.ds(pl.multiple_of(out_at + low * 32, 8), 32), :] = clip * up_ref[
            2 * slices : 2 * slices + 32, :
        ].astype(F32)
        for high in range(2):
            to = pl.ds(pl.multiple_of((4 * high + low) * 8, 8), 8)
            rows_ref[to, :] = clip * small.astype(F32)[8 * high : 8 * high + 8]

    for turn, (quarter, rows, first, rest) in enumerate(
        ((q0_ref, r0_ref, y0_ref, rest0_ref), (q1_ref, r1_ref, y1_ref, rest1_ref))
    ):
        small = sort_rows(quarter, rows, sorted_ref.at[0], sorted_ref.at[1])
        place(sorted_ref.at[0], sorted_ref.at[1], small, (2 * turn) ^ (dp & 3))
        got_ref[side] = first[...]
        got_ref[1 - side] = rest[0:main, :]
        place(got_ref.at[0], got_ref.at[1], rest[main:, :], (2 * turn + 1) ^ (dp & 3))
    mu_out[...] = MUON_MOMENTUM * mu_ref[...] + jnp.transpose(all_ref[0:units, :])
    md_out[...] = MUON_MOMENTUM * md_ref[...] + all_ref[units : 2 * units, :]
    mo_out[...] = MUON_MOMENTUM * mo_ref[...] + all_ref[out_at:qkv_at, :]
    mq_out[...] = MUON_MOMENTUM * mq_ref[...] + jnp.transpose(heads_apart(all_ref[qkv_at:, :], True))
    vocab = emb_ref.shape[0]
    head_m_out[...], head_v_out[...], head_out[...] = adam_step(
        head_ref[...], rows_ref[0:vocab, :], head_m_ref[...], head_v_ref[...], HEAD_RATE, WEIGHT_DECAY
    )
    emb_m_out[...], emb_v_out[...], emb_out[...] = adam_step(
        emb_ref[...], rows_ref[vocab : 2 * vocab, :], emb_m_ref[...], emb_v_ref[...], EMBED_RATE, WEIGHT_DECAY
    )
    gain_m_out[...], gain_v_out[...], gain_out[...] = adam_step(
        gain_ref[...], rows_ref[2 * vocab : 2 * vocab + 3, :], gain_m_ref[...], gain_v_ref[...], GAIN_RATE, 0.0
    )


def rows_kernel(where_ref, out_ref, out_got_ref, grad_ref, grad_got_ref, block_ref, input_ref):
    row = where_ref[ROW]
    size = out_got_ref.shape[0]
    block_ref[row] = out_ref[0:size, :]
    block_ref[1 - row] = out_got_ref[...]
    input_ref[row] = grad_ref[0:size, :]
    input_ref[1 - row] = grad_got_ref[...].astype(F32)


def squares_kernel(quarter_ref, quarter_z_ref, rows_ref, rows_z_ref, out_ref):
    wide = 3 * PAIR // 8
    total = 0.0
    for ref in (quarter_ref, quarter_z_ref):
        values = ref[...].astype(F32)
        total = total + jnp.sum(values * values)
    for ref in (rows_ref, rows_z_ref):
        for at in range(ref.shape[0]):
            values = ref[at].astype(F32)
            total = total + jnp.sum(values[0:wide] * values[0:wide]) + 0.25 * jnp.sum(values[wide:] * values[wide:])
    out_ref[...] = jnp.full(out_ref.shape, total, F32)


def three(left, right):
    left_high, left_low = halves(left)
    right_high, right_low = halves(right)
    return nn(
        jnp.concatenate([left_high, left_high, left_low], axis=1),
        jnp.concatenate([right_high, right_low, right_high], axis=0),
    )


def once(left, right):
    return nn(left.astype(BF16), right.astype(BF16))


def schulz_kernel(where_ref, mine_ref, other_ref, near_ref, far_ref, pack_ref, poly_ref, gram_ref, tri_ref):
    half, block = mine_ref.shape
    size = 2 * block
    core = where_ref[CORE]
    pack_ref[pl.ds(pl.multiple_of(core * half, 8), half), :] = mine_ref[...]
    pack_ref[pl.ds(pl.multiple_of((1 - core) * half, 8), half), :] = other_ref[...]
    gram_ref[0:block, 0:block] = pack_ref[0:block, :]
    corner = pack_ref[block:size, :]
    gram_ref[0:block, block:] = corner
    gram_ref[block:, 0:block] = jnp.transpose(corner)
    gram_ref[block:, block:] = pack_ref[size:, :]
    gram = gram_ref[...]
    rows = lax.broadcasted_iota(jnp.int32, gram.shape, 0)
    columns = lax.broadcasted_iota(jnp.int32, gram.shape, 1)
    diagonal = rows == columns
    trace = jnp.sum(jnp.where(diagonal, gram, 0.0))
    inverse = 1.0 / (jnp.sqrt(jnp.full((1, size), trace, F32)) + 1e-07)
    gram = gram * (inverse * inverse)

    def sweep(gram, poly, times, last=False):
        change = SCHULZ_SQUARE * gram + SCHULZ_CUBE * times(gram, gram)
        if poly is None:
            poly_ref[...] = change * inverse + jnp.where(diagonal, SCHULZ_LINEAR * inverse, 0.0)
        else:
            poly_ref[...] = SCHULZ_LINEAR * poly + times(change, poly)
        if not last:
            moved = SCHULZ_LINEAR * gram + times(change, gram)
            gram_ref[...] = SCHULZ_LINEAR * moved + times(moved, change)

    sweep(gram, None, once)
    sweep(gram_ref[...], poly_ref[...], once)
    sweep(gram_ref[...], poly_ref[...], once)
    for index in range(3, NS_STEPS):
        sweep(gram_ref[...], poly_ref[...], three, index == NS_STEPS - 1)
    poly = poly_ref[...]
    spine = jnp.sum(jnp.where(diagonal, poly, 0.0), axis=0, keepdims=True)
    off = jnp.where(diagonal, 0.0, poly).astype(BF16)
    high = spine.astype(BF16).astype(F32)
    low = spine - high
    rest = jnp.zeros((14, block), F32)
    tops = [
        jnp.concatenate([high[:, at], low[:, at], rest], axis=0).astype(BF16)
        for at in (slice(0, block), slice(block, size))
    ]
    part = half - block
    tri_ref[0, 0:block, :] = off[0:block, 0:block]
    tri_ref[0, block:half, :] = off[0:part, block:]
    tri_ref[0, half:, :] = tops[0]
    tri_ref[1, 0 : block - part, :] = off[part:block, block:]
    tri_ref[1, block - part : half, :] = off[block:, block:]
    tri_ref[1, half:, :] = tops[1]
    near_ref[...] = tri_ref[core]
    far_ref[...] = tri_ref[1 - core]


def muon_kernel(
    where_ref, mq_ref, mo_ref, mu_ref, md_ref, near0, near1, near2, near3, far0, far1, far2, far3,
    wq_ref, wo_ref, wu_ref, wd_ref, wq_out, wo_out, wu_out, wd_out, tri_ref,
):
    across, core, side = where_ref[ROW], where_ref[CORE], where_ref[SIDE]
    held = 2 * side + across
    for at, (near, far) in enumerate(((near0, far0), (near1, far1), (near2, far2), (near3, far3))):
        tri_ref[at, core] = near[...]
        tri_ref[at, 1 - core] = far[...]
    block = near0.shape[1]
    half = near0.shape[0] - 16
    part = half - block

    def ortho(matrix, values, left):
        slot = matrix ^ held
        first = tri_ref[slot, 0]
        second = tri_ref[slot, 1]
        corner = jnp.concatenate([first[block:half], second[0 : block - part]], axis=0)
        upper = jnp.concatenate([first[0:block], corner], axis=1)
        lower = jnp.concatenate([jnp.transpose(corner), second[block - part : half]], axis=1)
        poly = jnp.concatenate([upper, lower], axis=0)
        spines = [tri[half:].astype(F32) for tri in (first, second)]
        spine = jnp.concatenate([s[0:1] + s[1:2] for s in spines], axis=1)
        if left:
            spine = jnp.transpose(jnp.broadcast_to(spine, (8, 2 * block)))[:, 0:1]
            return nn(poly, values.astype(BF16)) + values * spine
        return nn(values.astype(BF16), poly) + values * spine

    def moved(weight, ortho, longest):
        return weight * (1.0 - MUON_RATE * MUON_DECAY) - MUON_RATE * 0.2 * math.sqrt(longest) * ortho

    wu_out[...] = moved(wu_ref[...], ortho(0, mu_ref[...], True), max(D, FF))
    wo_out[...] = moved(wo_ref[...], ortho(1, mo_ref[...], False), D)
    wq_out[...] = moved(wq_ref[...], ortho(2, mq_ref[...], True), 3 * D)
    wd_out[...] = moved(wd_ref[...], ortho(3, md_ref[...], False), max(D, FF))


VMEM = pl.BlockSpec(memory_space=pltpu.VMEM)
SMEM = pl.BlockSpec(memory_space=pltpu.SMEM)
VMEM_LIMIT = 14 * 1024 * 1024


def call(body, name, ins, outs, scratch=(), scalars=0, plain=(), far=(), micros=1):
    shapes = [
        (pltpu.HBM if at in far else pltpu.VMEM)(shape, dtype)
        for at, (shape, dtype) in enumerate(outs)
    ]
    held = [
        value if at < scalars else pltpu.with_memory_space_constraint(value, pltpu.HBM if at in plain else pltpu.VMEM)
        for at, value in enumerate(ins)
    ]
    return pl.pallas_call(
        body,
        name=name,
        out_shape=shapes,
        in_specs=[SMEM] * scalars + [VMEM] * (len(ins) - scalars),
        out_specs=[VMEM] * len(shapes),
        scratch_shapes=list(scratch),
        compiler_params=pltpu.CompilerParams(vmem_limit_bytes=VMEM_LIMIT),
        cost_estimate=pl.CostEstimate(flops=micros * 10**8, bytes_accessed=0, transcendentals=0),
    )(*held)


def swap(values, bit):
    return lax.ppermute(values, "tensor", [(i, i ^ bit) for i in range(4)])


def swap_dp(values, bit):
    return lax.ppermute(values, "dp", [(i, i ^ bit) for i in range(lax.axis_size("dp"))])


def swap_both(values, bit, dp_bit):
    width = lax.axis_size("tensor")
    pairs = [
        (p * width + t, (p ^ dp_bit) * width + (t ^ bit)) for p in range(lax.axis_size("dp")) for t in range(width)
    ]
    return lax.ppermute(values, ("dp", "tensor"), pairs)


def add(left, right):
    return (left.astype(F32) + right.astype(F32)).astype(BF16)


def join(*parts):
    return jnp.concatenate(parts, axis=-2)


def after(values, done):
    return lax.optimization_barrier((values, done))[0]


def over_rest(piece):
    bit = 8
    while bit < lax.axis_size("dp"):
        piece = add(piece, swap_dp(piece, bit))
        bit *= 2
    return piece


def on_device(
    noised, targets, timesteps, segments, embedding, out_head, norm_gains,
    w_qkv, w_out, w_up, w_down, mom_qkv, mom_out, mom_up, mom_down,
    embed_m, embed_v, head_m, head_v, gains_m, gains_v,
):
    place = lax.axis_index("tensor")
    group = lax.axis_index("dp") & 7
    row = place // 2
    core = place % 2
    size = noised.shape[1]
    length = segments.shape[1]
    own = 2 * size
    order = jnp.stack([place, place ^ 2, place ^ 1, place ^ 3])

    ids = jnp.stack([noised, targets])
    mine = lax.dynamic_index_in_dim(ids, row, 1, keepdims=False)
    send_ids = lax.dynamic_index_in_dim(ids, 1 - row, 1, keepdims=False)
    got = swap(send_ids, 2)
    own_ids = jnp.stack([mine, got], axis=1)
    tok = jnp.concatenate([own_ids[0], swap(own_ids[0], 1)], axis=0)
    seg_row = lax.dynamic_index_in_dim(segments, row, 0, keepdims=False)
    span_ids = jnp.arange(timesteps.shape[1], dtype=jnp.int32)
    starts = jnp.sum((seg_row[None, :] < span_ids[:, None]).astype(jnp.int32), axis=1)
    times = lax.dynamic_index_in_dim(timesteps, row, 0, keepdims=False)
    stand = jnp.stack([group, row, core, group & 1])
    where = jnp.concatenate([row * 4 + order, order, times, starts, stand]).astype(jnp.int32)
    table = jnp.asarray(position_table(max(length, 1000), D))

    unit_rows = w_up.shape[1]
    out_rows = w_out.shape[0]
    side = (group & 1).reshape(1).astype(jnp.int32)
    pack_rows = 3 * PAIR + out_rows
    wa_mine, wa_part = call(
        attention_weights_kernel, "attention_weights", [side, after(w_qkv, send_ids), w_out],
        [((pack_rows, D), BF16), ((pack_rows // 2, D), BF16)], scalars=1, plain=(1, 2),
    )
    (wb_mine,) = call(
        ffn_weights_kernel, "ffn_weights", [after(w_up, wa_part), w_down], [((2 * unit_rows, D), BF16)], plain=(0, 1)
    )
    wa_part = swap(wa_part, 2)

    hidden0, a1, aug = call(
        embed_kernel, "embed",
        [where, tok, segments.reshape(-1, size), table, embedding, norm_gains],
        [((own, D), F32), ((length, D), BF16), ((length, PAIR), BF16)],
        [pltpu.VMEM((VOCAB_PAD + SPAN_PAD, 2 * D), F32)],
        scalars=1, plain=(2, 3, 4, 5), micros=4,
    )

    def attend(first, second):
        return call(
            attend_kernel, "attend", [a1, aug, first, second],
            [((2, length, 3 * PAIR), BF16), ((2 * PAIR, own), F32), ((4, length, own), BF16), ((8, own), F32)],
            micros=5,
        )

    wb_across = swap(wb_mine, 2)
    wa = [wa_mine, swap(wa_mine, 1)]
    qkv_a, ctx_a, weights_a, inverse_a = attend(*wa)
    wa_part = after(wa_part, a1)
    (wa_across,) = call(
        join_kernel, "join", [where, wa_part, after(swap_dp(wa_part, 1), ctx_a)], [((2, pack_rows // 2, D), BF16)], scalars=1
    )
    wa_across = wa_across.reshape(pack_rows, D)
    wa += [wa_across, swap(wa_across, 1)]
    qkv_b, ctx_b, weights_b, inverse_b = attend(*wa[2:])
    wb = [wb_mine, swap(wb_mine, 1)]
    half_chunks = FF // CHUNK // 2
    hidden1, partial2, a2, act_a, slope_a = call(
        ffn_up_kernel, "ffn_up", [ctx_a, ctx_b, hidden0, norm_gains, *wa, *wb],
        [((own, D), F32), ((own, D), F32), ((own, D), BF16)] + [((half_chunks, own, CHUNK), BF16)] * 2,
        plain=(3,), micros=7,
    )
    wb_across = after(wb_across, a2)
    wb += [wb_across, swap(wb_across, 1)]
    slices = unit_rows // 4
    hidden2, d_h2, d_ffn, d_a2, act_b, slope_b, keep_a, send_a, part = call(
        ffn_kernel, "ffn",
        [where, partial2, a2, out_head.T, norm_gains, own_ids[1], act_a, slope_a, *wb],
        [((own, D), BF16), ((own, D), F32), ((own, D), BF16), ((own, D), F32)]
        + [((2, own, CHUNK), BF16)] * 2 + [((8, slices, D), BF16)] * 2 + [((VOCAB_PAD + 8, D), F32)],
        [
            pltpu.VMEM((half_chunks, own, CHUNK), BF16),
            pltpu.VMEM((half_chunks, own, CHUNK), BF16),
            pltpu.VMEM((VOCAB_PAD, D), F32),
        ],
        scalars=1, plain=(3, 4), far=(0,), micros=10,
    )
    got_a = swap(send_a, 1)
    d_h1, d_attn, keep_b, send_b, keep_o, send_o, gain1 = call(
        ffn_end_kernel, "ffn_end",
        [where, ctx_a, ctx_b, hidden1, d_h2, d_ffn, d_a2, a2, norm_gains, act_a, slope_a, act_b, slope_b, *wb],
        [((own, D), F32), ((own, D), BF16)] + [((8, slices, D), BF16)] * 2 + [((8, out_rows // 4, D), BF16)] * 2 + [((8, D), F32)],
        [pltpu.VMEM((own, D), F32)], scalars=1, plain=(8,), micros=5,
    )
    got_b, got_o = swap(send_b, 1), swap(send_o, 1)

    def back(qkv, weights, ctx, inverse, d_attn, packs):
        return call(
            attend_back_kernel, "attend_back", [qkv, weights, ctx, inverse, d_attn, *packs],
            [((2, own, PAIR), BF16), ((2, own, 2 * PAIR), BF16), ((2, own, 2 * PAIR), BF16)], micros=5,
        )

    keep_x, send_x = add(keep_a[0:4], got_a[0:4]), add(keep_a[4:8], got_a[4:8])
    got_x = swap(send_x, 2)
    got_b = after(got_b, send_x)
    keep_y, send_y = add(keep_b[0:4], got_b[0:4]), add(keep_b[4:8], got_b[4:8])
    got_y = swap_dp(send_y, 1)
    got_o = after(got_o, send_y)
    keep_o, send_o = add(keep_o[0:4], got_o[0:4]), add(keep_o[4:8], got_o[4:8])
    got_o = swap(send_o, 2)
    d_attn = after(d_attn, (send_x, send_y, send_o))
    dq_b, near_b, far_b = back(qkv_b, weights_b, ctx_b, inverse_b, d_attn, wa[2:])
    far_b = swap(far_b, 1)
    dq_a, near_a, far_a = back(qkv_a, weights_a, ctx_a, inverse_a, after(d_attn, dq_b), wa[:2])
    far_a = swap(far_a, 1)
    out_got = swap(after(hidden2, dq_a)[size:], 2)
    got_x, got_o, dq_b = lax.optimization_barrier((got_x, got_o, dq_b))
    half_a = join(add(keep_x, got_x), add(keep_o, got_o))
    near_b = after(near_b, half_a)
    grads = [((own, D), F32), ((8, 48, D), BF16), ((8, 48, D), BF16)]
    d_a1, keep2_b, send2_b = call(
        input_far_kernel, "input_far", [where, dq_b, near_b, far_b, a1, *wa[2:]], grads, scalars=1, micros=4
    )
    got2_b = swap(send2_b, 1)
    got_y, d_a1 = lax.optimization_barrier((got_y, d_a1))
    half_b = add(keep_y, got_y)
    d_a1 = after(d_a1, (half_a, half_b))
    got_y, got_x = swap_dp(half_a[2:4], 1), swap(half_b[2:4], 2)
    igrad, keep2, send2, small = call(
        input_kernel, "input_grad",
        [where, dq_a, near_a, far_a, a1, *wa[:2], d_a1, hidden0, d_h1, norm_gains, tok, part, gain1],
        grads + [((8, 8, D), F32)], [pltpu.VMEM((64, D), F32)], scalars=1, plain=(10,), micros=5,
    )
    got_x, got_y, small, out_got = lax.optimization_barrier((got_x, got_y, small, out_got))
    got2 = swap(send2, 1)
    small = small.astype(BF16)
    got_small = swap(small, 1)
    half_a, half_b = add(half_a[0:2], got_y), add(half_b[0:2], got_x)
    send_z = join(half_a[1], half_b[1])
    got_z = swap_dp(send_z, 2)
    near2, far2 = (values.reshape(2, 4, 48, D) for values in (add(keep2, got2), add(keep2_b, after(got2_b, send_z))))
    small = add(small, got_small).reshape(2, 4, 8, D)

    got2_y = swap_dp(join(near2[1], small[1], far2[1]), 1)
    quarter = add(join(half_a[0], half_b[0]), got_z)
    igrad_got = swap(igrad[size:].astype(BF16), 2)
    rows = add(join(near2[0], small[0], far2[0]), after(got2_y, igrad_got))
    wide = near2.shape[-2]
    got2_x = swap(join(rows[:, wide + 8 :], rows[:, wide : wide + 8]), 2)
    rows = add(rows[:, 0 : wide + 8], got2_x)
    rows = after(rows, quarter)
    rows = add(rows[0:2], swap_dp(rows[2:4], 2))
    got_z = swap_dp(quarter, 4)
    quarter = over_rest(add(quarter, got_z))
    rows = after(rows, quarter)
    rows = over_rest(add(rows, swap_dp(rows, 4)))
    quarter_z, rows_z = swap_dp(quarter, 2), swap_dp(rows, 2)
    main = 2 * slices // 2 + 3 * PAIR // 4

    def choose(quarter, rows):
        return call(
            choose_kernel, "choose", [where, quarter, rows], [((main, D), BF16), ((main + 16, D), BF16)],
            [pltpu.VMEM((2, main, D), BF16)], scalars=1,
        )

    first0, rest0 = choose(quarter, rows)
    first0 = swap_dp(first0, 1)
    first1, rest1 = choose(quarter_z, rows_z)
    first1 = swap_dp(first1, 1)
    (square,) = call(squares_kernel, "squares", [quarter, quarter_z, rows, rows_z], [((8, 128), F32)])
    square = square + swap(square, 1)
    square = (square + swap(square, 2)) + (swap_dp(square, 1) + swap_both(square, 2, 1))
    rest0, rest1 = (swap_dp(rest, 1) for rest in after((rest0, rest1), square))

    def like(*arrays):
        return [(a.shape, F32) for a in arrays]

    heads = [out_head.T, head_m.T, head_v.T]
    triangle = ((2, 3 * D // 4, D // 2), F32)
    sums = [where, square, quarter, rows, quarter_z, rows_z, first0, first1]
    moments = [mom_qkv, mom_out, mom_up, mom_down]
    sorted_rows = pltpu.VMEM((4, main, D), BF16)
    near, far = call(
        gram_kernel, "gram", sums + moments, [triangle, triangle],
        [pltpu.VMEM((2 * unit_rows, D), F32), pltpu.VMEM((3 * D // 2, D // 2), F32), sorted_rows], scalars=1, micros=3,
    )
    far = swap(far, 1)
    half = after(near[0] + far[0], rest0) + swap(near[1] + far[1], 2)
    poly = [((16 + 3 * D // 4, D // 2), BF16)] * 2
    near, far = call(
        schulz_kernel, "schulz", [where, half, swap(half, 1)], poly,
        [pltpu.VMEM((3 * D // 2, D // 2), F32), pltpu.VMEM((D, D), F32), pltpu.VMEM((D, D), F32),
         pltpu.VMEM((2, 16 + 3 * D // 4, D // 2), BF16)],
        scalars=1, micros=10,
    )
    near, far = after((near, far), rest1)
    block_out, input_grad = call(
        rows_kernel, "rows", [where, hidden2, after(out_got, near), igrad, igrad_got],
        [((2, size, D), BF16), ((2, size, D), F32)], scalars=1, plain=(1, 3), far=(0, 1),
    )
    outs = call(
        momentum_kernel, "momentum",
        [where, after(square, near)] + sums[2:] + [rest0, rest1] + moments
        + [embedding, embed_m, embed_v, *heads, norm_gains, gains_m, gains_v],
        [((8, 128), F32)] + like(mom_qkv, mom_out, mom_up, mom_down, embed_m, embed_v, embedding)
        + like(*heads, gains_m, gains_v, norm_gains),
        [
            pltpu.VMEM((2 * unit_rows + out_rows + 3 * PAIR, D), F32), pltpu.VMEM((64, D), F32),
            pltpu.VMEM((2, main, D), BF16), pltpu.VMEM((2, main, D), BF16),
        ],
        scalars=1, plain=range(14, 23), far=range(14), micros=5,
    )
    norm = outs[0]
    moms = outs[1:5]
    mom_qkv_new, mom_out_new, mom_up_new, mom_down_new = moms
    embed_new, head_new, gains_new = outs[5:8], [h.T for h in outs[8:11]], outs[11:14]
    grad_norm = norm[0, 0]
    near_x, near_y = swap(near, 2), swap_dp(near, 1)
    nears = [near, *after((near_x, near_y, swap_both(near, 2, 1)), (moms, block_out, input_grad))]
    fars = [far] + [swap(values, 1) for values in nears[1:]]
    qkv_new, out_new, up_new, down_new = call(
        muon_kernel, "muon",
        [where, *moms, *nears, *fars, w_qkv, w_out, w_up, w_down],
        like(w_qkv, w_out, w_up, w_down),
        [pltpu.VMEM((4, 2, 16 + 3 * D // 4, D // 2), BF16)],
        scalars=1, plain=(1, 2, 3, 4), far=range(4), micros=5,
    )
    return (
        block_out, input_grad, grad_norm,
        mom_qkv_new, qkv_new, mom_out_new, out_new, mom_up_new, up_new, mom_down_new, down_new,
        *embed_new, *head_new, *gains_new,
    )


def solution(mesh):
    columns, rows = P(None, "tensor"), P("tensor", None)
    matrices = (columns, rows, columns, rows)
    in_specs = (
        (P("dp", "tensor"), P("dp", "tensor"), P("dp", None), P("dp", None), P(), P(), P())
        + matrices + matrices + (P(),) * 6
    )
    out_specs = (
        (P("dp", "tensor", None), P("dp", "tensor", None), P())
        + (columns, columns, rows, rows, columns, columns, rows, rows) + (P(),) * 9
    )
    return jax.shard_map(on_device, mesh=mesh, in_specs=in_specs, out_specs=out_specs, check_vma=False)
```

```python
import math

import jax
import jax.numpy as jnp
import numpy as np
from jax import lax
from jax.experimental import pallas as pl
from jax.experimental.pallas import tpu as pltpu
from jax.sharding import PartitionSpec as P

D = 512
HEAD_DIM = 64
PAIR = 2 * HEAD_DIM
FF = 2048
NS_STEPS = 5
STEP = 10
CHUNK = 256
VOCAB_PAD = 32
SPAN_PAD = 16
GROUP, ROW, CORE, SIDE = 16, 17, 18, 19

HIGHEST = lax.Precision.HIGHEST
F32 = jnp.float32
BF16 = jnp.bfloat16
NORM_EPS = 1e-05
MASK_FILL = 1e30
MUON_MOMENTUM = 0.5
MUON_RATE = 0.3
MUON_DECAY = 0.1
SCHULZ_LINEAR = 3.4445
SCHULZ_SQUARE = -4.775
SCHULZ_CUBE = 2.0315
ADAM_BETA_ONE = 0.9
ADAM_BETA_TWO = 0.95
ADAM_EPS = 1e-08
EMBED_RATE = 0.3
HEAD_RATE = 0.02
GAIN_RATE = 0.6
WEIGHT_DECAY = 0.1
CLIP_NORM = 1.0


def nn(left, right, precision=None):
    return lax.dot_general(
        left, right, (((1,), (0,)), ((), ())), preferred_element_type=F32, precision=precision
    )


def nt(left, right, precision=None):
    return lax.dot_general(
        left, right, (((1,), (1,)), ((), ())), preferred_element_type=F32, precision=precision
    )


def tn(left, right, precision=None):
    return lax.dot_general(
        left, right, (((0,), (0,)), ((), ())), preferred_element_type=F32, precision=precision
    )


def halves(values):
    high = values.astype(BF16)
    return high, (values - high.astype(F32)).astype(BF16)


def position_table(length, width):
    half = width // 2
    rates = np.exp(-math.log(10000.0) * np.arange(half) / half)
    angles = np.arange(length)[:, None] * rates[None, :]
    return np.concatenate([np.sin(angles), np.cos(angles)], axis=1).astype(np.float32)


def normed_parts(values):
    centered = values - jnp.mean(values, axis=-1, keepdims=True)
    inv_std = lax.rsqrt(jnp.mean(centered * centered, axis=-1, keepdims=True) + NORM_EPS)
    return centered * inv_std, inv_std


def norm_back(grad_out, source, gain):
    normed, inv_std = normed_parts(source)
    scaled = grad_out * gain
    grad_in = inv_std * (
        scaled
        - jnp.mean(scaled, axis=-1, keepdims=True)
        - normed * jnp.mean(scaled * normed, axis=-1, keepdims=True)
    )
    return grad_in, jnp.sum(grad_out * normed, axis=0, keepdims=True)


def embed_kernel(where_ref, tok_ref, seg_ref, table_ref, emb_ref, gains_ref, h0_ref, a1_ref, aug_ref, rows_ref):
    vocab, width = emb_ref.shape
    half = width // 2
    blocks, size = tok_ref.shape
    spans = SPAN_PAD // 4
    rows_ref[...] = jnp.zeros_like(rows_ref)
    rows_ref[0:vocab, 0:width] = emb_ref[...]
    for span in range(spans):
        at_time = table_ref[pl.ds(where_ref[8 + span], 1), :]
        at_start = table_ref[pl.ds(where_ref[12 + span], 1), :]
        row = VOCAB_PAD + span
        rows_ref[row : row + 1, 0:width] = at_time
        rows_ref[row : row + 1, width : width + half] = at_start[:, half:]
        rows_ref[row : row + 1, width + half :] = at_start[:, :half]
    rows = rows_ref[...]
    high = rows.astype(BF16)
    rest = rows - high.astype(F32)
    middle = rest.astype(BF16)
    low = (rest - middle.astype(F32)).astype(BF16)
    stacked = jnp.concatenate([high, middle, low], axis=0)
    gain = gains_ref[0:1, :]
    for block in range(blocks):
        tok = tok_ref[block : block + 1, :]
        seg = seg_ref[pl.ds(where_ref[block], 1), :]
        hot_tok = (lax.broadcasted_iota(jnp.int32, (VOCAB_PAD, size), 0) == tok).astype(F32)
        hot_seg = (lax.broadcasted_iota(jnp.int32, (SPAN_PAD, size), 0) == seg).astype(F32)
        hot = jnp.concatenate([hot_tok, hot_seg], axis=0).astype(BF16)
        picked = tn(jnp.concatenate([hot, hot, hot], axis=0), stacked)
        table = table_ref[pl.ds(pl.multiple_of(where_ref[4 + block] * size, size), size), :]
        sin_p, cos_p = table[:, :half], table[:, half:]
        cos_s, sin_s = picked[:, width : width + half], picked[:, width + half :]
        place = jnp.concatenate([sin_p * cos_s - cos_p * sin_s, cos_p * cos_s + sin_p * sin_s], axis=1)
        hidden = picked[:, :width] + place
        if block * size < h0_ref.shape[0]:
            h0_ref[block * size : (block + 1) * size, :] = hidden
        a1_ref[block * size : (block + 1) * size, :] = (normed_parts(hidden)[0] * gain).astype(BF16)
        wide = (lax.broadcasted_iota(jnp.int32, (PAIR, size), 0) == seg).astype(F32)
        aug_ref[block * size : (block + 1) * size, :] = jnp.transpose(wide).astype(BF16)


def query_side(aug, own):
    return ((aug[:own].astype(F32) - 1.0) * MASK_FILL).astype(BF16)


def half_mask(values, head):
    lanes = lax.broadcasted_iota(jnp.int32, values.shape, 1)
    keep = (lanes >= head * HEAD_DIM) & (lanes < (head + 1) * HEAD_DIM)
    return jnp.where(keep, values.astype(F32), 0.0).astype(BF16)


def query_side(aug, own):
    return ((aug[:own].astype(F32) - 1.0) * MASK_FILL).astype(BF16)


def half_mask(values, head):
    lanes = lax.broadcasted_iota(jnp.int32, values.shape, 1)
    keep = (lanes >= head * HEAD_DIM) & (lanes < (head + 1) * HEAD_DIM)
    return jnp.where(keep, values.astype(F32), 0.0).astype(BF16)


def heads_apart(rows, back):
    count = rows.shape[0] // HEAD_DIM
    heads = count // 3
    if back:
        index = [j * heads + h for h in range(heads) for j in range(3)]
    else:
        index = [h * 3 + j for j in range(3) for h in range(heads)]
    return jnp.concatenate([rows[i * HEAD_DIM : (i + 1) * HEAD_DIM] for i in index], axis=0)


def attention_weights_kernel(side_ref, wq_ref, wo_ref, out_ref, part_ref):
    wide = wq_ref.shape[1]
    out_ref[0:wide, :] = heads_apart(jnp.transpose(wq_ref[...]), False).astype(BF16)
    out_ref[wide:, :] = wo_ref[...].astype(BF16)
    half = part_ref.shape[0]
    part_ref[...] = out_ref[pl.ds(pl.multiple_of(side_ref[0] * half, half), half), :]


def join_kernel(where_ref, mine_ref, got_ref, out_ref):
    side = where_ref[SIDE]
    out_ref[side] = mine_ref[...]
    out_ref[1 - side] = got_ref[...]


def ffn_weights_kernel(wu_ref, wd_ref, out_ref):
    units = wu_ref.shape[1]
    out_ref[0:units, :] = jnp.transpose(wu_ref[...]).astype(BF16)
    out_ref[units:, :] = wd_ref[...].astype(BF16)


def attend_kernel(a1_ref, aug_ref, w0, w1, qkv_ref, ctx_ref, weights_ref, inverse_ref):
    own = ctx_ref.shape[1]
    scale = HEAD_DIM**-0.5
    aug = aug_ref[...]
    aug_q = query_side(aug, own)
    inverse_ref[...] = jnp.zeros_like(inverse_ref)
    for shard, weight in enumerate((w0, w1)):
        qkv = nt(a1_ref[...], weight[0 : 3 * PAIR, :]).astype(BF16)
        qkv_ref[shard] = qkv
        keys = jnp.concatenate([qkv[:, PAIR : 2 * PAIR], aug], axis=1)
        value = qkv[:, 2 * PAIR :]
        query = qkv[:own, :PAIR].astype(F32) * scale
        for head in range(2):
            q_side = jnp.concatenate([half_mask(query, head), aug_q], axis=1)
            scores = nt(keys, q_side)
            top = jnp.max(scores, axis=0, keepdims=True)
            raised = jnp.exp(scores - top)
            inverse = 1.0 / jnp.sum(raised, axis=0, keepdims=True)
            weights = raised.astype(BF16)
            weights_ref[2 * shard + head] = weights
            out = tn(value, weights)
            at = shard * PAIR + head * HEAD_DIM
            ctx_ref[at : at + HEAD_DIM, :] = out[head * HEAD_DIM : (head + 1) * HEAD_DIM] * inverse
            inverse_ref[2 * shard + head : 2 * shard + head + 1, :] = inverse


def low_bits(piece, mine):
    return (piece ^ mine) & 1, lax.shift_right_logical(piece ^ mine, 1) & 1


def gelu_parts(upper):
    size = jnp.abs(upper)
    pdf = jnp.exp(-0.5 * upper * upper) * (1.0 / math.sqrt(2.0 * math.pi))
    turn = 1.0 / (1.0 + 0.2316419 * size)
    series = turn * (
        0.319381530
        + turn * (-0.356563782 + turn * (1.781477937 + turn * (-1.821255978 + turn * 1.330274429)))
    )
    tail = pdf * series
    cdf = jnp.where(upper < 0.0, tail, 1.0 - tail)
    return (upper * cdf).astype(BF16), (cdf + upper * pdf).astype(BF16)


def up_chunks(a2_ref, packs, act_ref, slope_ref, acc_ref, first):
    units = packs[0].shape[0] // 2
    parts = units // CHUNK
    for at, pack in enumerate(packs):
        act, slope = gelu_parts(nt(a2_ref[...], pack[0:units, :]))
        for part in range(parts):
            columns = slice(part * CHUNK, (part + 1) * CHUNK)
            act_ref[first + at * parts + part] = act[:, columns]
            slope_ref[first + at * parts + part] = slope[:, columns]
        acc_ref[...] += nn(act, pack[units:, :])


def ffn_up_kernel(
    ctx_a_ref, ctx_b_ref, h0_ref, gains_ref, wa0, wa1, wa2, wa3, wb0, wb1,
    h1_ref, acc_ref, a2_ref, act_ref, slope_ref,
):
    hidden1 = h0_ref[...]
    for ctx_ref, first, second in ((ctx_a_ref, wa0, wa1), (ctx_b_ref, wa2, wa3)):
        weight = jnp.concatenate([first[3 * PAIR :, :], second[3 * PAIR :, :]], axis=0)
        hidden1 = hidden1 + tn(ctx_ref[...].astype(BF16), weight)
    h1_ref[...] = hidden1
    acc_ref[...] = hidden1
    a2_ref[...] = (normed_parts(hidden1)[0] * gains_ref[1:2, :]).astype(BF16)
    up_chunks(a2_ref, (wb0, wb1), act_ref, slope_ref, acc_ref, 0)


def back_pair(d_ffn, acts, slopes, packs, part, a2_ref, acc_ref):
    units = packs[0].shape[0] // 2
    at = part * CHUNK
    up = jnp.concatenate([pack[at : at + CHUNK, :] for pack in packs], axis=0)
    down = jnp.concatenate([pack[units + at : units + at + CHUNK, :] for pack in packs], axis=0)
    d_up = (nt(d_ffn, down) * jnp.concatenate(slopes, axis=1).astype(F32)).astype(BF16)
    acc_ref[...] += nn(d_up, up)
    return tn(d_up, a2_ref[...]), tn(jnp.concatenate(acts, axis=1), d_ffn)


def ffn_next_kernel(part_ref, a2_ref, pack_ref, acc_ref, act_ref, slope_ref):
    acc_ref[...] = part_ref[...]
    up_chunks(a2_ref, (pack_ref,), act_ref, slope_ref, acc_ref, 0)


def ffn_kernel(
    where_ref, part_ref, a2_ref, head_ref, gains_ref, tgt_ref, act_a_ref, slope_a_ref, act_b_ref, slope_b_ref,
    wb0, wb1, wb2, wb3, out_ref, dh2_ref, dffn_ref, acc_ref, act_c_ref, slope_c_ref, keep_ref, send_ref, small_ref,
    act_ref, slope_ref, pad_ref,
):
    vocab = head_ref.shape[0]
    width = out_ref.shape[1]
    mine = where_ref[GROUP]
    pad_ref[...] = jnp.zeros_like(pad_ref)
    pad_ref[0:vocab, :] = head_ref[...]
    acc_ref[...] = part_ref[...]
    up_chunks(a2_ref, (wb3,), act_ref, slope_ref, acc_ref, 0)
    hidden2 = acc_ref[...]
    out_ref[...] = hidden2.astype(BF16)
    normed3, _ = normed_parts(hidden2)
    a3 = normed3 * gains_ref[2:3, :]
    head = pad_ref[...]
    a3_high, a3_low = halves(a3)
    head_high, head_low = halves(head)
    both = nt(jnp.concatenate([head_high, head_low], axis=0), a3_high)
    logits = both[0:VOCAB_PAD] + both[VOCAB_PAD:] + nt(head_high, a3_low)
    classes = lax.broadcasted_iota(jnp.int32, logits.shape, 0)
    logits = jnp.where(classes < vocab, logits, -MASK_FILL)
    raised = jnp.exp(logits - jnp.max(logits, axis=0, keepdims=True))
    targets = jnp.concatenate([tgt_ref[0:1, :], tgt_ref[1:2, :]], axis=1)
    d_logits = raised / jnp.sum(raised, axis=0, keepdims=True) - (classes == targets).astype(F32)
    d_high, d_low = halves(d_logits)
    both = nn(jnp.concatenate([d_high, d_low], axis=0), a3_high)
    small_ref[0:VOCAB_PAD, :] = both[0:VOCAB_PAD] + both[VOCAB_PAD:] + nn(d_high, a3_low)
    d_a3 = tn(
        jnp.concatenate([d_high, d_low, d_high], axis=0), jnp.concatenate([head_high, head_high, head_low], axis=0)
    )
    d_h2, g_gain2 = norm_back(d_a3, hidden2, gains_ref[2:3, :])
    small_ref[VOCAB_PAD:, :] = jnp.concatenate([g_gain2, jnp.zeros((7, width), F32)], axis=0)
    dh2_ref[...] = d_h2
    d_ffn = d_h2.astype(BF16)
    dffn_ref[...] = d_ffn
    acc_ref[...] = jnp.zeros_like(acc_ref)
    rows = CHUNK // 4
    near = ([act_a_ref[0], act_a_ref[2]], [slope_a_ref[0], slope_a_ref[2]], (wb0, wb1))
    far = ([act_b_ref[0], act_ref[0]], [slope_b_ref[0], slope_ref[0]], (wb2, wb3))
    for across, (acts, slopes, packs) in enumerate((near, far)):
        g_up, g_down = back_pair(d_ffn, acts, slopes, packs, 0, a2_ref, acc_ref)
        for core, target in enumerate((keep_ref, send_ref)):
            for piece in range(4):
                b0, b1 = low_bits(piece, mine)
                at = core * CHUNK + piece * rows
                target[4 * across + 2 * b0 + b1, 0:rows, :] = g_up[at : at + rows].astype(BF16)
                target[4 * across + 2 * b0 + b1, rows:, :] = g_down[at : at + rows].astype(BF16)
    act_c_ref[...] = act_ref[1]
    slope_c_ref[...] = slope_ref[1]


def ffn_end_kernel(
    where_ref, dffn_ref, part_ref, a2_ref, act_a_ref, slope_a_ref, act_b_ref, slope_b_ref, act_c_ref, slope_c_ref,
    wb0, wb1, wb2, wb3, acc_ref, keep_ref, send_ref,
):
    mine = where_ref[GROUP]
    d_ffn = dffn_ref[...]
    acc_ref[...] = part_ref[...]
    rows = CHUNK // 4
    near = ([act_a_ref[1], act_a_ref[3]], [slope_a_ref[1], slope_a_ref[3]], (wb0, wb1))
    far = ([act_b_ref[1], act_c_ref[...]], [slope_b_ref[1], slope_c_ref[...]], (wb2, wb3))
    for across, (acts, slopes, packs) in enumerate((near, far)):
        g_up, g_down = back_pair(d_ffn, acts, slopes, packs, 1, a2_ref, acc_ref)
        for core, target in enumerate((keep_ref, send_ref)):
            for piece in range(4):
                b0, b1 = low_bits(piece, mine)
                at = core * CHUNK + piece * rows
                target[4 * b0 + 2 * across + b1, 0:rows, :] = g_up[at : at + rows].astype(BF16)
                target[4 * b0 + 2 * across + b1, rows:, :] = g_down[at : at + rows].astype(BF16)


def ffn_norm_kernel(
    where_ref, ctx_a_ref, ctx_b_ref, h1_ref, dh2_ref, part_ref, gains_ref,
    dh1_ref, dattn_ref, keep_ref, send_ref, gain_ref,
):
    mine = where_ref[GROUP]
    d_h1_part, g_gain1 = norm_back(part_ref[...], h1_ref[...], gains_ref[1:2, :])
    d_h1 = dh2_ref[...] + d_h1_part
    dh1_ref[...] = d_h1
    d_attn = d_h1.astype(BF16)
    dattn_ref[...] = d_attn
    gain_ref[...] = jnp.broadcast_to(g_gain1, gain_ref.shape)
    out_rows = ctx_a_ref.shape[0] // 2
    for across, ctx_ref in enumerate((ctx_a_ref, ctx_b_ref)):
        g_out = nn(ctx_ref[...].astype(BF16), d_attn)
        for core in range(2):
            target = send_ref if core else keep_ref
            for piece in range(4):
                b0, b1 = low_bits(piece, mine)
                at = core * out_rows + piece * (out_rows // 4)
                target[4 * across + 2 * b0 + b1] = g_out[at : at + out_rows // 4].astype(BF16)


def attend_back_kernel(qkv_ref, weights_ref, ctx_ref, inverse_ref, dattn_ref, w0, w1, dq_ref, near_ref, far_ref):
    own = ctx_ref.shape[1]
    scale = HEAD_DIM**-0.5
    d_attn = dattn_ref[...]
    columns = jnp.transpose(inverse_ref[...])
    for shard, weight_ref in enumerate((w0, w1)):
        weight = weight_ref[3 * PAIR :, :]
        d_ctx = nt(d_attn, weight).astype(BF16).astype(F32)
        d_ctx_t = nt(weight, d_attn).astype(BF16).astype(F32)
        inner = d_ctx_t * ctx_ref[shard * PAIR : (shard + 1) * PAIR, :]
        key = qkv_ref[shard, :, PAIR : 2 * PAIR]
        value = qkv_ref[shard, :, 2 * PAIR :]
        query = qkv_ref[shard, 0:own, 0:PAIR].astype(F32) * scale
        dq_parts = []
        d_key = None
        d_value = None
        for head in range(2):
            mine = slice(head * HEAD_DIM, (head + 1) * HEAD_DIM)
            at = 2 * shard + head
            q_head = half_mask(query, head)
            d_ctx_head = half_mask(d_ctx * columns[:, at : at + 1], head)
            delta = jnp.sum(inner[mine], axis=0, keepdims=True) * inverse_ref[at : at + 1, :]
            weights = weights_ref[at]
            d_scores = (weights.astype(F32) * (nt(value, d_ctx_head) - delta)).astype(BF16)
            d_value_part = nn(weights, d_ctx_head)
            d_key_part = nn(d_scores, q_head)
            dq_parts.append(tn(key, d_scores)[mine])
            d_key = d_key_part if d_key is None else d_key + d_key_part
            d_value = d_value_part if d_value is None else d_value + d_value_part
        dq_ref[shard] = jnp.transpose(jnp.concatenate(dq_parts, axis=0) * scale).astype(BF16)
        near_ref[shard, :, 0:PAIR] = d_key[:own].astype(BF16)
        near_ref[shard, :, PAIR:] = d_value[:own].astype(BF16)
        far_ref[shard ^ 1, :, 0:PAIR] = d_key[own:].astype(BF16)
        far_ref[shard ^ 1, :, PAIR:] = d_value[own:].astype(BF16)


def qkv_grads(where_ref, dq_ref, near_ref, far_ref, a1, weights, keep_ref, send_ref, total):
    for shard, weight in enumerate(weights):
        d_kv = (near_ref[shard].astype(F32) + far_ref[shard].astype(F32)).astype(BF16)
        d_qkv = jnp.concatenate([dq_ref[shard], d_kv], axis=1)
        grad = tn(d_qkv, a1)
        target = send_ref if shard else keep_ref
        rows = grad.shape[0] // 8
        for piece in range(8):
            b0, b1 = low_bits(piece, where_ref[GROUP])
            target[4 * b0 + 2 * b1 + piece // 4] = grad[piece * rows : (piece + 1) * rows].astype(BF16)
        part = nn(d_qkv, weight[0 : 3 * PAIR, :])
        total = part if total is None else total + part
    return total


def input_far_kernel(where_ref, dq_ref, near_ref, far_ref, a1_ref, w0, w1, total_ref, keep_ref, send_ref):
    own = total_ref.shape[0]
    total_ref[...] = qkv_grads(where_ref, dq_ref, near_ref, far_ref, a1_ref[0:own, :], (w0, w1), keep_ref, send_ref, None)


def input_kernel(
    where_ref, dq_ref, near_ref, far_ref, a1_ref, w0, w1, total_ref, h0_ref, dh1_ref, gains_ref, tok_ref, part_ref, gain1_ref,
    igrad_ref, keep_ref, send_ref, small_ref, rows_ref,
):
    own, width = h0_ref.shape
    vocab = 27
    d_a1 = qkv_grads(
        where_ref, dq_ref, near_ref, far_ref, a1_ref[0:own, :], (w0, w1), keep_ref, send_ref, total_ref[...]
    )
    d_h0_part, g_gain0 = norm_back(d_a1, h0_ref[...], gains_ref[0:1, :])
    d_h0 = dh1_ref[...] + d_h0_part
    igrad_ref[...] = d_h0
    high, low = halves(d_h0)
    tok = jnp.concatenate([tok_ref[0:1, :], tok_ref[1:2, :]], axis=1)
    hot = (lax.broadcasted_iota(jnp.int32, (VOCAB_PAD, own), 0) == tok).astype(F32).astype(BF16)
    rows_ref[...] = jnp.zeros_like(rows_ref)
    rows_ref[0:vocab, :] = part_ref[0:vocab, :]
    rows_ref[vocab : 2 * vocab, :] = (nn(hot, high) + nn(hot, low))[0:vocab]
    rows_ref[2 * vocab : 2 * vocab + 1, :] = g_gain0
    rows_ref[2 * vocab + 1 : 2 * vocab + 2, :] = gain1_ref[0:1, :]
    rows_ref[2 * vocab + 2 : 2 * vocab + 3, :] = part_ref[VOCAB_PAD : VOCAB_PAD + 1, :]
    for piece in range(8):
        b0, b1 = low_bits(piece, where_ref[GROUP])
        small_ref[4 * b0 + 2 * b1 + piece // 4] = rows_ref[piece * 8 : (piece + 1) * 8, :]


def adam_step(weight, grad, first_m, second_m, rate, decay):
    first_new = ADAM_BETA_ONE * first_m + (1.0 - ADAM_BETA_ONE) * grad
    second_new = ADAM_BETA_TWO * second_m + (1.0 - ADAM_BETA_TWO) * grad * grad
    first_hat = first_new / (1.0 - ADAM_BETA_ONE**STEP)
    second_hat = second_new / (1.0 - ADAM_BETA_TWO**STEP)
    weight_new = weight * (1.0 - rate * decay) - rate * first_hat / (jnp.sqrt(second_hat) + ADAM_EPS)
    return first_new, second_new, weight_new


def gram_triangle(store, values, product):
    high, low = halves(values)
    half = store.shape[1]

    def part(side, at):
        return side[at * half : (at + 1) * half, :] if product is nt else side[:, at * half : (at + 1) * half]

    for at, (i, j) in enumerate(((0, 0), (0, 1), (1, 1))):
        store[at * half : (at + 1) * half, :] = (
            product(part(high, i), part(high, j))
            + product(part(high, i), part(low, j))
            + product(part(low, i), part(high, j))
        )


def sort_rows(quarter_ref, rows_ref, up_ref, down_ref):
    slices = (quarter_ref.shape[0] - 32) // 4
    wide = 3 * PAIR // 8
    for high in range(2):
        at = slice(high * slices, (high + 1) * slices)
        first = high * (2 * slices + 32)
        up_ref[at, :] = quarter_ref[first : first + slices, :]
        down_ref[at, :] = quarter_ref[first + slices : first + 2 * slices, :]
        values = rows_ref[high].astype(F32)
        down_ref[2 * slices + high * wide : 2 * slices + (high + 1) * wide, :] = values[0:wide].astype(BF16)
    up_ref[2 * slices : 2 * slices + 32, :] = quarter_ref[2 * slices : 2 * slices + 32, :]
    up_ref[2 * slices + 32 : 2 * slices + 2 * wide, :] = jnp.zeros((2 * wide - 32, up_ref.shape[1]), BF16)
    return jnp.concatenate([rows_ref[high].astype(F32)[wide:] for high in range(2)], axis=0).astype(BF16)


def choose_kernel(where_ref, quarter_ref, rows_ref, first_ref, rest_ref, sorted_ref):
    side = where_ref[SIDE]
    main = first_ref.shape[0]
    small = sort_rows(quarter_ref, rows_ref, sorted_ref.at[0], sorted_ref.at[1])
    first_ref[...] = sorted_ref[1 - side]
    rest_ref[0:main, :] = sorted_ref[side]
    rest_ref[main:, :] = small


def put(all_ref, scale, sources, low, base_rows, matrix):
    for high, (ref, at) in enumerate(sources):
        piece = 4 * high + low
        to = pl.ds(pl.multiple_of(matrix + piece * base_rows, 8), base_rows)
        all_ref[to, :] = scale * ref[at : at + base_rows, :].astype(F32)


def gram_kernel(
    where_ref, square_ref, q0_ref, r0_ref, q1_ref, r1_ref, y0_ref, y1_ref, mq_ref, mo_ref, mu_ref, md_ref,
    near_ref, far_ref, all_ref, pack_ref, sorted_ref,
):
    dp, across, core, side = where_ref[GROUP], where_ref[ROW], where_ref[CORE], where_ref[SIDE]
    clip = jnp.max(CLIP_NORM / jnp.maximum(jnp.sqrt(square_ref[...]), CLIP_NORM))
    units, wide = mu_ref.shape[1], mq_ref.shape[1]
    slices = units // 8
    for turn, (quarter, rows) in enumerate(((q0_ref, r0_ref), (q1_ref, r1_ref))):
        sort_rows(quarter, rows, sorted_ref.at[2 * turn], sorted_ref.at[2 * turn + 1])

    def gather(type_index, put_rows):
        for turn, got in enumerate((y0_ref, y1_ref)):
            put_rows(sorted_ref.at[2 * turn + type_index], (2 * turn) ^ (dp & 3))
            put_rows(got, (2 * turn + 1) ^ (dp & 3))

    def grams(*pair):
        for index, (values, product) in enumerate(pair):
            gram_triangle(pack_ref, values, product)
            half = pack_ref.shape[0] // 2
            slot = index ^ across
            near_ref[slot] = pack_ref[pl.ds(pl.multiple_of(core * half, 8), half), :]
            far_ref[slot] = pack_ref[pl.ds(pl.multiple_of((1 - core) * half, 8), half), :]

    @pl.when(side == 0)
    def _():
        def up_out(ref, low):
            put(all_ref, clip, ((ref, 0), (ref, slices)), low, slices, 0)
            all_ref[pl.ds(pl.multiple_of(units + low * 32, 8), 32), :] = clip * ref[
                2 * slices : 2 * slices + 32, :
            ].astype(F32)

        gather(0, up_out)
        up = MUON_MOMENTUM * mu_ref[...] + jnp.transpose(all_ref[0:units, :])
        out = MUON_MOMENTUM * mo_ref[...] + all_ref[units : units + mo_ref.shape[0], :]
        grams((up, nt), (out, tn))

    @pl.when(side == 1)
    def _():
        def down_qkv(ref, low):
            put(all_ref, clip, ((ref, 0), (ref, slices)), low, slices, 0)
            put(all_ref, clip, ((ref, 2 * slices), (ref, 2 * slices + wide // 8)), low, wide // 8, units)

        gather(1, down_qkv)
        qkv = MUON_MOMENTUM * mq_ref[...] + jnp.transpose(heads_apart(all_ref[units : units + wide, :], True))
        down = MUON_MOMENTUM * md_ref[...] + all_ref[0:units, :]
        grams((qkv, nt), (down, tn))


def momentum_kernel(
    where_ref, square_ref, q0_ref, r0_ref, q1_ref, r1_ref, y0_ref, y1_ref, rest0_ref, rest1_ref,
    mq_ref, mo_ref, mu_ref, md_ref,
    emb_ref, emb_m_ref, emb_v_ref, head_ref, head_m_ref, head_v_ref, gain_ref, gain_m_ref, gain_v_ref,
    norm_ref, mq_out, mo_out, mu_out, md_out, mq_near, mo_near, mu_near, md_near,
    emb_m_out, emb_v_out, emb_out, head_m_out, head_v_out, head_out, gain_m_out, gain_v_out, gain_out,
    all_ref, rows_ref, sorted_ref, got_ref,
):
    dp, side = where_ref[GROUP], where_ref[SIDE]
    norm = jnp.sqrt(square_ref[...])
    norm_ref[...] = norm
    clip = jnp.max(CLIP_NORM / jnp.maximum(norm, CLIP_NORM))
    units, wide, out_rows = mu_ref.shape[1], mq_ref.shape[1], mo_ref.shape[0]
    slices = units // 8
    main = y0_ref.shape[0]
    qkv_at, out_at = 2 * units + out_rows, 2 * units

    def place(up_ref, down_ref, small, low):
        put(all_ref, clip, ((up_ref, 0), (up_ref, slices)), low, slices, 0)
        put(all_ref, clip, ((down_ref, 0), (down_ref, slices)), low, slices, units)
        put(all_ref, clip, ((down_ref, 2 * slices), (down_ref, 2 * slices + wide // 8)), low, wide // 8, qkv_at)
        all_ref[pl.ds(pl.multiple_of(out_at + low * 32, 8), 32), :] = clip * up_ref[
            2 * slices : 2 * slices + 32, :
        ].astype(F32)
        for high in range(2):
            to = pl.ds(pl.multiple_of((4 * high + low) * 8, 8), 8)
            rows_ref[to, :] = clip * small.astype(F32)[8 * high : 8 * high + 8]

    for turn, (quarter, rows, first, rest) in enumerate(
        ((q0_ref, r0_ref, y0_ref, rest0_ref), (q1_ref, r1_ref, y1_ref, rest1_ref))
    ):
        small = sort_rows(quarter, rows, sorted_ref.at[0], sorted_ref.at[1])
        place(sorted_ref.at[0], sorted_ref.at[1], small, (2 * turn) ^ (dp & 3))
        got_ref[side] = first[...]
        got_ref[1 - side] = rest[0:main, :]
        place(got_ref.at[0], got_ref.at[1], rest[main:, :], (2 * turn + 1) ^ (dp & 3))
    mu_out[...] = MUON_MOMENTUM * mu_ref[...] + jnp.transpose(all_ref[0:units, :])
    md_out[...] = MUON_MOMENTUM * md_ref[...] + all_ref[units : 2 * units, :]
    mo_out[...] = MUON_MOMENTUM * mo_ref[...] + all_ref[out_at:qkv_at, :]
    mq_out[...] = MUON_MOMENTUM * mq_ref[...] + jnp.transpose(heads_apart(all_ref[qkv_at:, :], True))
    for near, out in ((mq_near, mq_out), (mo_near, mo_out), (mu_near, mu_out), (md_near, md_out)):
        near[...] = out[...]
    vocab = emb_ref.shape[0]
    head_m_out[...], head_v_out[...], head_out[...] = adam_step(
        head_ref[...], rows_ref[0:vocab, :], head_m_ref[...], head_v_ref[...], HEAD_RATE, WEIGHT_DECAY
    )
    emb_m_out[...], emb_v_out[...], emb_out[...] = adam_step(
        emb_ref[...], rows_ref[vocab : 2 * vocab, :], emb_m_ref[...], emb_v_ref[...], EMBED_RATE, WEIGHT_DECAY
    )
    gain_m_out[...], gain_v_out[...], gain_out[...] = adam_step(
        gain_ref[...], rows_ref[2 * vocab : 2 * vocab + 3, :], gain_m_ref[...], gain_v_ref[...], GAIN_RATE, 0.0
    )


def rows_kernel(where_ref, out_ref, out_got_ref, grad_ref, grad_got_ref, block_ref, input_ref):
    row = where_ref[ROW]
    size = out_got_ref.shape[0]
    block_ref[row] = out_ref[0:size, :]
    block_ref[1 - row] = out_got_ref[...]
    input_ref[row] = grad_ref[0:size, :]
    input_ref[1 - row] = grad_got_ref[...].astype(F32)


def squares_kernel(quarter_ref, quarter_z_ref, rows_ref, rows_z_ref, out_ref):
    wide = 3 * PAIR // 8
    total = 0.0
    for ref in (quarter_ref, quarter_z_ref):
        values = ref[...].astype(F32)
        total = total + jnp.sum(values * values)
    for ref in (rows_ref, rows_z_ref):
        for at in range(ref.shape[0]):
            values = ref[at].astype(F32)
            total = total + jnp.sum(values[0:wide] * values[0:wide]) + 0.25 * jnp.sum(values[wide:] * values[wide:])
    out_ref[...] = jnp.full(out_ref.shape, total, F32)


def three(left, right):
    left_high, left_low = halves(left)
    right_high, right_low = halves(right)
    return nn(
        jnp.concatenate([left_high, left_high, left_low], axis=1),
        jnp.concatenate([right_high, right_low, right_high], axis=0),
    )


def once(left, right):
    return nn(left.astype(BF16), right.astype(BF16))


def schulz_kernel(where_ref, mine_ref, other_ref, near_ref, far_ref, pack_ref, poly_ref, gram_ref, tri_ref):
    half, block = mine_ref.shape
    size = 2 * block
    core = where_ref[CORE]
    pack_ref[pl.ds(pl.multiple_of(core * half, 8), half), :] = mine_ref[...]
    pack_ref[pl.ds(pl.multiple_of((1 - core) * half, 8), half), :] = other_ref[...]
    gram_ref[0:block, 0:block] = pack_ref[0:block, :]
    corner = pack_ref[block:size, :]
    gram_ref[0:block, block:] = corner
    gram_ref[block:, 0:block] = jnp.transpose(corner)
    gram_ref[block:, block:] = pack_ref[size:, :]
    gram = gram_ref[...]
    rows = lax.broadcasted_iota(jnp.int32, gram.shape, 0)
    columns = lax.broadcasted_iota(jnp.int32, gram.shape, 1)
    diagonal = rows == columns
    trace = jnp.sum(jnp.where(diagonal, gram, 0.0))
    inverse = 1.0 / (jnp.sqrt(jnp.full((1, size), trace, F32)) + 1e-07)
    gram = gram * (inverse * inverse)

    def sweep(gram, poly, times, last=False):
        change = SCHULZ_SQUARE * gram + SCHULZ_CUBE * times(gram, gram)
        if poly is None:
            poly_ref[...] = change * inverse + jnp.where(diagonal, SCHULZ_LINEAR * inverse, 0.0)
        else:
            poly_ref[...] = SCHULZ_LINEAR * poly + times(change, poly)
        if not last:
            moved = SCHULZ_LINEAR * gram + times(change, gram)
            gram_ref[...] = SCHULZ_LINEAR * moved + times(moved, change)

    sweep(gram, None, once)
    sweep(gram_ref[...], poly_ref[...], once)
    sweep(gram_ref[...], poly_ref[...], once)
    for index in range(3, NS_STEPS):
        sweep(gram_ref[...], poly_ref[...], three, index == NS_STEPS - 1)
    poly = poly_ref[...]
    spine = jnp.sum(jnp.where(diagonal, poly, 0.0), axis=0, keepdims=True)
    off = jnp.where(diagonal, 0.0, poly).astype(BF16)
    high = spine.astype(BF16).astype(F32)
    low = spine - high
    rest = jnp.zeros((14, block), F32)
    tops = [
        jnp.concatenate([high[:, at], low[:, at], rest], axis=0).astype(BF16)
        for at in (slice(0, block), slice(block, size))
    ]
    part = half - block
    tri_ref[0, 0:block, :] = off[0:block, 0:block]
    tri_ref[0, block:half, :] = off[0:part, block:]
    tri_ref[0, half:, :] = tops[0]
    tri_ref[1, 0 : block - part, :] = off[part:block, block:]
    tri_ref[1, block - part : half, :] = off[block:, block:]
    tri_ref[1, half:, :] = tops[1]
    near_ref[...] = tri_ref[core]
    far_ref[...] = tri_ref[1 - core]


def muon_kernel(
    where_ref, mq_ref, mo_ref, mu_ref, md_ref, near0, near1, near2, near3, far0, far1, far2, far3,
    wq_ref, wo_ref, wu_ref, wd_ref, wq_out, wo_out, wu_out, wd_out, tri_ref,
):
    across, core, side = where_ref[ROW], where_ref[CORE], where_ref[SIDE]
    held = 2 * side + across
    for at, (near, far) in enumerate(((near0, far0), (near1, far1), (near2, far2), (near3, far3))):
        tri_ref[at, core] = near[...]
        tri_ref[at, 1 - core] = far[...]
    block = near0.shape[1]
    half = near0.shape[0] - 16
    part = half - block

    def ortho(matrix, values, left):
        slot = matrix ^ held
        first = tri_ref[slot, 0]
        second = tri_ref[slot, 1]
        corner = jnp.concatenate([first[block:half], second[0 : block - part]], axis=0)
        upper = jnp.concatenate([first[0:block], corner], axis=1)
        lower = jnp.concatenate([jnp.transpose(corner), second[block - part : half]], axis=1)
        poly = jnp.concatenate([upper, lower], axis=0)
        spines = [tri[half:].astype(F32) for tri in (first, second)]
        spine = jnp.concatenate([s[0:1] + s[1:2] for s in spines], axis=1)
        if left:
            spine = jnp.transpose(jnp.broadcast_to(spine, (8, 2 * block)))[:, 0:1]
            return nn(poly, values.astype(BF16)) + values * spine
        return nn(values.astype(BF16), poly) + values * spine

    def moved(weight, ortho, longest):
        return weight * (1.0 - MUON_RATE * MUON_DECAY) - MUON_RATE * 0.2 * math.sqrt(longest) * ortho

    wu_out[...] = moved(wu_ref[...], ortho(0, mu_ref[...], True), max(D, FF))
    wo_out[...] = moved(wo_ref[...], ortho(1, mo_ref[...], False), D)
    wq_out[...] = moved(wq_ref[...], ortho(2, mq_ref[...], True), 3 * D)
    wd_out[...] = moved(wd_ref[...], ortho(3, md_ref[...], False), max(D, FF))


VMEM = pl.BlockSpec(memory_space=pltpu.VMEM)
SMEM = pl.BlockSpec(memory_space=pltpu.SMEM)
VMEM_LIMIT = 14 * 1024 * 1024


def call(body, name, ins, outs, scratch=(), scalars=0, plain=(), far=(), micros=1):
    shapes = [
        (pltpu.HBM if at in far else pltpu.VMEM)(shape, dtype)
        for at, (shape, dtype) in enumerate(outs)
    ]
    held = [
        value if at < scalars else pltpu.with_memory_space_constraint(value, pltpu.HBM if at in plain else pltpu.VMEM)
        for at, value in enumerate(ins)
    ]
    return pl.pallas_call(
        body,
        name=name,
        out_shape=shapes,
        in_specs=[SMEM] * scalars + [VMEM] * (len(ins) - scalars),
        out_specs=[VMEM] * len(shapes),
        scratch_shapes=list(scratch),
        compiler_params=pltpu.CompilerParams(vmem_limit_bytes=VMEM_LIMIT),
        cost_estimate=pl.CostEstimate(flops=micros * 10**8, bytes_accessed=0, transcendentals=0),
    )(*held)


def swap(values, bit):
    return lax.ppermute(values, "tensor", [(i, i ^ bit) for i in range(4)])


def swap_dp(values, bit):
    return lax.ppermute(values, "dp", [(i, i ^ bit) for i in range(lax.axis_size("dp"))])


def swap_both(values, bit, dp_bit):
    width = lax.axis_size("tensor")
    pairs = [
        (p * width + t, (p ^ dp_bit) * width + (t ^ bit)) for p in range(lax.axis_size("dp")) for t in range(width)
    ]
    return lax.ppermute(values, ("dp", "tensor"), pairs)


def add(left, right):
    return (left.astype(F32) + right.astype(F32)).astype(BF16)


def join(*parts):
    return jnp.concatenate(parts, axis=-2)


def after(values, done):
    return lax.optimization_barrier((values, done))[0]


def over_rest(piece):
    bit = 8
    while bit < lax.axis_size("dp"):
        piece = add(piece, swap_dp(piece, bit))
        bit *= 2
    return piece


def on_device(
    noised, targets, timesteps, segments, embedding, out_head, norm_gains,
    w_qkv, w_out, w_up, w_down, mom_qkv, mom_out, mom_up, mom_down,
    embed_m, embed_v, head_m, head_v, gains_m, gains_v,
):
    place = lax.axis_index("tensor")
    group = lax.axis_index("dp") & 7
    row = place // 2
    core = place % 2
    size = noised.shape[1]
    length = segments.shape[1]
    own = 2 * size
    order = jnp.stack([place, place ^ 2, place ^ 1, place ^ 3])

    ids = jnp.stack([noised, targets])
    mine = lax.dynamic_index_in_dim(ids, row, 1, keepdims=False)
    send_ids = lax.dynamic_index_in_dim(ids, 1 - row, 1, keepdims=False)
    got = swap(send_ids, 2)
    own_ids = jnp.stack([mine, got], axis=1)
    tok = jnp.concatenate([own_ids[0], swap(own_ids[0], 1)], axis=0)
    seg_row = lax.dynamic_index_in_dim(segments, row, 0, keepdims=False)
    span_ids = jnp.arange(timesteps.shape[1], dtype=jnp.int32)
    starts = jnp.sum((seg_row[None, :] < span_ids[:, None]).astype(jnp.int32), axis=1)
    times = lax.dynamic_index_in_dim(timesteps, row, 0, keepdims=False)
    stand = jnp.stack([group, row, core, group & 1])
    where = jnp.concatenate([row * 4 + order, order, times, starts, stand]).astype(jnp.int32)
    table = jnp.asarray(position_table(max(length, 1000), D))

    unit_rows = w_up.shape[1]
    out_rows = w_out.shape[0]
    side = (group & 1).reshape(1).astype(jnp.int32)
    pack_rows = 3 * PAIR + out_rows
    wa_mine, wa_part = call(
        attention_weights_kernel, "attention_weights", [side, after(w_qkv, send_ids), w_out],
        [((pack_rows, D), BF16), ((pack_rows // 2, D), BF16)], scalars=1, plain=(1, 2),
    )
    (wb_mine,) = call(
        ffn_weights_kernel, "ffn_weights", [after(w_up, wa_part), w_down], [((2 * unit_rows, D), BF16)], plain=(0, 1)
    )
    wa_part = swap(wa_part, 2)

    hidden0, a1, aug = call(
        embed_kernel, "embed",
        [where, tok, segments.reshape(-1, size), table, embedding, norm_gains],
        [((own, D), F32), ((length, D), BF16), ((length, PAIR), BF16)],
        [pltpu.VMEM((VOCAB_PAD + SPAN_PAD, 2 * D), F32)],
        scalars=1, plain=(2, 3, 4, 5), micros=4,
    )

    def attend(first, second):
        return call(
            attend_kernel, "attend", [a1, aug, first, second],
            [((2, length, 3 * PAIR), BF16), ((2 * PAIR, own), F32), ((4, length, own), BF16), ((8, own), F32)],
            micros=5,
        )

    wb_across = swap(wb_mine, 2)
    wa = [wa_mine, swap(wa_mine, 1)]
    qkv_a, ctx_a, weights_a, inverse_a = attend(*wa)
    wa_part = after(wa_part, a1)
    (wa_across,) = call(
        join_kernel, "join", [where, wa_part, after(swap_dp(wa_part, 1), ctx_a)], [((2, pack_rows // 2, D), BF16)], scalars=1
    )
    wa_across = wa_across.reshape(pack_rows, D)
    wa += [wa_across, swap(wa_across, 1)]
    qkv_b, ctx_b, weights_b, inverse_b = attend(*wa[2:])
    wb = [wb_mine, swap(wb_mine, 1)]
    half_chunks = FF // CHUNK // 2
    hidden1, partial2, a2, act_a, slope_a = call(
        ffn_up_kernel, "ffn_up", [ctx_a, ctx_b, hidden0, norm_gains, *wa, *wb],
        [((own, D), F32), ((own, D), F32), ((own, D), BF16)] + [((half_chunks, own, CHUNK), BF16)] * 2,
        plain=(3,), micros=7,
    )
    wb_across = after(wb_across, a2)
    wb += [wb_across, swap(wb_across, 1)]
    slices = unit_rows // 4
    units = ((2, own, CHUNK), BF16)
    partial2, act_b, slope_b = call(
        ffn_next_kernel, "ffn_next", [partial2, a2, wb[2]], [((own, D), F32), units, units], micros=3
    )
    chunk = ((own, CHUNK), BF16)
    hidden2, d_h2, d_ffn, d_a2, act_c, slope_c, keep_a, send_a, part = call(
        ffn_kernel, "ffn",
        [where, partial2, a2, out_head.T, norm_gains, own_ids[1], act_a, slope_a, act_b, slope_b, *wb],
        [((own, D), BF16), ((own, D), F32), ((own, D), BF16), ((own, D), F32), chunk, chunk]
        + [((8, slices, D), BF16)] * 2 + [((VOCAB_PAD + 8, D), F32)],
        [pltpu.VMEM((2, own, CHUNK), BF16), pltpu.VMEM((2, own, CHUNK), BF16), pltpu.VMEM((VOCAB_PAD, D), F32)],
        scalars=1, plain=(3, 4), far=(0,), micros=10,
    )
    got_a = swap(send_a, 1)
    d_a2, keep_b, send_b = call(
        ffn_end_kernel, "ffn_end",
        [where, d_ffn, d_a2, a2, act_a, slope_a, act_b, slope_b, act_c, slope_c, *wb],
        [((own, D), F32)] + [((8, slices, D), BF16)] * 2, scalars=1, micros=3,
    )
    got_b = swap(send_b, 1)
    keep_x, send_x = add(keep_a[0:4], got_a[0:4]), add(keep_a[4:8], after(got_a, d_a2)[4:8])
    got_x = swap(send_x, 2)
    d_a2 = after(d_a2, send_x)
    d_h1, d_attn, keep_o, send_o, gain1 = call(
        ffn_norm_kernel, "ffn_norm", [where, ctx_a, ctx_b, hidden1, d_h2, d_a2, norm_gains],
        [((own, D), F32), ((own, D), BF16)] + [((8, out_rows // 4, D), BF16)] * 2 + [((8, D), F32)],
        scalars=1, plain=(6,), micros=3,
    )
    got_o = swap(send_o, 1)

    def back(qkv, weights, ctx, inverse, d_attn, packs):
        return call(
            attend_back_kernel, "attend_back", [qkv, weights, ctx, inverse, d_attn, *packs],
            [((2, own, PAIR), BF16), ((2, own, 2 * PAIR), BF16), ((2, own, 2 * PAIR), BF16)], micros=5,
        )

    keep_y, send_y = add(keep_b[0:4], got_b[0:4]), add(keep_b[4:8], got_b[4:8])
    got_y = swap_dp(send_y, 1)
    got_o = after(got_o, send_y)
    keep_o, send_o = add(keep_o[0:4], got_o[0:4]), add(keep_o[4:8], got_o[4:8])
    got_o = swap(send_o, 2)
    d_attn = after(d_attn, (send_x, send_y, send_o))
    dq_b, near_b, far_b = back(qkv_b, weights_b, ctx_b, inverse_b, d_attn, wa[2:])
    far_b = swap(far_b, 1)
    dq_a, near_a, far_a = back(qkv_a, weights_a, ctx_a, inverse_a, after(d_attn, dq_b), wa[:2])
    far_a = swap(far_a, 1)
    got_x, got_y, got_o, dq_b = lax.optimization_barrier((got_x, got_y, got_o, dq_b))
    half_a = join(add(keep_x, got_x), add(keep_o, got_o))
    half_b = add(keep_y, got_y)
    near_b = after(near_b, (half_a, half_b))
    grads = [((own, D), F32), ((8, 48, D), BF16), ((8, 48, D), BF16)]
    d_a1, keep2_b, send2_b = call(
        input_far_kernel, "input_far", [where, dq_b, near_b, far_b, a1, *wa[2:]], grads, scalars=1, micros=4
    )
    got2_b = swap(send2_b, 1)
    got_y, got_x = swap_dp(half_a[2:4], 1), swap(half_b[2:4], 2)
    igrad, keep2, send2, small = call(
        input_kernel, "input_grad",
        [where, dq_a, near_a, far_a, a1, *wa[:2], d_a1, hidden0, d_h1, norm_gains, tok, part, gain1],
        grads + [((8, 8, D), F32)], [pltpu.VMEM((64, D), F32)], scalars=1, plain=(10,), micros=5,
    )
    got_x, got_y, hidden2 = lax.optimization_barrier((got_x, got_y, hidden2))
    got2 = swap(send2, 1)
    small = small.astype(BF16)
    got_small = swap(small, 1)
    half_a, half_b = add(half_a[0:2], got_y), add(half_b[0:2], got_x)
    send_z = join(half_a[1], half_b[1])
    got_z = swap_dp(send_z, 2)
    near2, far2 = (values.reshape(2, 4, 48, D) for values in (add(keep2, got2), add(keep2_b, after(got2_b, send_z))))
    small = add(small, got_small).reshape(2, 4, 8, D)

    got2_y = swap_dp(join(near2[1], small[1], far2[1]), 1)
    quarter = add(join(half_a[0], half_b[0]), got_z)
    out_got = swap(after(hidden2, igrad)[size:], 2)
    rows = add(join(near2[0], small[0], far2[0]), after(got2_y, (out_got, quarter)))
    wide = near2.shape[-2]
    got2_x = swap(join(rows[:, wide + 8 :], rows[:, wide : wide + 8]), 2)
    igrad_got = swap(after(igrad, got2_x)[size:].astype(BF16), 2)
    rows = add(rows[:, 0 : wide + 8], got2_x)
    rows = add(rows[0:2], swap_dp(rows[2:4], 2))
    pairs = [[i, i ^ 4] for i in range(lax.axis_size("dp")) if not i & 4]
    both = lax.all_to_all(jnp.stack([quarter, quarter]), "dp", 0, 0, axis_index_groups=pairs, tiled=True)
    quarter = over_rest(add(both[0], both[1]))
    rows = after(rows, (quarter, igrad_got))
    rows = over_rest(add(rows, swap_dp(rows, 4)))
    quarter_z, rows_z = swap_dp(quarter, 2), swap_dp(rows, 2)
    main = 2 * slices // 2 + 3 * PAIR // 4

    def choose(quarter, rows):
        return call(
            choose_kernel, "choose", [where, quarter, rows], [((main, D), BF16), ((main + 16, D), BF16)],
            [pltpu.VMEM((2, main, D), BF16)], scalars=1,
        )

    first0, rest0 = choose(quarter, rows)
    first0 = swap_dp(first0, 1)
    first1, rest1 = choose(quarter_z, rows_z)
    first1 = swap_dp(first1, 1)
    (square,) = call(squares_kernel, "squares", [quarter, quarter_z, rows, rows_z], [((8, 128), F32)])
    square = square + swap(square, 1)
    square = (square + swap(square, 2)) + (swap_dp(square, 1) + swap_both(square, 2, 1))
    rest0, rest1 = (swap_dp(rest, 1) for rest in after((rest0, rest1), square))

    def like(*arrays):
        return [(a.shape, F32) for a in arrays]

    heads = [out_head.T, head_m.T, head_v.T]
    triangle = ((2, 3 * D // 4, D // 2), F32)
    sums = [where, square, quarter, rows, quarter_z, rows_z, first0, first1]
    moments = [mom_qkv, mom_out, mom_up, mom_down]
    sorted_rows = pltpu.VMEM((4, main, D), BF16)
    near, far = call(
        gram_kernel, "gram", sums + moments, [triangle, triangle],
        [pltpu.VMEM((2 * unit_rows, D), F32), pltpu.VMEM((3 * D // 2, D // 2), F32), sorted_rows], scalars=1, micros=3,
    )
    far = swap(far, 1)
    half = after(near[0] + far[0], rest0) + swap(near[1] + far[1], 2)
    poly = [((16 + 3 * D // 4, D // 2), BF16)] * 2
    near, far = call(
        schulz_kernel, "schulz", [where, half, swap(half, 1)], poly,
        [pltpu.VMEM((3 * D // 2, D // 2), F32), pltpu.VMEM((D, D), F32), pltpu.VMEM((D, D), F32),
         pltpu.VMEM((2, 16 + 3 * D // 4, D // 2), BF16)],
        scalars=1, micros=10,
    )
    near, far = after((near, far), rest1)
    block_out, input_grad = call(
        rows_kernel, "rows", [where, hidden2, after(out_got, near), igrad, igrad_got],
        [((2, size, D), BF16), ((2, size, D), F32)], scalars=1, plain=(1, 3), far=(0, 1),
    )
    outs = call(
        momentum_kernel, "momentum",
        [where, after(square, near)] + sums[2:] + [rest0, rest1] + moments
        + [embedding, embed_m, embed_v, *heads, norm_gains, gains_m, gains_v],
        [((8, 128), F32)] + like(*moments, *moments, embed_m, embed_v, embedding)
        + like(*heads, gains_m, gains_v, norm_gains),
        [
            pltpu.VMEM((2 * unit_rows + out_rows + 3 * PAIR, D), F32), pltpu.VMEM((64, D), F32),
            pltpu.VMEM((2, main, D), BF16), pltpu.VMEM((2, main, D), BF16),
        ],
        scalars=1, plain=range(14, 23), far=[*range(5), *range(9, 18)], micros=5,
    )
    norm = outs[0]
    mom_qkv_new, mom_out_new, mom_up_new, mom_down_new = outs[1:5]
    moms = outs[5:9]
    embed_new, head_new, gains_new = outs[9:12], [h.T for h in outs[12:15]], outs[15:18]
    grad_norm = norm[0, 0]
    near_x, near_y = swap(near, 2), swap_dp(near, 1)
    nears = [near, *after((near_x, near_y, swap_both(near, 2, 1)), (moms, grad_norm, block_out, input_grad))]
    fars = [far] + [swap(values, 1) for values in nears[1:]]
    qkv_new, out_new, up_new, down_new = call(
        muon_kernel, "muon",
        [where, *moms, *nears, *fars, w_qkv, w_out, w_up, w_down],
        like(w_qkv, w_out, w_up, w_down),
        [pltpu.VMEM((4, 2, 16 + 3 * D // 4, D // 2), BF16)],
        scalars=1, far=range(4), micros=5,
    )
    return (
        block_out, input_grad, grad_norm,
        mom_qkv_new, qkv_new, mom_out_new, out_new, mom_up_new, up_new, mom_down_new, down_new,
        *embed_new, *head_new, *gains_new,
    )


def solution(mesh):
    columns, rows = P(None, "tensor"), P("tensor", None)
    matrices = (columns, rows, columns, rows)
    in_specs = (
        (P("dp", "tensor"), P("dp", "tensor"), P("dp", None), P("dp", None), P(), P(), P())
        + matrices + matrices + (P(),) * 6
    )
    out_specs = (
        (P("dp", "tensor", None), P("dp", "tensor", None), P())
        + (columns, columns, rows, rows, columns, columns, rows, rows) + (P(),) * 9
    )
    return jax.shard_map(on_device, mesh=mesh, in_specs=in_specs, out_specs=out_specs, check_vma=False)
```

```python
import math

import jax
import jax.numpy as jnp
import numpy as np
from jax import lax
from jax.experimental import pallas as pl
from jax.experimental.pallas import tpu as pltpu
from jax.sharding import PartitionSpec as P

D = 512
HEAD_DIM = 64
PAIR = 2 * HEAD_DIM
FF = 2048
NS_STEPS = 5
STEP = 10
CHUNK = 256
VOCAB_PAD = 32
SPAN_PAD = 16
GROUP, ROW, CORE, SIDE = 16, 17, 18, 19

HIGHEST = lax.Precision.HIGHEST
F32 = jnp.float32
BF16 = jnp.bfloat16
NORM_EPS = 1e-05
MASK_FILL = 1e30
MUON_MOMENTUM = 0.5
MUON_RATE = 0.3
MUON_DECAY = 0.1
SCHULZ_LINEAR = 3.4445
SCHULZ_SQUARE = -4.775
SCHULZ_CUBE = 2.0315
ADAM_BETA_ONE = 0.9
ADAM_BETA_TWO = 0.95
ADAM_EPS = 1e-08
EMBED_RATE = 0.3
HEAD_RATE = 0.02
GAIN_RATE = 0.6
WEIGHT_DECAY = 0.1
CLIP_NORM = 1.0


def nn(left, right, precision=None):
    return lax.dot_general(
        left, right, (((1,), (0,)), ((), ())), preferred_element_type=F32, precision=precision
    )


def nt(left, right, precision=None):
    return lax.dot_general(
        left, right, (((1,), (1,)), ((), ())), preferred_element_type=F32, precision=precision
    )


def tn(left, right, precision=None):
    return lax.dot_general(
        left, right, (((0,), (0,)), ((), ())), preferred_element_type=F32, precision=precision
    )


def halves(values):
    high = values.astype(BF16)
    return high, (values - high.astype(F32)).astype(BF16)


def position_table(length, width):
    half = width // 2
    rates = np.exp(-math.log(10000.0) * np.arange(half) / half)
    angles = np.arange(length)[:, None] * rates[None, :]
    return np.concatenate([np.sin(angles), np.cos(angles)], axis=1).astype(np.float32)


def normed_parts(values):
    centered = values - jnp.mean(values, axis=-1, keepdims=True)
    inv_std = lax.rsqrt(jnp.mean(centered * centered, axis=-1, keepdims=True) + NORM_EPS)
    return centered * inv_std, inv_std


def norm_back(grad_out, source, gain):
    normed, inv_std = normed_parts(source)
    scaled = grad_out * gain
    grad_in = inv_std * (
        scaled
        - jnp.mean(scaled, axis=-1, keepdims=True)
        - normed * jnp.mean(scaled * normed, axis=-1, keepdims=True)
    )
    return grad_in, jnp.sum(grad_out * normed, axis=0, keepdims=True)


def embed_kernel(where_ref, tok_ref, seg_ref, table_ref, emb_ref, gains_ref, h0_ref, a1_ref, aug_ref, rows_ref):
    vocab, width = emb_ref.shape
    half = width // 2
    blocks, size = tok_ref.shape
    spans = SPAN_PAD // 4
    rows_ref[...] = jnp.zeros_like(rows_ref)
    rows_ref[0:vocab, 0:width] = emb_ref[...]
    for span in range(spans):
        at_time = table_ref[pl.ds(where_ref[8 + span], 1), :]
        at_start = table_ref[pl.ds(where_ref[12 + span], 1), :]
        row = VOCAB_PAD + span
        rows_ref[row : row + 1, 0:width] = at_time
        rows_ref[row : row + 1, width : width + half] = at_start[:, half:]
        rows_ref[row : row + 1, width + half :] = at_start[:, :half]
    rows = rows_ref[...]
    high = rows.astype(BF16)
    rest = rows - high.astype(F32)
    middle = rest.astype(BF16)
    low = (rest - middle.astype(F32)).astype(BF16)
    stacked = jnp.concatenate([high, middle, low], axis=0)
    gain = gains_ref[0:1, :]
    for block in range(blocks):
        tok = tok_ref[block : block + 1, :]
        seg = seg_ref[pl.ds(where_ref[block], 1), :]
        hot_tok = (lax.broadcasted_iota(jnp.int32, (VOCAB_PAD, size), 0) == tok).astype(F32)
        hot_seg = (lax.broadcasted_iota(jnp.int32, (SPAN_PAD, size), 0) == seg).astype(F32)
        hot = jnp.concatenate([hot_tok, hot_seg], axis=0).astype(BF16)
        picked = tn(jnp.concatenate([hot, hot, hot], axis=0), stacked)
        table = table_ref[pl.ds(pl.multiple_of(where_ref[4 + block] * size, size), size), :]
        sin_p, cos_p = table[:, :half], table[:, half:]
        cos_s, sin_s = picked[:, width : width + half], picked[:, width + half :]
        place = jnp.concatenate([sin_p * cos_s - cos_p * sin_s, cos_p * cos_s + sin_p * sin_s], axis=1)
        hidden = picked[:, :width] + place
        if block * size < h0_ref.shape[0]:
            h0_ref[block * size : (block + 1) * size, :] = hidden
        a1_ref[block * size : (block + 1) * size, :] = (normed_parts(hidden)[0] * gain).astype(BF16)
        wide = (lax.broadcasted_iota(jnp.int32, (PAIR, size), 0) == seg).astype(F32)
        aug_ref[block * size : (block + 1) * size, :] = jnp.transpose(wide).astype(BF16)


def query_side(aug, own):
    return ((aug[:own].astype(F32) - 1.0) * MASK_FILL).astype(BF16)


def half_mask(values, head):
    lanes = lax.broadcasted_iota(jnp.int32, values.shape, 1)
    keep = (lanes >= head * HEAD_DIM) & (lanes < (head + 1) * HEAD_DIM)
    return jnp.where(keep, values.astype(F32), 0.0).astype(BF16)


def query_side(aug, own):
    return ((aug[:own].astype(F32) - 1.0) * MASK_FILL).astype(BF16)


def half_mask(values, head):
    lanes = lax.broadcasted_iota(jnp.int32, values.shape, 1)
    keep = (lanes >= head * HEAD_DIM) & (lanes < (head + 1) * HEAD_DIM)
    return jnp.where(keep, values.astype(F32), 0.0).astype(BF16)


def heads_apart(rows, back):
    count = rows.shape[0] // HEAD_DIM
    heads = count // 3
    if back:
        index = [j * heads + h for h in range(heads) for j in range(3)]
    else:
        index = [h * 3 + j for j in range(3) for h in range(heads)]
    return jnp.concatenate([rows[i * HEAD_DIM : (i + 1) * HEAD_DIM] for i in index], axis=0)


def attention_weights_kernel(side_ref, wq_ref, wo_ref, out_ref, part_ref):
    wide = wq_ref.shape[1]
    out_ref[0:wide, :] = heads_apart(jnp.transpose(wq_ref[...]), False).astype(BF16)
    out_ref[wide:, :] = wo_ref[...].astype(BF16)
    half = part_ref.shape[0]
    part_ref[...] = out_ref[pl.ds(pl.multiple_of(side_ref[0] * half, half), half), :]


def join_kernel(where_ref, mine_ref, got_ref, out_ref):
    side = where_ref[SIDE]
    out_ref[side] = mine_ref[...]
    out_ref[1 - side] = got_ref[...]


def ffn_weights_kernel(wu_ref, wd_ref, out_ref):
    units = wu_ref.shape[1]
    out_ref[0:units, :] = jnp.transpose(wu_ref[...]).astype(BF16)
    out_ref[units:, :] = wd_ref[...].astype(BF16)


def attend_kernel(a1_ref, aug_ref, w0, w1, qkv_ref, ctx_ref, weights_ref, inverse_ref):
    own = ctx_ref.shape[1]
    scale = HEAD_DIM**-0.5
    aug = aug_ref[...]
    aug_q = query_side(aug, own)
    inverse_ref[...] = jnp.zeros_like(inverse_ref)
    for shard, weight in enumerate((w0, w1)):
        qkv = nt(a1_ref[...], weight[0 : 3 * PAIR, :]).astype(BF16)
        qkv_ref[shard] = qkv
        keys = jnp.concatenate([qkv[:, PAIR : 2 * PAIR], aug], axis=1)
        value = qkv[:, 2 * PAIR :]
        query = qkv[:own, :PAIR].astype(F32) * scale
        for head in range(2):
            q_side = jnp.concatenate([half_mask(query, head), aug_q], axis=1)
            scores = nt(keys, q_side)
            top = jnp.max(scores, axis=0, keepdims=True)
            raised = jnp.exp(scores - top)
            inverse = 1.0 / jnp.sum(raised, axis=0, keepdims=True)
            weights = raised.astype(BF16)
            weights_ref[2 * shard + head] = weights
            out = tn(value, weights)
            at = shard * PAIR + head * HEAD_DIM
            ctx_ref[at : at + HEAD_DIM, :] = out[head * HEAD_DIM : (head + 1) * HEAD_DIM] * inverse
            inverse_ref[2 * shard + head : 2 * shard + head + 1, :] = inverse


def low_bits(piece, mine):
    return (piece ^ mine) & 1, lax.shift_right_logical(piece ^ mine, 1) & 1


def gelu_parts(upper):
    size = jnp.abs(upper)
    pdf = jnp.exp(-0.5 * upper * upper) * (1.0 / math.sqrt(2.0 * math.pi))
    turn = 1.0 / (1.0 + 0.2316419 * size)
    series = turn * (
        0.319381530
        + turn * (-0.356563782 + turn * (1.781477937 + turn * (-1.821255978 + turn * 1.330274429)))
    )
    tail = pdf * series
    cdf = jnp.where(upper < 0.0, tail, 1.0 - tail)
    return (upper * cdf).astype(BF16), (cdf + upper * pdf).astype(BF16)


def up_chunks(a2_ref, packs, act_ref, slope_ref, acc_ref, first):
    units = packs[0].shape[0] // 2
    parts = units // CHUNK
    for at, pack in enumerate(packs):
        act, slope = gelu_parts(nt(a2_ref[...], pack[0:units, :]))
        for part in range(parts):
            columns = slice(part * CHUNK, (part + 1) * CHUNK)
            act_ref[first + at * parts + part] = act[:, columns]
            slope_ref[first + at * parts + part] = slope[:, columns]
        acc_ref[...] += nn(act, pack[units:, :])


def ffn_up_kernel(
    ctx_a_ref, ctx_b_ref, h0_ref, gains_ref, wa0, wa1, wa2, wa3, wb0, wb1,
    h1_ref, acc_ref, a2_ref, act_ref, slope_ref,
):
    hidden1 = h0_ref[...]
    for ctx_ref, first, second in ((ctx_a_ref, wa0, wa1), (ctx_b_ref, wa2, wa3)):
        weight = jnp.concatenate([first[3 * PAIR :, :], second[3 * PAIR :, :]], axis=0)
        hidden1 = hidden1 + tn(ctx_ref[...].astype(BF16), weight)
    h1_ref[...] = hidden1
    acc_ref[...] = hidden1
    a2_ref[...] = (normed_parts(hidden1)[0] * gains_ref[1:2, :]).astype(BF16)
    up_chunks(a2_ref, (wb0, wb1), act_ref, slope_ref, acc_ref, 0)


def back_pair(d_ffn, acts, slopes, packs, part, a2_ref, acc_ref):
    units = packs[0].shape[0] // 2
    at = part * CHUNK
    up = jnp.concatenate([pack[at : at + CHUNK, :] for pack in packs], axis=0)
    down = jnp.concatenate([pack[units + at : units + at + CHUNK, :] for pack in packs], axis=0)
    d_up = (nt(d_ffn, down) * jnp.concatenate(slopes, axis=1).astype(F32)).astype(BF16)
    acc_ref[...] += nn(d_up, up)
    return tn(d_up, a2_ref[...]), tn(jnp.concatenate(acts, axis=1), d_ffn)


def ffn_next_kernel(part_ref, a2_ref, pack_ref, acc_ref, act_ref, slope_ref):
    acc_ref[...] = part_ref[...]
    up_chunks(a2_ref, (pack_ref,), act_ref, slope_ref, acc_ref, 0)


def ffn_kernel(
    where_ref, part_ref, a2_ref, head_ref, gains_ref, tgt_ref, act_a_ref, slope_a_ref, act_b_ref, slope_b_ref,
    wb0, wb1, wb2, wb3, out_ref, dh2_ref, dffn_ref, acc_ref, act_c_ref, slope_c_ref, keep_ref, send_ref, small_ref,
    act_ref, slope_ref, pad_ref,
):
    vocab = head_ref.shape[0]
    width = out_ref.shape[1]
    mine = where_ref[GROUP]
    pad_ref[...] = jnp.zeros_like(pad_ref)
    pad_ref[0:vocab, :] = head_ref[...]
    acc_ref[...] = part_ref[...]
    up_chunks(a2_ref, (wb3,), act_ref, slope_ref, acc_ref, 0)
    hidden2 = acc_ref[...]
    out_ref[...] = hidden2.astype(BF16)
    normed3, _ = normed_parts(hidden2)
    a3 = normed3 * gains_ref[2:3, :]
    head = pad_ref[...]
    a3_high, a3_low = halves(a3)
    head_high, head_low = halves(head)
    both = nt(jnp.concatenate([head_high, head_low], axis=0), a3_high)
    logits = both[0:VOCAB_PAD] + both[VOCAB_PAD:] + nt(head_high, a3_low)
    classes = lax.broadcasted_iota(jnp.int32, logits.shape, 0)
    logits = jnp.where(classes < vocab, logits, -MASK_FILL)
    raised = jnp.exp(logits - jnp.max(logits, axis=0, keepdims=True))
    targets = jnp.concatenate([tgt_ref[0:1, :], tgt_ref[1:2, :]], axis=1)
    d_logits = raised / jnp.sum(raised, axis=0, keepdims=True) - (classes == targets).astype(F32)
    d_high, d_low = halves(d_logits)
    both = nn(jnp.concatenate([d_high, d_low], axis=0), a3_high)
    small_ref[0:VOCAB_PAD, :] = both[0:VOCAB_PAD] + both[VOCAB_PAD:] + nn(d_high, a3_low)
    d_a3 = tn(
        jnp.concatenate([d_high, d_low, d_high], axis=0), jnp.concatenate([head_high, head_high, head_low], axis=0)
    )
    d_h2, g_gain2 = norm_back(d_a3, hidden2, gains_ref[2:3, :])
    small_ref[VOCAB_PAD:, :] = jnp.concatenate([g_gain2, jnp.zeros((7, width), F32)], axis=0)
    dh2_ref[...] = d_h2
    d_ffn = d_h2.astype(BF16)
    dffn_ref[...] = d_ffn
    acc_ref[...] = jnp.zeros_like(acc_ref)
    rows = CHUNK // 4
    near = ([act_a_ref[0], act_a_ref[2]], [slope_a_ref[0], slope_a_ref[2]], (wb0, wb1))
    far = ([act_b_ref[0], act_ref[0]], [slope_b_ref[0], slope_ref[0]], (wb2, wb3))
    for across, (acts, slopes, packs) in enumerate((near, far)):
        g_up, g_down = back_pair(d_ffn, acts, slopes, packs, 0, a2_ref, acc_ref)
        for core, target in enumerate((keep_ref, send_ref)):
            for piece in range(4):
                b0, b1 = low_bits(piece, mine)
                at = core * CHUNK + piece * rows
                target[4 * across + 2 * b0 + b1, 0:rows, :] = g_up[at : at + rows].astype(BF16)
                target[4 * across + 2 * b0 + b1, rows:, :] = g_down[at : at + rows].astype(BF16)
    act_c_ref[...] = act_ref[1]
    slope_c_ref[...] = slope_ref[1]


def ffn_end_kernel(
    where_ref, dffn_ref, part_ref, a2_ref, act_a_ref, slope_a_ref, act_b_ref, slope_b_ref, act_c_ref, slope_c_ref,
    wb0, wb1, wb2, wb3, acc_ref, keep_ref, send_ref,
):
    mine = where_ref[GROUP]
    d_ffn = dffn_ref[...]
    acc_ref[...] = part_ref[...]
    rows = CHUNK // 4
    near = ([act_a_ref[1], act_a_ref[3]], [slope_a_ref[1], slope_a_ref[3]], (wb0, wb1))
    far = ([act_b_ref[1], act_c_ref[...]], [slope_b_ref[1], slope_c_ref[...]], (wb2, wb3))
    for across, (acts, slopes, packs) in enumerate((near, far)):
        g_up, g_down = back_pair(d_ffn, acts, slopes, packs, 1, a2_ref, acc_ref)
        for core, target in enumerate((keep_ref, send_ref)):
            for piece in range(4):
                b0, b1 = low_bits(piece, mine)
                at = core * CHUNK + piece * rows
                target[4 * b0 + 2 * across + b1, 0:rows, :] = g_up[at : at + rows].astype(BF16)
                target[4 * b0 + 2 * across + b1, rows:, :] = g_down[at : at + rows].astype(BF16)


def ffn_norm_kernel(
    where_ref, ctx_a_ref, ctx_b_ref, h1_ref, dh2_ref, part_ref, gains_ref,
    dh1_ref, dattn_ref, keep_ref, send_ref, gain_ref,
):
    mine = where_ref[GROUP]
    d_h1_part, g_gain1 = norm_back(part_ref[...], h1_ref[...], gains_ref[1:2, :])
    d_h1 = dh2_ref[...] + d_h1_part
    dh1_ref[...] = d_h1
    d_attn = d_h1.astype(BF16)
    dattn_ref[...] = d_attn
    gain_ref[...] = jnp.broadcast_to(g_gain1, gain_ref.shape)
    out_rows = ctx_a_ref.shape[0] // 2
    for across, ctx_ref in enumerate((ctx_a_ref, ctx_b_ref)):
        g_out = nn(ctx_ref[...].astype(BF16), d_attn)
        for core in range(2):
            target = send_ref if core else keep_ref
            for piece in range(4):
                b0, b1 = low_bits(piece, mine)
                at = core * out_rows + piece * (out_rows // 4)
                target[4 * across + 2 * b0 + b1] = g_out[at : at + out_rows // 4].astype(BF16)


def attend_back_kernel(qkv_ref, weights_ref, ctx_ref, inverse_ref, dattn_ref, w0, w1, dq_ref, near_ref, far_ref):
    own = ctx_ref.shape[1]
    scale = HEAD_DIM**-0.5
    d_attn = dattn_ref[...]
    columns = jnp.transpose(inverse_ref[...])
    for shard, weight_ref in enumerate((w0, w1)):
        weight = weight_ref[3 * PAIR :, :]
        d_ctx = nt(d_attn, weight).astype(BF16).astype(F32)
        d_ctx_t = nt(weight, d_attn).astype(BF16).astype(F32)
        inner = d_ctx_t * ctx_ref[shard * PAIR : (shard + 1) * PAIR, :]
        key = qkv_ref[shard, :, PAIR : 2 * PAIR]
        value = qkv_ref[shard, :, 2 * PAIR :]
        query = qkv_ref[shard, 0:own, 0:PAIR].astype(F32) * scale
        dq_parts = []
        d_key = None
        d_value = None
        for head in range(2):
            mine = slice(head * HEAD_DIM, (head + 1) * HEAD_DIM)
            at = 2 * shard + head
            q_head = half_mask(query, head)
            d_ctx_head = half_mask(d_ctx * columns[:, at : at + 1], head)
            delta = jnp.sum(inner[mine], axis=0, keepdims=True) * inverse_ref[at : at + 1, :]
            weights = weights_ref[at]
            d_scores = (weights.astype(F32) * (nt(value, d_ctx_head) - delta)).astype(BF16)
            d_value_part = nn(weights, d_ctx_head)
            d_key_part = nn(d_scores, q_head)
            dq_parts.append(tn(key, d_scores)[mine])
            d_key = d_key_part if d_key is None else d_key + d_key_part
            d_value = d_value_part if d_value is None else d_value + d_value_part
        dq_ref[shard] = jnp.transpose(jnp.concatenate(dq_parts, axis=0) * scale).astype(BF16)
        near_ref[shard, :, 0:PAIR] = d_key[:own].astype(BF16)
        near_ref[shard, :, PAIR:] = d_value[:own].astype(BF16)
        far_ref[shard ^ 1, :, 0:PAIR] = d_key[own:].astype(BF16)
        far_ref[shard ^ 1, :, PAIR:] = d_value[own:].astype(BF16)


def qkv_grads(where_ref, dq_ref, near_ref, far_ref, a1, weights, keep_ref, send_ref, total):
    for shard, weight in enumerate(weights):
        d_kv = (near_ref[shard].astype(F32) + far_ref[shard].astype(F32)).astype(BF16)
        d_qkv = jnp.concatenate([dq_ref[shard], d_kv], axis=1)
        grad = tn(d_qkv, a1)
        target = send_ref if shard else keep_ref
        rows = grad.shape[0] // 8
        for piece in range(8):
            b0, b1 = low_bits(piece, where_ref[GROUP])
            target[4 * b0 + 2 * b1 + piece // 4] = grad[piece * rows : (piece + 1) * rows].astype(BF16)
        part = nn(d_qkv, weight[0 : 3 * PAIR, :])
        total = part if total is None else total + part
    return total


def input_far_kernel(where_ref, dq_ref, near_ref, far_ref, a1_ref, w0, w1, total_ref, keep_ref, send_ref):
    own = total_ref.shape[0]
    total_ref[...] = qkv_grads(where_ref, dq_ref, near_ref, far_ref, a1_ref[0:own, :], (w0, w1), keep_ref, send_ref, None)


def input_kernel(
    where_ref, dq_ref, near_ref, far_ref, a1_ref, w0, w1, total_ref, h0_ref, dh1_ref, gains_ref, tok_ref, part_ref, gain1_ref,
    igrad_ref, keep_ref, send_ref, small_ref, rows_ref,
):
    own, width = h0_ref.shape
    vocab = 27
    d_a1 = qkv_grads(
        where_ref, dq_ref, near_ref, far_ref, a1_ref[0:own, :], (w0, w1), keep_ref, send_ref, total_ref[...]
    )
    d_h0_part, g_gain0 = norm_back(d_a1, h0_ref[...], gains_ref[0:1, :])
    d_h0 = dh1_ref[...] + d_h0_part
    igrad_ref[...] = d_h0
    high, low = halves(d_h0)
    tok = jnp.concatenate([tok_ref[0:1, :], tok_ref[1:2, :]], axis=1)
    hot = (lax.broadcasted_iota(jnp.int32, (VOCAB_PAD, own), 0) == tok).astype(F32).astype(BF16)
    rows_ref[...] = jnp.zeros_like(rows_ref)
    rows_ref[0:vocab, :] = part_ref[0:vocab, :]
    rows_ref[vocab : 2 * vocab, :] = (nn(hot, high) + nn(hot, low))[0:vocab]
    rows_ref[2 * vocab : 2 * vocab + 1, :] = g_gain0
    rows_ref[2 * vocab + 1 : 2 * vocab + 2, :] = gain1_ref[0:1, :]
    rows_ref[2 * vocab + 2 : 2 * vocab + 3, :] = part_ref[VOCAB_PAD : VOCAB_PAD + 1, :]
    for piece in range(8):
        b0, b1 = low_bits(piece, where_ref[GROUP])
        small_ref[4 * b0 + 2 * b1 + piece // 4] = rows_ref[piece * 8 : (piece + 1) * 8, :]


def adam_step(weight, grad, first_m, second_m, rate, decay):
    first_new = ADAM_BETA_ONE * first_m + (1.0 - ADAM_BETA_ONE) * grad
    second_new = ADAM_BETA_TWO * second_m + (1.0 - ADAM_BETA_TWO) * grad * grad
    first_hat = first_new / (1.0 - ADAM_BETA_ONE**STEP)
    second_hat = second_new / (1.0 - ADAM_BETA_TWO**STEP)
    weight_new = weight * (1.0 - rate * decay) - rate * first_hat / (jnp.sqrt(second_hat) + ADAM_EPS)
    return first_new, second_new, weight_new


def gram_triangle(store, values, product):
    high, low = halves(values)
    half = store.shape[1]

    def part(side, at):
        return side[at * half : (at + 1) * half, :] if product is nt else side[:, at * half : (at + 1) * half]

    for at, (i, j) in enumerate(((0, 0), (0, 1), (1, 1))):
        store[at * half : (at + 1) * half, :] = (
            product(part(high, i), part(high, j))
            + product(part(high, i), part(low, j))
            + product(part(low, i), part(high, j))
        )


def sort_rows(quarter_ref, rows_ref, up_ref, down_ref):
    slices = (quarter_ref.shape[0] - 32) // 4
    wide = 3 * PAIR // 8
    for high in range(2):
        at = slice(high * slices, (high + 1) * slices)
        first = high * (2 * slices + 32)
        up_ref[at, :] = quarter_ref[first : first + slices, :]
        down_ref[at, :] = quarter_ref[first + slices : first + 2 * slices, :]
        values = rows_ref[high].astype(F32)
        down_ref[2 * slices + high * wide : 2 * slices + (high + 1) * wide, :] = values[0:wide].astype(BF16)
    up_ref[2 * slices : 2 * slices + 32, :] = quarter_ref[2 * slices : 2 * slices + 32, :]
    up_ref[2 * slices + 32 : 2 * slices + 2 * wide, :] = jnp.zeros((2 * wide - 32, up_ref.shape[1]), BF16)
    return jnp.concatenate([rows_ref[high].astype(F32)[wide:] for high in range(2)], axis=0).astype(BF16)


def choose_kernel(where_ref, quarter_ref, rows_ref, first_ref, rest_ref, sorted_ref):
    side = where_ref[SIDE]
    main = first_ref.shape[0]
    small = sort_rows(quarter_ref, rows_ref, sorted_ref.at[0], sorted_ref.at[1])
    first_ref[...] = sorted_ref[1 - side]
    rest_ref[0:main, :] = sorted_ref[side]
    rest_ref[main:, :] = small


def put(all_ref, scale, sources, low, base_rows, matrix):
    for high, (ref, at) in enumerate(sources):
        piece = 4 * high + low
        to = pl.ds(pl.multiple_of(matrix + piece * base_rows, 8), base_rows)
        all_ref[to, :] = scale * ref[at : at + base_rows, :].astype(F32)


def gram_kernel(
    where_ref, square_ref, q0_ref, r0_ref, q1_ref, r1_ref, y0_ref, y1_ref, mq_ref, mo_ref, mu_ref, md_ref,
    near_ref, far_ref, all_ref, pack_ref, sorted_ref,
):
    dp, across, core, side = where_ref[GROUP], where_ref[ROW], where_ref[CORE], where_ref[SIDE]
    clip = jnp.max(CLIP_NORM / jnp.maximum(jnp.sqrt(square_ref[...]), CLIP_NORM))
    units, wide = mu_ref.shape[1], mq_ref.shape[1]
    slices = units // 8
    for turn, (quarter, rows) in enumerate(((q0_ref, r0_ref), (q1_ref, r1_ref))):
        sort_rows(quarter, rows, sorted_ref.at[2 * turn], sorted_ref.at[2 * turn + 1])

    def gather(type_index, put_rows):
        for turn, got in enumerate((y0_ref, y1_ref)):
            put_rows(sorted_ref.at[2 * turn + type_index], (2 * turn) ^ (dp & 3))
            put_rows(got, (2 * turn + 1) ^ (dp & 3))

    def grams(*pair):
        for index, (values, product) in enumerate(pair):
            gram_triangle(pack_ref, values, product)
            half = pack_ref.shape[0] // 2
            slot = index ^ across
            near_ref[slot] = pack_ref[pl.ds(pl.multiple_of(core * half, 8), half), :]
            far_ref[slot] = pack_ref[pl.ds(pl.multiple_of((1 - core) * half, 8), half), :]

    @pl.when(side == 0)
    def _():
        def up_out(ref, low):
            put(all_ref, clip, ((ref, 0), (ref, slices)), low, slices, 0)
            all_ref[pl.ds(pl.multiple_of(units + low * 32, 8), 32), :] = clip * ref[
                2 * slices : 2 * slices + 32, :
            ].astype(F32)

        gather(0, up_out)
        up = MUON_MOMENTUM * mu_ref[...] + jnp.transpose(all_ref[0:units, :])
        out = MUON_MOMENTUM * mo_ref[...] + all_ref[units : units + mo_ref.shape[0], :]
        grams((up, nt), (out, tn))

    @pl.when(side == 1)
    def _():
        def down_qkv(ref, low):
            put(all_ref, clip, ((ref, 0), (ref, slices)), low, slices, 0)
            put(all_ref, clip, ((ref, 2 * slices), (ref, 2 * slices + wide // 8)), low, wide // 8, units)

        gather(1, down_qkv)
        qkv = MUON_MOMENTUM * mq_ref[...] + jnp.transpose(heads_apart(all_ref[units : units + wide, :], True))
        down = MUON_MOMENTUM * md_ref[...] + all_ref[0:units, :]
        grams((qkv, nt), (down, tn))


def momentum_kernel(
    where_ref, square_ref, q0_ref, r0_ref, q1_ref, r1_ref, y0_ref, y1_ref, rest0_ref, rest1_ref,
    mq_ref, mo_ref, mu_ref, md_ref,
    emb_ref, emb_m_ref, emb_v_ref, head_ref, head_m_ref, head_v_ref, gain_ref, gain_m_ref, gain_v_ref,
    norm_ref, mq_out, mo_out, mu_out, md_out, mq_near, mo_near, mu_near, md_near,
    emb_m_out, emb_v_out, emb_out, head_m_out, head_v_out, head_out, gain_m_out, gain_v_out, gain_out,
    all_ref, rows_ref, sorted_ref, got_ref,
):
    dp, side = where_ref[GROUP], where_ref[SIDE]
    norm = jnp.sqrt(square_ref[...])
    norm_ref[...] = norm
    clip = jnp.max(CLIP_NORM / jnp.maximum(norm, CLIP_NORM))
    units, wide, out_rows = mu_ref.shape[1], mq_ref.shape[1], mo_ref.shape[0]
    slices = units // 8
    main = y0_ref.shape[0]
    qkv_at, out_at = 2 * units + out_rows, 2 * units

    def place(up_ref, down_ref, small, low):
        put(all_ref, clip, ((up_ref, 0), (up_ref, slices)), low, slices, 0)
        put(all_ref, clip, ((down_ref, 0), (down_ref, slices)), low, slices, units)
        put(all_ref, clip, ((down_ref, 2 * slices), (down_ref, 2 * slices + wide // 8)), low, wide // 8, qkv_at)
        all_ref[pl.ds(pl.multiple_of(out_at + low * 32, 8), 32), :] = clip * up_ref[
            2 * slices : 2 * slices + 32, :
        ].astype(F32)
        for high in range(2):
            to = pl.ds(pl.multiple_of((4 * high + low) * 8, 8), 8)
            rows_ref[to, :] = clip * small.astype(F32)[8 * high : 8 * high + 8]

    for turn, (quarter, rows, first, rest) in enumerate(
        ((q0_ref, r0_ref, y0_ref, rest0_ref), (q1_ref, r1_ref, y1_ref, rest1_ref))
    ):
        small = sort_rows(quarter, rows, sorted_ref.at[0], sorted_ref.at[1])
        place(sorted_ref.at[0], sorted_ref.at[1], small, (2 * turn) ^ (dp & 3))
        got_ref[side] = first[...]
        got_ref[1 - side] = rest[0:main, :]
        place(got_ref.at[0], got_ref.at[1], rest[main:, :], (2 * turn + 1) ^ (dp & 3))
    mu_out[...] = MUON_MOMENTUM * mu_ref[...] + jnp.transpose(all_ref[0:units, :])
    md_out[...] = MUON_MOMENTUM * md_ref[...] + all_ref[units : 2 * units, :]
    mo_out[...] = MUON_MOMENTUM * mo_ref[...] + all_ref[out_at:qkv_at, :]
    mq_out[...] = MUON_MOMENTUM * mq_ref[...] + jnp.transpose(heads_apart(all_ref[qkv_at:, :], True))
    for near, out in ((mq_near, mq_out), (mo_near, mo_out), (mu_near, mu_out), (md_near, md_out)):
        near[...] = out[...]
    vocab = emb_ref.shape[0]
    head_m_out[...], head_v_out[...], head_out[...] = adam_step(
        head_ref[...], rows_ref[0:vocab, :], head_m_ref[...], head_v_ref[...], HEAD_RATE, WEIGHT_DECAY
    )
    emb_m_out[...], emb_v_out[...], emb_out[...] = adam_step(
        emb_ref[...], rows_ref[vocab : 2 * vocab, :], emb_m_ref[...], emb_v_ref[...], EMBED_RATE, WEIGHT_DECAY
    )
    gain_m_out[...], gain_v_out[...], gain_out[...] = adam_step(
        gain_ref[...], rows_ref[2 * vocab : 2 * vocab + 3, :], gain_m_ref[...], gain_v_ref[...], GAIN_RATE, 0.0
    )


def rows_kernel(where_ref, out_ref, out_got_ref, grad_ref, grad_got_ref, block_ref, input_ref):
    row = where_ref[ROW]
    size = out_got_ref.shape[0]
    block_ref[row] = out_ref[0:size, :]
    block_ref[1 - row] = out_got_ref[...]
    input_ref[row] = grad_ref[0:size, :]
    input_ref[1 - row] = grad_got_ref[...].astype(F32)


def squares_kernel(quarter_ref, quarter_z_ref, rows_ref, rows_z_ref, out_ref):
    wide = 3 * PAIR // 8
    total = 0.0
    for ref in (quarter_ref, quarter_z_ref):
        values = ref[...].astype(F32)
        total = total + jnp.sum(values * values)
    for ref in (rows_ref, rows_z_ref):
        for at in range(ref.shape[0]):
            values = ref[at].astype(F32)
            total = total + jnp.sum(values[0:wide] * values[0:wide]) + 0.25 * jnp.sum(values[wide:] * values[wide:])
    out_ref[...] = jnp.full(out_ref.shape, total, F32)


def three(left, right):
    left_high, left_low = halves(left)
    right_high, right_low = halves(right)
    return nn(
        jnp.concatenate([left_high, left_high, left_low], axis=1),
        jnp.concatenate([right_high, right_low, right_high], axis=0),
    )


def once(left, right):
    return nn(left.astype(BF16), right.astype(BF16))


def schulz_kernel(where_ref, mine_ref, other_ref, near_ref, far_ref, pack_ref, poly_ref, gram_ref, tri_ref):
    half, block = mine_ref.shape
    size = 2 * block
    core = where_ref[CORE]
    pack_ref[pl.ds(pl.multiple_of(core * half, 8), half), :] = mine_ref[...]
    pack_ref[pl.ds(pl.multiple_of((1 - core) * half, 8), half), :] = other_ref[...]
    gram_ref[0:block, 0:block] = pack_ref[0:block, :]
    corner = pack_ref[block:size, :]
    gram_ref[0:block, block:] = corner
    gram_ref[block:, 0:block] = jnp.transpose(corner)
    gram_ref[block:, block:] = pack_ref[size:, :]
    gram = gram_ref[...]
    rows = lax.broadcasted_iota(jnp.int32, gram.shape, 0)
    columns = lax.broadcasted_iota(jnp.int32, gram.shape, 1)
    diagonal = rows == columns
    trace = jnp.sum(jnp.where(diagonal, gram, 0.0))
    inverse = 1.0 / (jnp.sqrt(jnp.full((1, size), trace, F32)) + 1e-07)
    gram = gram * (inverse * inverse)

    def sweep(gram, poly, times, last=False):
        change = SCHULZ_SQUARE * gram + SCHULZ_CUBE * times(gram, gram)
        if poly is None:
            poly_ref[...] = change * inverse + jnp.where(diagonal, SCHULZ_LINEAR * inverse, 0.0)
        else:
            poly_ref[...] = SCHULZ_LINEAR * poly + times(change, poly)
        if not last:
            moved = SCHULZ_LINEAR * gram + times(change, gram)
            gram_ref[...] = SCHULZ_LINEAR * moved + times(moved, change)

    sweep(gram, None, once)
    sweep(gram_ref[...], poly_ref[...], once)
    sweep(gram_ref[...], poly_ref[...], once)
    for index in range(3, NS_STEPS):
        sweep(gram_ref[...], poly_ref[...], three, index == NS_STEPS - 1)
    poly = poly_ref[...]
    spine = jnp.sum(jnp.where(diagonal, poly, 0.0), axis=0, keepdims=True)
    off = jnp.where(diagonal, 0.0, poly).astype(BF16)
    high = spine.astype(BF16).astype(F32)
    low = spine - high
    rest = jnp.zeros((14, block), F32)
    tops = [
        jnp.concatenate([high[:, at], low[:, at], rest], axis=0).astype(BF16)
        for at in (slice(0, block), slice(block, size))
    ]
    part = half - block
    tri_ref[0, 0:block, :] = off[0:block, 0:block]
    tri_ref[0, block:half, :] = off[0:part, block:]
    tri_ref[0, half:, :] = tops[0]
    tri_ref[1, 0 : block - part, :] = off[part:block, block:]
    tri_ref[1, block - part : half, :] = off[block:, block:]
    tri_ref[1, half:, :] = tops[1]
    near_ref[...] = tri_ref[core]
    far_ref[...] = tri_ref[1 - core]


def muon_kernel(
    where_ref, mq_ref, mo_ref, mu_ref, md_ref, near0, near1, near2, near3, far0, far1, far2, far3,
    wq_ref, wo_ref, wu_ref, wd_ref, wq_out, wo_out, wu_out, wd_out, tri_ref,
):
    across, core, side = where_ref[ROW], where_ref[CORE], where_ref[SIDE]
    held = 2 * side + across
    for at, (near, far) in enumerate(((near0, far0), (near1, far1), (near2, far2), (near3, far3))):
        tri_ref[at, core] = near[...]
        tri_ref[at, 1 - core] = far[...]
    block = near0.shape[1]
    half = near0.shape[0] - 16
    part = half - block

    def ortho(matrix, values, left):
        slot = matrix ^ held
        first = tri_ref[slot, 0]
        second = tri_ref[slot, 1]
        corner = jnp.concatenate([first[block:half], second[0 : block - part]], axis=0)
        upper = jnp.concatenate([first[0:block], corner], axis=1)
        lower = jnp.concatenate([jnp.transpose(corner), second[block - part : half]], axis=1)
        poly = jnp.concatenate([upper, lower], axis=0)
        spines = [tri[half:].astype(F32) for tri in (first, second)]
        spine = jnp.concatenate([s[0:1] + s[1:2] for s in spines], axis=1)
        if left:
            spine = jnp.transpose(jnp.broadcast_to(spine, (8, 2 * block)))[:, 0:1]
            return nn(poly, values.astype(BF16)) + values * spine
        return nn(values.astype(BF16), poly) + values * spine

    def moved(weight, ortho, longest):
        return weight * (1.0 - MUON_RATE * MUON_DECAY) - MUON_RATE * 0.2 * math.sqrt(longest) * ortho

    wu_out[...] = moved(wu_ref[...], ortho(0, mu_ref[...], True), max(D, FF))
    wo_out[...] = moved(wo_ref[...], ortho(1, mo_ref[...], False), D)
    wq_out[...] = moved(wq_ref[...], ortho(2, mq_ref[...], True), 3 * D)
    wd_out[...] = moved(wd_ref[...], ortho(3, md_ref[...], False), max(D, FF))


VMEM = pl.BlockSpec(memory_space=pltpu.VMEM)
SMEM = pl.BlockSpec(memory_space=pltpu.SMEM)
VMEM_LIMIT = 14 * 1024 * 1024


def call(body, name, ins, outs, scratch=(), scalars=0, plain=(), far=(), micros=1):
    shapes = [
        (pltpu.HBM if at in far else pltpu.VMEM)(shape, dtype)
        for at, (shape, dtype) in enumerate(outs)
    ]
    held = [
        value if at < scalars else pltpu.with_memory_space_constraint(value, pltpu.HBM if at in plain else pltpu.VMEM)
        for at, value in enumerate(ins)
    ]
    return pl.pallas_call(
        body,
        name=name,
        out_shape=shapes,
        in_specs=[SMEM] * scalars + [VMEM] * (len(ins) - scalars),
        out_specs=[VMEM] * len(shapes),
        scratch_shapes=list(scratch),
        compiler_params=pltpu.CompilerParams(vmem_limit_bytes=VMEM_LIMIT),
        cost_estimate=pl.CostEstimate(flops=micros * 10**8, bytes_accessed=0, transcendentals=0),
    )(*held)


def swap(values, bit):
    return lax.ppermute(values, "tensor", [(i, i ^ bit) for i in range(4)])


def swap_dp(values, bit):
    return lax.ppermute(values, "dp", [(i, i ^ bit) for i in range(lax.axis_size("dp"))])


def swap_both(values, bit, dp_bit):
    width = lax.axis_size("tensor")
    pairs = [
        (p * width + t, (p ^ dp_bit) * width + (t ^ bit)) for p in range(lax.axis_size("dp")) for t in range(width)
    ]
    return lax.ppermute(values, ("dp", "tensor"), pairs)


def add(left, right):
    return (left.astype(F32) + right.astype(F32)).astype(BF16)


def join(*parts):
    return jnp.concatenate(parts, axis=-2)


def after(values, done):
    return lax.optimization_barrier((values, done))[0]


def over_rest(piece):
    bit = 8
    while bit < lax.axis_size("dp"):
        piece = add(piece, swap_dp(piece, bit))
        bit *= 2
    return piece


def on_device(
    noised, targets, timesteps, segments, embedding, out_head, norm_gains,
    w_qkv, w_out, w_up, w_down, mom_qkv, mom_out, mom_up, mom_down,
    embed_m, embed_v, head_m, head_v, gains_m, gains_v,
):
    place = lax.axis_index("tensor")
    group = lax.axis_index("dp") & 7
    row = place // 2
    core = place % 2
    size = noised.shape[1]
    length = segments.shape[1]
    own = 2 * size
    order = jnp.stack([place, place ^ 2, place ^ 1, place ^ 3])

    ids = jnp.stack([noised, targets])
    mine = lax.dynamic_index_in_dim(ids, row, 1, keepdims=False)
    send_ids = lax.dynamic_index_in_dim(ids, 1 - row, 1, keepdims=False)
    got = swap(send_ids, 2)
    own_ids = jnp.stack([mine, got], axis=1)
    tok = jnp.concatenate([own_ids[0], swap(own_ids[0], 1)], axis=0)
    seg_row = lax.dynamic_index_in_dim(segments, row, 0, keepdims=False)
    span_ids = jnp.arange(timesteps.shape[1], dtype=jnp.int32)
    starts = jnp.sum((seg_row[None, :] < span_ids[:, None]).astype(jnp.int32), axis=1)
    times = lax.dynamic_index_in_dim(timesteps, row, 0, keepdims=False)
    stand = jnp.stack([group, row, core, group & 1])
    where = jnp.concatenate([row * 4 + order, order, times, starts, stand]).astype(jnp.int32)
    table = jnp.asarray(position_table(max(length, 1000), D))

    unit_rows = w_up.shape[1]
    out_rows = w_out.shape[0]
    side = (group & 1).reshape(1).astype(jnp.int32)
    pack_rows = 3 * PAIR + out_rows
    wa_mine, wa_part = call(
        attention_weights_kernel, "attention_weights", [side, after(w_qkv, send_ids), w_out],
        [((pack_rows, D), BF16), ((pack_rows // 2, D), BF16)], scalars=1, plain=(1, 2),
    )
    (wb_mine,) = call(
        ffn_weights_kernel, "ffn_weights", [after(w_up, wa_part), w_down], [((2 * unit_rows, D), BF16)], plain=(0, 1)
    )
    wa_part = swap(wa_part, 2)

    hidden0, a1, aug = call(
        embed_kernel, "embed",
        [where, tok, segments.reshape(-1, size), table, embedding, norm_gains],
        [((own, D), F32), ((length, D), BF16), ((length, PAIR), BF16)],
        [pltpu.VMEM((VOCAB_PAD + SPAN_PAD, 2 * D), F32)],
        scalars=1, plain=(2, 3, 4, 5), micros=4,
    )

    def attend(first, second):
        return call(
            attend_kernel, "attend", [a1, aug, first, second],
            [((2, length, 3 * PAIR), BF16), ((2 * PAIR, own), F32), ((4, length, own), BF16), ((8, own), F32)],
            micros=5,
        )

    wb_across = swap(wb_mine, 2)
    wa = [wa_mine, swap(wa_mine, 1)]
    qkv_a, ctx_a, weights_a, inverse_a = attend(*wa)
    wa_part = after(wa_part, a1)
    (wa_across,) = call(
        join_kernel, "join", [where, wa_part, after(swap_dp(wa_part, 1), ctx_a)], [((2, pack_rows // 2, D), BF16)], scalars=1
    )
    wa_across = wa_across.reshape(pack_rows, D)
    wa += [wa_across, swap(wa_across, 1)]
    qkv_b, ctx_b, weights_b, inverse_b = attend(*wa[2:])
    wb = [wb_mine, swap(wb_mine, 1)]
    half_chunks = FF // CHUNK // 2
    hidden1, partial2, a2, act_a, slope_a = call(
        ffn_up_kernel, "ffn_up", [ctx_a, ctx_b, hidden0, norm_gains, *wa, *wb],
        [((own, D), F32), ((own, D), F32), ((own, D), BF16)] + [((half_chunks, own, CHUNK), BF16)] * 2,
        plain=(3,), micros=7,
    )
    wb_across = after(wb_across, a2)
    wb += [wb_across, swap(wb_across, 1)]
    slices = unit_rows // 4
    units = ((2, own, CHUNK), BF16)
    partial2, act_b, slope_b = call(
        ffn_next_kernel, "ffn_next", [partial2, a2, wb[2]], [((own, D), F32), units, units], micros=3
    )
    chunk = ((own, CHUNK), BF16)
    hidden2, d_h2, d_ffn, d_a2, act_c, slope_c, keep_a, send_a, part = call(
        ffn_kernel, "ffn",
        [where, partial2, a2, out_head.T, norm_gains, own_ids[1], act_a, slope_a, act_b, slope_b, *wb],
        [((own, D), BF16), ((own, D), F32), ((own, D), BF16), ((own, D), F32), chunk, chunk]
        + [((8, slices, D), BF16)] * 2 + [((VOCAB_PAD + 8, D), F32)],
        [pltpu.VMEM((2, own, CHUNK), BF16), pltpu.VMEM((2, own, CHUNK), BF16), pltpu.VMEM((VOCAB_PAD, D), F32)],
        scalars=1, plain=(3, 4), far=(0,), micros=10,
    )
    got_a = swap(send_a, 1)
    d_a2, keep_b, send_b = call(
        ffn_end_kernel, "ffn_end",
        [where, d_ffn, d_a2, a2, act_a, slope_a, act_b, slope_b, act_c, slope_c, *wb],
        [((own, D), F32)] + [((8, slices, D), BF16)] * 2, scalars=1, micros=3,
    )
    got_b = swap(send_b, 1)
    keep_x, send_x = add(keep_a[0:4], got_a[0:4]), add(keep_a[4:8], after(got_a, d_a2)[4:8])
    got_x = swap(send_x, 2)
    d_a2 = after(d_a2, send_x)
    d_h1, d_attn, keep_o, send_o, gain1 = call(
        ffn_norm_kernel, "ffn_norm", [where, ctx_a, ctx_b, hidden1, d_h2, d_a2, norm_gains],
        [((own, D), F32), ((own, D), BF16)] + [((8, out_rows // 4, D), BF16)] * 2 + [((8, D), F32)],
        scalars=1, plain=(6,), micros=3,
    )
    got_o = swap(send_o, 1)

    def back(qkv, weights, ctx, inverse, d_attn, packs):
        return call(
            attend_back_kernel, "attend_back", [qkv, weights, ctx, inverse, d_attn, *packs],
            [((2, own, PAIR), BF16), ((2, own, 2 * PAIR), BF16), ((2, own, 2 * PAIR), BF16)], micros=5,
        )

    keep_y, send_y = add(keep_b[0:4], got_b[0:4]), add(keep_b[4:8], got_b[4:8])
    got_y = swap_dp(send_y, 1)
    got_o = after(got_o, send_y)
    keep_o, send_o = add(keep_o[0:4], got_o[0:4]), add(keep_o[4:8], got_o[4:8])
    got_o = swap(send_o, 2)
    d_attn = after(d_attn, (send_x, send_y, send_o))
    dq_b, near_b, far_b = back(qkv_b, weights_b, ctx_b, inverse_b, d_attn, wa[2:])
    far_b = swap(far_b, 1)
    dq_a, near_a, far_a = back(qkv_a, weights_a, ctx_a, inverse_a, after(d_attn, dq_b), wa[:2])
    far_a = swap(far_a, 1)
    got_x, got_y, got_o, dq_b = lax.optimization_barrier((got_x, got_y, got_o, dq_b))
    half_a = join(add(keep_x, got_x), add(keep_o, got_o))
    half_b = add(keep_y, got_y)
    near_b = after(near_b, (half_a, half_b))
    grads = [((own, D), F32), ((8, 48, D), BF16), ((8, 48, D), BF16)]
    d_a1, keep2_b, send2_b = call(
        input_far_kernel, "input_far", [where, dq_b, near_b, far_b, a1, *wa[2:]], grads, scalars=1, micros=4
    )
    got2_b = swap(send2_b, 1)
    got_y, got_x = swap_dp(half_a[2:4], 1), swap(half_b[2:4], 2)
    igrad, keep2, send2, small = call(
        input_kernel, "input_grad",
        [where, dq_a, near_a, far_a, a1, *wa[:2], d_a1, hidden0, d_h1, norm_gains, tok, part, gain1],
        grads + [((8, 8, D), F32)], [pltpu.VMEM((64, D), F32)], scalars=1, plain=(10,), micros=5,
    )
    got_x, got_y, hidden2 = lax.optimization_barrier((got_x, got_y, hidden2))
    got2 = swap(send2, 1)
    small = small.astype(BF16)
    got_small = swap(small, 1)
    half_a, half_b = add(half_a[0:2], got_y), add(half_b[0:2], got_x)
    send_z = join(half_a[1], half_b[1])
    got_z = swap_dp(send_z, 2)
    near2, far2 = (values.reshape(2, 4, 48, D) for values in (add(keep2, got2), add(keep2_b, after(got2_b, send_z))))
    small = add(small, got_small).reshape(2, 4, 8, D)

    got2_y = swap_dp(join(near2[1], small[1], far2[1]), 1)
    quarter = add(join(half_a[0], half_b[0]), got_z)
    out_got = swap(after(hidden2, igrad)[size:], 2)
    rows = add(join(near2[0], small[0], far2[0]), after(got2_y, (out_got, quarter)))
    wide = near2.shape[-2]
    got2_x = swap(join(rows[:, wide + 8 :], rows[:, wide : wide + 8]), 2)
    igrad_got = swap(after(igrad, got2_x)[size:].astype(BF16), 2)
    rows = add(rows[:, 0 : wide + 8], got2_x)
    rows = add(rows[0:2], swap_dp(rows[2:4], 2))
    pairs = [[i, i ^ 4] for i in range(lax.axis_size("dp")) if not i & 4]
    both = lax.all_to_all(jnp.stack([quarter, quarter]), "dp", 0, 0, axis_index_groups=pairs, tiled=True)
    quarter = over_rest(add(both[0], both[1]))
    rows = after(rows, quarter)
    rows = over_rest(add(rows, swap_dp(rows, 4)))
    quarter_z, rows_z = swap_dp(quarter, 2), after(swap_dp(rows, 2), igrad_got)
    main = 2 * slices // 2 + 3 * PAIR // 4

    def choose(quarter, rows):
        return call(
            choose_kernel, "choose", [where, quarter, rows], [((main, D), BF16), ((main + 16, D), BF16)],
            [pltpu.VMEM((2, main, D), BF16)], scalars=1,
        )

    first0, rest0 = choose(quarter, rows)
    first0 = swap_dp(first0, 1)
    first1, rest1 = choose(quarter_z, rows_z)
    first1 = swap_dp(first1, 1)
    (square,) = call(squares_kernel, "squares", [quarter, quarter_z, rows, rows_z], [((8, 128), F32)])
    square = square + swap(square, 1)
    square = (square + swap(square, 2)) + (swap_dp(square, 1) + swap_both(square, 2, 1))
    rest0, rest1 = (swap_dp(rest, 1) for rest in after((rest0, rest1), square))

    def like(*arrays):
        return [(a.shape, F32) for a in arrays]

    heads = [out_head.T, head_m.T, head_v.T]
    triangle = ((2, 3 * D // 4, D // 2), F32)
    sums = [where, square, quarter, rows, quarter_z, rows_z, first0, first1]
    moments = [mom_qkv, mom_out, mom_up, mom_down]
    sorted_rows = pltpu.VMEM((4, main, D), BF16)
    near, far = call(
        gram_kernel, "gram", sums + moments, [triangle, triangle],
        [pltpu.VMEM((2 * unit_rows, D), F32), pltpu.VMEM((3 * D // 2, D // 2), F32), sorted_rows], scalars=1, micros=3,
    )
    far = swap(far, 1)
    half = after(near[0] + far[0], rest0) + swap(near[1] + far[1], 2)
    poly = [((16 + 3 * D // 4, D // 2), BF16)] * 2
    near, far = call(
        schulz_kernel, "schulz", [where, half, swap(half, 1)], poly,
        [pltpu.VMEM((3 * D // 2, D // 2), F32), pltpu.VMEM((D, D), F32), pltpu.VMEM((D, D), F32),
         pltpu.VMEM((2, 16 + 3 * D // 4, D // 2), BF16)],
        scalars=1, micros=10,
    )
    near, far = after((near, far), rest1)
    block_out, input_grad = call(
        rows_kernel, "rows", [where, hidden2, after(out_got, near), igrad, igrad_got],
        [((2, size, D), BF16), ((2, size, D), F32)], scalars=1, plain=(1, 3), far=(0, 1),
    )
    outs = call(
        momentum_kernel, "momentum",
        [where, after(square, near)] + sums[2:] + [rest0, rest1] + moments
        + [embedding, embed_m, embed_v, *heads, norm_gains, gains_m, gains_v],
        [((8, 128), F32)] + like(*moments, *moments, embed_m, embed_v, embedding)
        + like(*heads, gains_m, gains_v, norm_gains),
        [
            pltpu.VMEM((2 * unit_rows + out_rows + 3 * PAIR, D), F32), pltpu.VMEM((64, D), F32),
            pltpu.VMEM((2, main, D), BF16), pltpu.VMEM((2, main, D), BF16),
        ],
        scalars=1, plain=range(14, 23), far=[*range(5), *range(9, 18)], micros=5,
    )
    norm = outs[0]
    mom_qkv_new, mom_out_new, mom_up_new, mom_down_new = outs[1:5]
    moms = outs[5:9]
    embed_new, head_new, gains_new = outs[9:12], [h.T for h in outs[12:15]], outs[15:18]
    grad_norm = norm[0, 0]
    near_x, near_y = swap(near, 2), swap_dp(near, 1)
    nears = [near, *after((near_x, near_y, swap_both(near, 2, 1)), (moms, grad_norm, block_out, input_grad))]
    fars = [far] + [swap(values, 1) for values in nears[1:]]
    qkv_new, out_new, up_new, down_new = call(
        muon_kernel, "muon",
        [where, *moms, *nears, *fars, w_qkv, w_out, w_up, w_down],
        like(w_qkv, w_out, w_up, w_down),
        [pltpu.VMEM((4, 2, 16 + 3 * D // 4, D // 2), BF16)],
        scalars=1, far=range(4), micros=5,
    )
    return (
        block_out, input_grad, grad_norm,
        mom_qkv_new, qkv_new, mom_out_new, out_new, mom_up_new, up_new, mom_down_new, down_new,
        *embed_new, *head_new, *gains_new,
    )


def solution(mesh):
    columns, rows = P(None, "tensor"), P("tensor", None)
    matrices = (columns, rows, columns, rows)
    in_specs = (
        (P("dp", "tensor"), P("dp", "tensor"), P("dp", None), P("dp", None), P(), P(), P())
        + matrices + matrices + (P(),) * 6
    )
    out_specs = (
        (P("dp", "tensor", None), P("dp", "tensor", None), P())
        + (columns, columns, rows, rows, columns, columns, rows, rows) + (P(),) * 9
    )
    return jax.shard_map(on_device, mesh=mesh, in_specs=in_specs, out_specs=out_specs, check_vma=False)
```
